32 devices in a mesh: groups: 2 (over y), charge: 8 (over z, core), split: 2 (over x).
Axes of the slice: x: 2, y: 2, z: 4, core: 2. Of those that a mesh axis runs over, the one named last changes fastest.
Arguments:
- left_env: bfloat16 [16, 1024, 1024], P(('groups', 'charge'), 'split'), parts along dimension 0, may hold values from -6 to 6
- site_tensor: bfloat16 [16, 4, 1024, 1024], P(('groups', 'charge'), None, None, 'split'), parts along dimension 0, may hold values from -0.1875 to 0.1875
- left_sizes: int32 [16], P(('groups', 'charge')), parts along dimension 0, may hold values from 1 to 1024, 4096 in all
- right_sizes: int32 [16], P('groups'), parts along dimension 0, may hold values from 1 to 1024, 4096 in all
- targets: int32 [16, 4], P(('groups', 'charge')), parts along dimension 0, may hold values from 0 to 7, all different within a row
Outputs:
- new_env: float32 [16, 1024, 1024], P('groups', 'charge', 'split'), parts along dimension 0
The draws below stay inside these ranges and needn't reach their ends.
There are 2 independent parts, one for each index of `groups`. The reference program is written for one: setup_inputs(seed, part) draws one part's arguments, and reference() takes and returns one part's arrays. A program takes and returns all parts, laid end to end along the dimension named above; each array names one. Nothing has to cross between parts.
Inputs may be any that keep to these rules, and one draw needn't show every extreme that they name: `targets`: the 4 entries of one row are distinct, and every right-bond sector is reached by some row. `left_sizes`: they sum to 8 * B // 2 and the largest is exactly 1024. `right_sizes`: they sum to 8 * B // 2 and the largest is exactly 1024.
All inputs are finite; a program needn't handle non-finite values. No bound on the sum of `left_sizes` on one device may be relied on, other than what follows from the above.
Results may differ from the reference program's by a relative error of at most 0.015.
Values may be sent and summed in bfloat16 or wider, within the bound.
A program may use at most 64 MiB of HBM per device.

```python
import math
import jax
import jax.numpy as jnp
import numpy as np
from jax import lax

B = 1024
PHYS = 4
SECTORS = 8


def level_of(key, dims, cuts, low, high):
    def one(dim, shards_of):
        draws = jax.random.uniform(jax.random.fold_in(jax.random.fold_in(key, 6), dim), (shards_of,), jnp.float32, low / len(cuts), high / len(cuts))
        return jnp.repeat(jnp.exp(draws), dims[dim] // shards_of).reshape((-1,) + (1,) * (len(dims) - dim - 1))

    level = one(*cuts[0])
    for cut in cuts[1:]:
        level = level * one(*cut)
    return level


def distinct(stream_key, rows, number_of, top, lift):
    sequence = jax.random.permutation(jax.random.fold_in(stream_key, 1), number_of)
    boost = sequence
    for power in range(3):
        boost = boost * boost // number_of
    boost = boost * lift // number_of
    chance = jax.random.randint(jax.random.fold_in(stream_key, 2), (rows, number_of), 0, 4096) + boost
    holders = jax.random.permutation(jax.random.fold_in(stream_key, 3), rows)[jnp.arange(number_of) % rows]
    chance = jnp.where(jnp.arange(rows)[:, None] == holders[None, :], 1 << 14, chance)
    score = chance * number_of + jnp.arange(number_of)
    return lax.top_k(score.astype(jnp.int32), top)[1].astype(jnp.int32)


def profile(number_of, total, most, slope):
    loads = [(1 << 20) // math.isqrt(rank ** slope) + 1 for rank in range(2, number_of + 1)]
    surplus, counts = total - most - (number_of - 1), [1] * (number_of - 1)
    while surplus > 0:
        movable = [i for i in range(number_of - 1) if counts[i] < most]
        whole, remaining = sum([loads[i] for i in movable]), surplus
        for i in movable:
            more = min(most - counts[i], max(1, remaining * loads[i] // whole), surplus)
            counts[i] = counts[i] + more
            surplus = surplus - more
    return np.array([most] + counts)


def uneven(rng, number_of, total, reach, slope):
    if number_of == 2:
        one = jax.random.randint(rng, (), max(1, total - reach), min(reach, total - 1) + 1)
        return jnp.stack([one, total - one])
    lengths = jnp.asarray(profile(number_of, total, reach, slope), jnp.int32)
    twos = (number_of - 1) // 2
    source_of, taker = lengths[1:1 + 2 * twos:2], lengths[2:2 + 2 * twos:2]
    slack = jnp.minimum(source_of - 1, reach - taker)
    moved = jax.random.randint(jax.random.fold_in(rng, 1), (twos,), 0, 1 << 20) % (slack + 1)
    lengths = lengths.at[1:1 + 2 * twos:2].set(source_of - moved).at[2:2 + 2 * twos:2].set(taker + moved)
    return lengths[jax.random.permutation(jax.random.fold_in(rng, 2), number_of)]


def centred(rng, shape, deviation, reach, cuts=(), kind=jnp.bfloat16):
    gain = level_of(rng, shape, cuts, -0.22, 0.18) if cuts else 1.0
    values = jax.random.normal(rng, shape, jnp.float32) * deviation * gain
    return jnp.minimum(jnp.maximum(values, -reach), reach).astype(kind)


def setup_inputs(seed: int = 0, part: int = 0) -> dict:
    arg_keys = jax.random.split(jax.random.key(seed), 6)
    own_keys = jax.random.split(jax.random.fold_in(arg_keys[5], part), 6)
    return {
        "left_env": centred(own_keys[0], (SECTORS, B, B), 1.0, 6.0, ((0, 8), (1, 2))),
        "site_tensor": centred(own_keys[1], (SECTORS, PHYS, B, B), B ** -0.5, 0.1875, ((0, 8), (3, 2))),
        "left_sizes": uneven(own_keys[2], SECTORS, SECTORS * B // 2, B, 1).astype(jnp.int32),
        "right_sizes": uneven(own_keys[3], SECTORS, SECTORS * B // 2, B, 1).astype(jnp.int32),
        "targets": distinct(own_keys[4], SECTORS, SECTORS, PHYS, 8192),
    }


def reference(left_env, site_tensor, left_sizes, right_sizes, targets):
    sectors = left_env.shape[0]
    span = left_env.shape[1]
    rows = jnp.arange(span, dtype=jnp.int32)

    def one_sector(carry, index):
        block = left_env[index].astype(jnp.float32)
        tensors = site_tensor[index]
        reached = targets[index]
        live_cols = right_sizes[reached]
        keep = (rows[None, :, None] < left_sizes[index]) & (rows[None, None, :] < live_cols[:, None, None])
        masked = jnp.where(keep, tensors, jnp.zeros((), jnp.bfloat16)).astype(jnp.float32)
        product = jnp.einsum("ik,skj->sij", block, masked).astype(jnp.bfloat16)
        term = jnp.einsum("ski,skj->sij", masked, product.astype(jnp.float32)).astype(jnp.bfloat16)
        carry = carry.at[reached].add(term.astype(jnp.float32))
        return carry, None

    start = jnp.zeros((sectors, span, span), jnp.float32)
    result, unused = lax.scan(one_sector, start, jnp.arange(sectors, dtype=jnp.int32))
    return result
```

```python
import functools

import jax
import jax.numpy as jnp
from jax import lax
from jax.experimental import pallas as pl
from jax.experimental.pallas import tpu as pltpu
from jax.sharding import PartitionSpec as P

MESH = pl.DeviceIdType.MESH
LADDER = ((8, 8, 6, 3), (8, 8, 6, 4), (8, 8, 6, 6), (8, 8, 8, 8))


def gathered_body(left_env, site_tensor, left_sizes, right_sizes, targets):
    states = site_tensor.shape[1]
    span = site_tensor.shape[2]
    width = site_tensor.shape[3]
    sectors = right_sizes.shape[0]
    column_base = lax.axis_index("split") * width
    row_ids = lax.broadcasted_iota(jnp.int32, (1, span, 1), 1)
    column_ids = lax.broadcasted_iota(jnp.int32, (1, 1, width), 2) + column_base
    slot_ids = lax.broadcasted_iota(jnp.int32, (states, sectors), 1)
    route = targets[0][:, None] == slot_ids
    live_cols = jnp.sum(jnp.where(route, right_sizes[None, :], 0), axis=1)
    keep = (row_ids < left_sizes[0]) & (column_ids < live_cols[:, None, None])
    masked = jnp.where(keep, site_tensor[0], jnp.zeros((), jnp.bfloat16))[None]
    product = jnp.einsum(
        "ik,skj->sij",
        lax.all_gather(left_env, "split", axis=1, tiled=True)[0],
        masked[0],
        preferred_element_type=jnp.float32,
    ).astype(jnp.bfloat16)
    terms = jnp.einsum(
        "ski,skj->sij",
        lax.all_gather(masked, "split", axis=3, tiled=True)[0],
        product,
        preferred_element_type=jnp.float32,
    ).astype(jnp.bfloat16)
    placed = jnp.einsum(
        "st,sij->tij", route.astype(jnp.bfloat16), terms, preferred_element_type=jnp.float32
    ).astype(jnp.bfloat16)
    return lax.psum_scatter(placed, "charge", scatter_dimension=1, tiled=True).astype(jnp.float32)


def agree(targets_ref, left_ref, right_ref, l_ref, m_ref, inv_ref, meta_ref, pick_ref, lf, ms,
          info, got, seen, site, send, recv, sem, lsend, lrecv, lown, mown):
    g = lax.axis_index("groups")
    me = lax.axis_index("charge")
    h = lax.axis_index("split")
    devices, sectors = inv_ref.shape[0] // 2, right_ref.shape[0]
    others = got.shape[0]
    states = targets_ref.shape[1]
    mine = g * devices + me

    barrier = pltpu.get_barrier_semaphore()

    def place(i):
        n = lax.rem(mine + i, others)
        return {"groups": n // devices, "charge": lax.rem(n, devices)}

    def greet(i, c):
        pl.semaphore_signal(barrier, inc=1, device_id=place(i), device_id_type=MESH)
        return c

    lax.fori_loop(1, others, greet, 0)
    pl.semaphore_signal(barrier, inc=1, device_id={"split": 1 - h}, device_id_type=MESH)

    span, width = ms.shape[1], ms.shape[2]
    half_rows = pl.ds(pl.multiple_of(h * width, width), width)
    m_own = pltpu.make_async_copy(m_ref, site, mown)
    m_own.start()
    l_own = pltpu.make_async_copy(l_ref, lf.at[half_rows], lown)
    l_own.start()
    to = [targets_ref[0, j] for j in range(states)]
    size = [right_ref[t] for t in to]
    rank = []
    for j in range(states):
        ahead = jnp.int32(0)
        for k in range(states):
            if k != j:
                first = size[k] >= size[j] if k < j else size[k] > size[j]
                ahead = ahead + jnp.where(first, 1, 0)
        rank.append(ahead)
    lane = lax.broadcasted_iota(jnp.int32, info.shape, 1)
    packed = jnp.zeros(info.shape, jnp.int32)
    for slot in range(states):
        state, live, target = jnp.int32(0), jnp.int32(0), jnp.int32(0)
        for j in range(states):
            here = rank[j] == slot
            state = jnp.where(here, j, state)
            live = jnp.where(here, size[j], live)
            target = jnp.where(here, to[j], target)
        meta_ref[slot] = state
        meta_ref[states + slot] = live
        packed = jnp.where(lane == slot, target, packed)
        packed = jnp.where(lane == states + slot, live, packed)
    meta_ref[2 * states] = left_ref[0]
    for r in range(sectors):
        meta_ref[2 * states + 1 + r] = right_ref[r]
    info[...] = packed
    got[mine] = packed
    pl.semaphore_wait(barrier, others)
    l_copy = pltpu.make_async_remote_copy(
        src_ref=l_ref, dst_ref=lf.at[half_rows], send_sem=lsend, recv_sem=lrecv,
        device_id={"split": 1 - h}, device_id_type=MESH)
    l_copy.start()

    def copy(i):
        return pltpu.make_async_remote_copy(
            src_ref=info, dst_ref=got.at[mine], send_sem=send.at[i], recv_sem=recv.at[mine],
            device_id=place(i), device_id_type=MESH)

    def start(i, c):
        copy(i).start()
        return c

    def finish(i, c):
        n = lax.rem(mine + i, others)
        copy(i).wait_send()
        pltpu.make_async_remote_copy(
            src_ref=info, dst_ref=got.at[n], send_sem=send.at[i], recv_sem=recv.at[n],
            device_id=place(i), device_id_type=MESH).wait_recv()
        return c

    lax.fori_loop(1, others, start, 0)
    m_own.wait()

    def mask(j, c):
        state, live, deep = meta_ref[j], meta_ref[states + j], meta_ref[2 * states]

        def tile(i, c):
            part = pl.ds(pl.multiple_of(i * 128, 128), 128)
            row_ids = lax.broadcasted_iota(jnp.int32, (128, width), 0) + i * 128
            col_ids = lax.broadcasted_iota(jnp.int32, (128, width), 1) + h * width
            keep = (row_ids < deep) & (col_ids < live)
            ms[j, part] = jnp.where(keep, site[state, part].astype(jnp.float32), 0.0).astype(jnp.bfloat16)
            return c

        return lax.fori_loop(0, span // 128, tile, c)

    lax.fori_loop(0, states, mask, 0)
    lax.fori_loop(1, others, finish, 0)
    local = pltpu.make_async_copy(got, seen, sem)
    local.start()
    local.wait()

    half = devices // 2
    relayed = (h == 0) & (me < half)
    wants, passes = [], []
    for r in range(sectors):
        wants.append(right_ref[r] > jnp.maximum(me * (span // devices), h * width))
        passes.append(right_ref[r] > (me - half) * (span // devices))

    def route(q, c):
        reached = [seen[g * devices + q, 0, j] for j in range(states)]
        for r in range(sectors):
            slot = jnp.int32(states)
            for j in range(states):
                slot = jnp.where(reached[j] == r, j, slot)
            direct = wants[r] & jnp.logical_not(relayed & (q >= half))
            inv_ref[q, r] = jnp.where(direct, slot, states)
            inv_ref[devices + q, r] = jnp.where(passes[r], slot, states)
        return c

    lax.fori_loop(0, devices, route, 0)

    def widest(n, most):
        return tuple(jnp.maximum(m, seen[n, 0, states + j]) for j, m in enumerate(most))

    most = lax.fori_loop(0, others, widest, (jnp.int32(0),) * states)
    pick = jnp.int32(len(LADDER) - 1)
    for at in range(len(LADDER) - 2, -1, -1):
        fits = most[0] <= LADDER[at][0] * 128
        for j in range(1, states):
            fits = fits & (most[j] <= LADDER[at][j] * 128)
        pick = jnp.where(fits, at, pick)
    pick_ref[0] = pick
    l_own.wait()
    l_copy.wait()


def kernel(caps, inv_ref, meta_ref, lf, ms, o_ref, mr, pb, tb, zr, ag, up, down, px, xb,
           xsend, xrecv, msend, mrecv, zsend, zrecv, usend, urecv, dsend, drecv):
    me = lax.axis_index("charge")
    h = lax.axis_index("split")
    devices, empty, rows, width = zr.shape[0], zr.shape[1] - 1, zr.shape[2], zr.shape[3]
    states, span = ms.shape[0], ms.shape[1]
    half = devices // 2
    wide = mr.shape[0]
    f32, bf16 = jnp.float32, jnp.bfloat16

    barrier = pltpu.get_barrier_semaphore()
    pl.semaphore_signal(barrier, inc=1, device_id={"split": 1 - h}, device_id_type=MESH)

    def greet(i, c):
        pl.semaphore_signal(barrier, inc=1, device_id={"charge": lax.rem(me + i, devices)}, device_id_type=MESH)
        return c

    lax.fori_loop(1, devices, greet, 0)
    pl.semaphore_wait(barrier, devices)

    def to_other(src, dst, send, recv):
        return pltpu.make_async_remote_copy(
            src_ref=src, dst_ref=dst, send_sem=send, recv_sem=recv,
            device_id={"split": 1 - h}, device_id_type=MESH)

    m_copies = [to_other(ms.at[j], mr.at[j], msend.at[j], mrecv.at[j]) for j in range(wide)]

    slim = [half < c <= half + 256 // rows for c in caps]
    thin = px.shape[1]

    def slim_copy(j):
        return to_other(ms.at[j, :, pl.ds(0, thin)], mr.at[j, :, pl.ds(0, thin)], msend.at[j], mrecv.at[j])

    def back_copy(j):
        return to_other(xb.at[j], tb.at[j, pl.ds(0, width), pl.ds(0, thin)], xsend.at[j], xrecv.at[j])

    def start_m(j):
        if slim[j]:
            pl.when(h == 1)(lambda: slim_copy(j).start())
        else:
            m_copies[j].start()

    start_m(0)

    def product(j):
        def tile(i, c):
            part = pl.ds(pl.multiple_of(i * 256, 256), 256)
            pb[j, part] = jnp.dot(lf[part], ms[j], preferred_element_type=f32).astype(bf16)
            return c

        lax.fori_loop(0, span // 256, tile, 0)

    def term(j, columns, which):
        for i in range(width // 256):
            part = pl.ds(pl.multiple_of(which * width + i * 256, 256), 256)
            tb[j, part] = lax.dot_general(
                columns[j, :, i * 256:(i + 1) * 256], pb[j], (((0,), (0,)), ((), ())),
                preferred_element_type=f32).astype(bf16)

    def live_width(j, side):
        return (caps[j] - half if side else min(caps[j], half)) * rows

    def chunk(j, d, source, side):
        part = pl.ds(pl.multiple_of(d * rows, rows), rows)
        columns = pl.ds(0, live_width(j, side))
        return pltpu.make_async_remote_copy(
            src_ref=tb.at[j, part, columns], dst_ref=zr.at[source, j, :, columns],
            send_sem=zsend.at[j, d], recv_sem=zrecv.at[source, j],
            device_id={"charge": d}, device_id_type=MESH)

    def scatter(j, side, lower):
        first = 0 if lower else half
        count = min(caps[j], half) if lower else caps[j] - half

        def one(i, c):
            d = first + lax.rem(me + 1 + i, count)

            @pl.when(d != me)
            def _():
                chunk(j, d, me, side).start()

            @pl.when(d == me)
            def _():
                zr[me, j] = tb[j, pl.ds(pl.multiple_of(d * rows, rows), rows)]

            return c

        lax.fori_loop(0, count, one, 0)

    upper, lower = (h == 0) & (me >= half), (h == 0) & (me < half)
    sectors = o_ref.shape[0]

    def lift(j, d, source):
        part = pl.ds(pl.multiple_of(d * rows, rows), rows)
        columns = pl.ds(0, live_width(j, 0))
        return pltpu.make_async_remote_copy(
            src_ref=tb.at[j, part, columns], dst_ref=ag.at[source, j, :, columns],
            send_sem=usend.at[j, d], recv_sem=urecv.at[source, j],
            device_id={"charge": half + d}, device_id_type=MESH)

    def collect(j):
        count = min(caps[j], half)

        def one(i, c):
            d = lax.rem(me + 1 + i, count)

            @pl.when(half + d != me)
            def _():
                lift(j, d, me - half).start()

            @pl.when(half + d == me)
            def _():
                ag[me - half, j] = tb[j, pl.ds(pl.multiple_of(d * rows, rows), rows)]

            return c

        lax.fori_loop(0, count, one, 0)

    def hand_down(r):
        return pltpu.make_async_remote_copy(
            src_ref=up.at[r], dst_ref=down.at[r], send_sem=dsend.at[r], recv_sem=drecv.at[r],
            device_id={"charge": me - half}, device_id_type=MESH)

    def relay():
        own = me - half

        def arrive(i, c):
            source = lax.rem(own + i, half)
            for j in range(states):
                pl.when(own < caps[j])(lambda j=j: lift(j, source, source).wait_recv())
            return c

        lax.fori_loop(1, half, arrive, 0)

        def send(r, c):
            total = ag[0, inv_ref[devices + half, r]].astype(f32)
            for source in range(1, half):
                total = total + ag[source, inv_ref[devices + half + source, r]].astype(f32)
            up[r] = total.astype(bf16)
            hand_down(r).start()
            return c

        lax.fori_loop(0, sectors, send, 0)

    def relay_sent():
        def left(i, c):
            d = lax.rem(me - half + i, half)
            for j in range(states):
                pl.when(d < caps[j])(lambda j=j: lift(j, d, d).wait_send())
            return c

        lax.fori_loop(1, half, left, 0)

        def gone(r, c):
            hand_down(r).wait_send()
            return c

        lax.fori_loop(0, sectors, gone, 0)

    def relay_received():
        def got(r, c):
            pltpu.make_async_remote_copy(
                src_ref=up.at[r], dst_ref=down.at[r], send_sem=dsend.at[r], recv_sem=drecv.at[r],
                device_id={"charge": me + half}, device_id_type=MESH).wait_recv()
            return c

        lax.fori_loop(0, sectors, got, 0)

    def near(j):
        product(j)
        term(j, ms, h)
        pl.when(lower)(functools.partial(scatter, j, 0, True))
        pl.when(upper)(functools.partial(collect, j))
        if caps[j] > half:
            pl.when(h == 1)(functools.partial(scatter, j, 1, False))

    for j in range(states):
        if j < wide:
            near(j)
        else:
            pl.when(h == 0)(functools.partial(near, j))
        if j == 1:
            start_m(1)
    zr[:, empty] = jnp.zeros((devices, rows, width), bf16)
    ag[:, empty] = jnp.zeros((half, rows, width), bf16)

    @pl.when(jnp.logical_not(lower))
    def _():
        down[...] = jnp.zeros(down.shape, bf16)

    def far_slim(j):
        slim_copy(j).wait_recv()

        def tile(i, c):
            part = pl.ds(pl.multiple_of(i * 256, 256), 256)
            px[part] = jnp.dot(lf[part], mr[j, :, 0:thin], preferred_element_type=f32).astype(bf16)
            return c

        lax.fori_loop(0, span // 256, tile, 0)
        for i in range(width // 256):
            xb[j, i * 256:(i + 1) * 256] = lax.dot_general(
                ms[j, :, i * 256:(i + 1) * 256], px[...], (((0,), (0,)), ((), ())),
                preferred_element_type=f32).astype(bf16)
        back_copy(j).start()
        tb[j, width:width + thin] = lax.dot_general(
            mr[j, :, 0:thin], pb[j], (((0,), (0,)), ((), ())), preferred_element_type=f32).astype(bf16)
        scatter(j, 0, False)

    def far_back(j):
        back_copy(j).wait_recv()
        scatter(j, 1, True)

    for j in range(wide):
        if slim[j]:
            if j + 2 < wide:
                start_m(j + 2)
            pl.when(h == 0)(functools.partial(far_slim, j))
            pl.when(h == 1)(functools.partial(far_back, j))
            continue
        m_copies[j].wait()
        if j + 2 < wide:
            start_m(j + 2)
        term(j, mr, 1 - h)
        pl.when(h == 0)(functools.partial(scatter, j, 0, False))
        pl.when(h == 1)(functools.partial(scatter, j, 1, True))
        if j == 0:
            pl.when(upper)(relay)
    for j in range(wide):
        if slim[j]:
            pl.when(h == 1)(lambda j=j: slim_copy(j).wait_send())
            pl.when(h == 0)(lambda j=j: back_copy(j).wait_send())

    def settle(i, c):
        other = lax.rem(me + i, devices)
        for j in range(states):
            for side in range(2 if j < wide else 1):
                here, there = (h == side) & (me < caps[j]), (h == side) & (other < caps[j])
                if side == 0:
                    here = here & ((me >= half) | (other < half))
                    there = there & ((me < half) | (other >= half))
                pl.when(here)(lambda j=j, side=side: chunk(j, me, other, side).wait_recv())
                pl.when(there)(lambda j=j, side=side: chunk(j, other, me, side).wait_send())
        return c

    lax.fori_loop(1, devices, settle, 0)
    pl.when(upper)(relay_sent)
    pl.when(lower)(relay_received)

    def add(r, c):
        total = down[r].astype(f32)
        for source in range(devices):
            total = total + zr[source, inv_ref[source, r]].astype(f32)
        col_ids = lax.broadcasted_iota(jnp.int32, total.shape, 1) + h * width
        o_ref[r] = jnp.where(col_ids < meta_ref[2 * states + 1 + r], total, 0.0)
        return c

    lax.fori_loop(0, sectors, add, 0)


def fused(at, inv, meta, whole, site):
    caps = LADDER[at]
    states, span, width = site.shape
    devices, sectors = inv.shape[0] // 2, inv.shape[1]
    rows = span // devices
    wide = sum(c > devices // 2 for c in caps)
    bf16 = jnp.bfloat16
    dma = pltpu.SemaphoreType.DMA
    return pl.pallas_call(
        functools.partial(kernel, caps),
        out_shape=jax.ShapeDtypeStruct((sectors, rows, width), jnp.float32),
        in_specs=[pl.BlockSpec(memory_space=pltpu.SMEM)] * 2 + [pl.BlockSpec(memory_space=pltpu.VMEM)] * 2,
        out_specs=pl.BlockSpec(memory_space=pltpu.VMEM),
        scratch_shapes=[
            pltpu.VMEM((wide, span, width), bf16),
            pltpu.VMEM((states, span, width), bf16),
            pltpu.VMEM((states, span, width), bf16),
            pltpu.VMEM((devices, states + 1, rows, width), bf16),
            pltpu.VMEM((devices // 2, states + 1, rows, width), bf16),
            pltpu.VMEM((sectors, rows, width), bf16),
            pltpu.VMEM((sectors, rows, width), bf16),
            pltpu.VMEM((span, 256), bf16),
            pltpu.VMEM((wide, width, 256), bf16),
            dma((wide,)), dma((wide,)), dma((wide,)), dma((wide,)),
            dma((states, devices)), dma((devices, states)),
            dma((states, devices // 2)), dma((devices // 2, states)), dma((sectors,)), dma((sectors,)),
        ],
        compiler_params=pltpu.CompilerParams(
            collective_id=1 + at, has_side_effects=True, vmem_limit_bytes=50 * 2**20),
        cost_estimate=pl.CostEstimate(
            flops=4 * states * span * span * width, bytes_accessed=16 * 2**20, transcendentals=0),
    )(inv, meta, whole, site)


def body(groups, devices, left_env, site_tensor, left_sizes, right_sizes, targets):
    states = site_tensor.shape[1]
    sectors = right_sizes.shape[0]
    others = groups * devices
    i32 = jnp.int32
    dma = pltpu.SemaphoreType.DMA
    smem = pl.BlockSpec(memory_space=pltpu.SMEM)
    vmem = pl.BlockSpec(memory_space=pltpu.VMEM)
    inv, meta, pick, whole, masked = pl.pallas_call(
        agree,
        out_shape=[
            jax.ShapeDtypeStruct((2 * devices, sectors), i32),
            jax.ShapeDtypeStruct((2 * states + 1 + sectors,), i32),
            jax.ShapeDtypeStruct((1,), i32),
            jax.ShapeDtypeStruct((site_tensor.shape[2],) * 2, jnp.bfloat16),
            jax.ShapeDtypeStruct(site_tensor.shape[1:], jnp.bfloat16),
        ],
        in_specs=[smem] * 3 + [pl.BlockSpec(memory_space=pltpu.HBM)] * 2,
        out_specs=[smem] * 3 + [vmem] * 2,
        scratch_shapes=[
            pltpu.VMEM((8, 128), i32), pltpu.VMEM((others, 8, 128), i32), pltpu.SMEM((others, 8, 128), i32),
            pltpu.VMEM(site_tensor.shape[1:], jnp.bfloat16),
            dma((others,)), dma((others,)), dma, dma, dma, dma, dma,
        ],
        compiler_params=pltpu.CompilerParams(collective_id=0, has_side_effects=True, vmem_limit_bytes=54 * 2**20),
    )(targets, left_sizes, right_sizes, left_env[0], site_tensor[0])
    branches = [functools.partial(fused, at) for at in range(len(LADDER))]
    return lax.switch(pick[0], branches, inv, meta, whole, masked)


def solution(mesh):
    in_specs = (
        P(("groups", "charge"), "split", None),
        P(("groups", "charge"), None, None, "split"),
        P(("groups", "charge")),
        P("groups"),
        P(("groups", "charge"), None),
    )
    out_specs = P("groups", "charge", "split")
    if mesh.shape["split"] == 2 and mesh.shape["charge"] == 8:
        inner = functools.partial(body, mesh.shape["groups"], mesh.shape["charge"])
    else:
        inner = gathered_body
    return jax.shard_map(inner, mesh=mesh, in_specs=in_specs, out_specs=out_specs, check_vma=False)
```

```python
import functools

import jax
import jax.numpy as jnp
from jax import lax
from jax.experimental import pallas as pl
from jax.experimental.pallas import tpu as pltpu
from jax.sharding import PartitionSpec as P

MESH = pl.DeviceIdType.MESH
HOST = (1, 0, 0, 1)
LADDER = (
    ((8, 7, 5, 4), (8, 7, 6, 6, 5, 3, 3, 3)),
    ((8, 8, 5, 4), (8, 8, 6, 6, 5, 3, 3, 3)),
    ((8, 8, 6, 6), (8, 8, 6, 6, 6, 4, 4, 4)),
    ((8, 8, 8, 8), (8, 8, 8, 8, 8, 8, 8, 8)),
)


def gathered_body(left_env, site_tensor, left_sizes, right_sizes, targets):
    states = site_tensor.shape[1]
    span = site_tensor.shape[2]
    width = site_tensor.shape[3]
    sectors = right_sizes.shape[0]
    column_base = lax.axis_index("split") * width
    row_ids = lax.broadcasted_iota(jnp.int32, (1, span, 1), 1)
    column_ids = lax.broadcasted_iota(jnp.int32, (1, 1, width), 2) + column_base
    slot_ids = lax.broadcasted_iota(jnp.int32, (states, sectors), 1)
    route = targets[0][:, None] == slot_ids
    live_cols = jnp.sum(jnp.where(route, right_sizes[None, :], 0), axis=1)
    keep = (row_ids < left_sizes[0]) & (column_ids < live_cols[:, None, None])
    masked = jnp.where(keep, site_tensor[0], jnp.zeros((), jnp.bfloat16))[None]
    product = jnp.einsum(
        "ik,skj->sij",
        lax.all_gather(left_env, "split", axis=1, tiled=True)[0],
        masked[0],
        preferred_element_type=jnp.float32,
    ).astype(jnp.bfloat16)
    terms = jnp.einsum(
        "ski,skj->sij",
        lax.all_gather(masked, "split", axis=3, tiled=True)[0],
        product,
        preferred_element_type=jnp.float32,
    ).astype(jnp.bfloat16)
    placed = jnp.einsum(
        "st,sij->tij", route.astype(jnp.bfloat16), terms, preferred_element_type=jnp.float32
    ).astype(jnp.bfloat16)
    return lax.psum_scatter(placed, "charge", scatter_dimension=1, tiled=True).astype(jnp.float32)


def agree(targets_ref, left_ref, right_ref, l_ref, m_ref, inv_ref, meta_ref, pick_ref, lf, ms,
          info, got, seen, site, send, recv, sem, lsend, lrecv, lown, mown):
    g = lax.axis_index("groups")
    me = lax.axis_index("charge")
    h = lax.axis_index("split")
    devices, sectors = inv_ref.shape[0], right_ref.shape[0]
    others = got.shape[0]
    states = targets_ref.shape[1]
    mine = g * devices + me
    rights = 2 * states + 1
    orders = rights + sectors
    ranks = orders + sectors

    barrier = pltpu.get_barrier_semaphore()

    def place(i):
        n = lax.rem(mine + i, others)
        return {"groups": n // devices, "charge": lax.rem(n, devices)}

    def greet(i, c):
        pl.semaphore_signal(barrier, inc=1, device_id=place(i), device_id_type=MESH)
        return c

    lax.fori_loop(1, others, greet, 0)
    pl.semaphore_signal(barrier, inc=1, device_id={"split": 1 - h}, device_id_type=MESH)

    span, width = ms.shape[1], ms.shape[2]
    half_rows = pl.ds(pl.multiple_of(h * width, width), width)
    m_own = pltpu.make_async_copy(m_ref, site, mown)
    m_own.start()
    l_own = pltpu.make_async_copy(l_ref, lf.at[half_rows], lown)
    l_own.start()
    every = [right_ref[r] for r in range(sectors)]
    place_of = []
    for r in range(sectors):
        ahead = jnp.int32(0)
        for k in range(sectors):
            if k != r:
                first = every[k] >= every[r] if k < r else every[k] > every[r]
                ahead = ahead + jnp.where(first, 1, 0)
        place_of.append(ahead)
        meta_ref[rights + r] = every[r]
        meta_ref[ranks + r] = ahead
    ordered = []
    for k in range(sectors):
        which, much = jnp.int32(0), jnp.int32(0)
        for r in range(sectors):
            which = jnp.where(place_of[r] == k, r, which)
            much = jnp.where(place_of[r] == k, every[r], much)
        meta_ref[orders + k] = which
        ordered.append(much)
    to = [targets_ref[0, j] for j in range(states)]
    size = [right_ref[t] for t in to]
    grade = [meta_ref[ranks + t] for t in to]
    rank = []
    for j in range(states):
        ahead = jnp.int32(0)
        for k in range(states):
            if k != j:
                ahead = ahead + jnp.where(grade[k] < grade[j], 1, 0)
        rank.append(ahead)
    lane = lax.broadcasted_iota(jnp.int32, info.shape, 1)
    packed = jnp.zeros(info.shape, jnp.int32)
    for slot in range(states):
        state, live, target = jnp.int32(0), jnp.int32(0), jnp.int32(0)
        for j in range(states):
            here = rank[j] == slot
            state = jnp.where(here, j, state)
            live = jnp.where(here, size[j], live)
            target = jnp.where(here, to[j], target)
        meta_ref[slot] = state
        meta_ref[states + slot] = live
        packed = jnp.where(lane == slot, target, packed)
        packed = jnp.where(lane == states + slot, live, packed)
    for k in range(sectors):
        packed = jnp.where(lane == 2 * states + k, ordered[k], packed)
    meta_ref[2 * states] = left_ref[0]
    info[...] = packed
    got[mine] = packed
    pl.semaphore_wait(barrier, others)
    l_copy = pltpu.make_async_remote_copy(
        src_ref=l_ref, dst_ref=lf.at[half_rows], send_sem=lsend, recv_sem=lrecv,
        device_id={"split": 1 - h}, device_id_type=MESH)
    l_copy.start()

    def copy(i):
        return pltpu.make_async_remote_copy(
            src_ref=info, dst_ref=got.at[mine], send_sem=send.at[i], recv_sem=recv.at[mine],
            device_id=place(i), device_id_type=MESH)

    def start(i, c):
        copy(i).start()
        return c

    def finish(i, c):
        n = lax.rem(mine + i, others)
        copy(i).wait_send()
        pltpu.make_async_remote_copy(
            src_ref=info, dst_ref=got.at[n], send_sem=send.at[i], recv_sem=recv.at[n],
            device_id=place(i), device_id_type=MESH).wait_recv()
        return c

    lax.fori_loop(1, others, start, 0)
    m_own.wait()

    def mask(j, c):
        state, live, deep = meta_ref[j], meta_ref[states + j], meta_ref[2 * states]

        def tile(i, c):
            part = pl.ds(pl.multiple_of(i * 128, 128), 128)
            row_ids = lax.broadcasted_iota(jnp.int32, (128, width), 0) + i * 128
            col_ids = lax.broadcasted_iota(jnp.int32, (128, width), 1) + h * width
            keep = (row_ids < deep) & (col_ids < live)
            ms[j, part] = jnp.where(keep, site[state, part].astype(jnp.float32), 0.0).astype(jnp.bfloat16)
            return c

        return lax.fori_loop(0, span // 128, tile, c)

    lax.fori_loop(0, states, mask, 0)
    lax.fori_loop(1, others, finish, 0)
    local = pltpu.make_async_copy(got, seen, sem)
    local.start()
    local.wait()

    half = devices // 2
    rows = span // devices
    side, seat = lax.div(me, half), lax.rem(me, half)
    for kind in range(2):
        block = (side if kind == 0 else 1 - side) * half + seat
        wants = [every[r] > jnp.maximum(block * rows, h * width) for r in range(sectors)]

        def route(s, c):
            reached = [seen[mine - seat + s, 0, j] for j in range(states)]
            for r in range(sectors):
                slot = jnp.int32(states)
                for j in range(states):
                    slot = jnp.where(reached[j] == r, j, slot)
                inv_ref[kind * half + s, r] = jnp.where(wants[r], slot, states)
            return c

        lax.fori_loop(0, half, route, 0)

    def widest(n, most):
        return tuple(jnp.maximum(m, seen[n, 0, states + j]) for j, m in enumerate(most))

    most = lax.fori_loop(0, others, widest, (jnp.int32(0),) * (states + sectors))
    pick = jnp.int32(len(LADDER) - 1)
    for at in range(len(LADDER) - 2, -1, -1):
        caps = LADDER[at][0] + LADDER[at][1]
        fits = most[0] <= caps[0] * rows
        for j in range(1, states + sectors):
            fits = fits & (most[j] <= caps[j] * rows)
        pick = jnp.where(fits, at, pick)
    pick_ref[0] = pick
    l_own.wait()
    l_copy.wait()


def kernel(caps, crops, inv_ref, meta_ref, lf, ms, o_ref, mr, pb, px, xb, tb, w0, w1, up, down,
           msend, mrecv, xsend, xrecv, zsend, zrecv, usend, drecv):
    me = lax.axis_index("charge")
    h = lax.axis_index("split")
    states, span, width = ms.shape
    sectors, rows = o_ref.shape[0], o_ref.shape[1]
    devices = span // rows
    half = devices // 2
    empty = states
    f32, bf16 = jnp.float32, jnp.bfloat16
    own, seat = lax.div(me, half), lax.rem(me, half)
    partner = {"charge": lax.rem(me + half, devices)}
    wide = [j for j in range(states) if caps[j] > half]
    rights, orders, ranks = 2 * states + 1, 2 * states + 1 + sectors, 2 * states + 1 + 2 * sectors

    def blocks(cap, side):
        return min(cap, half) if side == 0 else max(cap - half, 0)

    def live(cap, side):
        return blocks(cap, side) * rows

    barrier = pltpu.get_barrier_semaphore()
    pl.semaphore_signal(barrier, inc=1, device_id={"split": 1 - h}, device_id_type=MESH)
    pl.semaphore_signal(barrier, inc=1, device_id=partner, device_id_type=MESH)
    for i in range(1, half):
        pl.semaphore_signal(
            barrier, inc=1, device_id={"charge": own * half + lax.rem(seat + i, half)}, device_id_type=MESH)
    pl.semaphore_wait(barrier, half + 1)

    def m_copy(j):
        columns = pl.ds(0, live(caps[j], 1 - HOST[j]))
        return pltpu.make_async_remote_copy(
            src_ref=ms.at[j, :, columns], dst_ref=mr.at[j, :, columns], send_sem=msend.at[j],
            recv_sem=mrecv.at[j], device_id={"split": 1 - h}, device_id_type=MESH)

    def x_copy(j):
        s = HOST[j]
        deep, columns = live(caps[j], s), pl.ds(0, live(caps[j], 1 - s))
        return pltpu.make_async_remote_copy(
            src_ref=xb.at[j, pl.ds(0, deep), columns], dst_ref=tb.at[j, pl.ds(s * width, deep), columns],
            send_sem=xsend.at[j], recv_sem=xrecv.at[j], device_id={"split": 1 - h}, device_id_type=MESH)

    def chunk(j, part, side, to, source, kind):
        w = (w0, w1)[kind]
        columns = pl.ds(0, live(caps[j], side))
        from_rows = pl.ds(pl.multiple_of((part * half + to) * rows, rows), rows)
        return pltpu.make_async_remote_copy(
            src_ref=tb.at[j, from_rows, columns], dst_ref=w.at[source, j, :, columns],
            send_sem=zsend.at[j, part * half + to], recv_sem=zrecv.at[kind, source, j],
            device_id={"charge": own * half + to}, device_id_type=MESH)

    def scatter(j, part, side):
        for kind in range(2):
            pl.when(own == part ^ kind)(functools.partial(scatter_to, j, part, side, kind))

    def scatter_to(j, part, side, kind):
        count, columns = blocks(caps[j], part), live(caps[j], side)
        w = (w0, w1)[kind]

        def one(i, c):
            to = lax.rem(seat + 1 + i, count)

            @pl.when(to != seat)
            def _():
                chunk(j, part, side, to, seat, kind).start()

            @pl.when(to == seat)
            def _():
                from_rows = pl.ds(pl.multiple_of((part * half + to) * rows, rows), rows)
                w[seat, j, :, 0:columns] = tb[j, from_rows, 0:columns]

            return c

        lax.fori_loop(0, count, one, 0)

    def arrive(j, part, side, kind):
        if live(caps[j], side) == 0 or blocks(caps[j], part) == 0:
            return

        @pl.when(seat < blocks(caps[j], part))
        def _():
            def one(i, c):
                chunk(j, part, side, seat, lax.rem(seat + i, half), kind).wait_recv()
                return c

            lax.fori_loop(1, half, one, 0)

    def sent(j, part, side):
        count = blocks(caps[j], part)
        if live(caps[j], side) == 0 or count == 0:
            return

        def one(to, c):
            pl.when(to != seat)(lambda: chunk(j, part, side, to, seat, 0).wait_send())
            return c

        lax.fori_loop(0, count, one, 0)

    def hand(k, side):
        columns = pl.ds(0, live(crops[k], side))
        return pltpu.make_async_remote_copy(
            src_ref=up.at[k, :, columns], dst_ref=down.at[k, :, columns], send_sem=usend.at[k],
            recv_sem=drecv.at[k], device_id=partner, device_id_type=MESH)

    def handed(k, part, side, act):
        if live(crops[k], side) and blocks(crops[k], part):
            pl.when(seat < blocks(crops[k], part))(act)

    def relay(k, part, side):
        def act():
            columns = live(crops[k], side)
            r = meta_ref[orders + k]
            total = jnp.zeros((rows, columns), f32)
            for source in range(half):
                slot = inv_ref[half + source, r]
                if k < states - 1:
                    for j in range(k + 1):
                        total = total + jnp.where(slot == j, w1[source, j, :, 0:columns].astype(f32), 0.0)
                else:
                    total = total + w1[source, slot, :, 0:columns].astype(f32)
            up[k, :, 0:columns] = total.astype(bf16)
            hand(k, side).start()

        handed(k, part, side, act)

    def turns(n):
        return [(i, min(256, n - i)) for i in range(0, n, 256)]

    def product(j):
        def tile(i, c):
            part = pl.ds(pl.multiple_of(i * 256, 256), 256)
            pb[j, part] = jnp.dot(lf[part], ms[j], preferred_element_type=f32).astype(bf16)
            return c

        lax.fori_loop(0, span // 256, tile, 0)

    def flipped(columns, right):
        return lax.dot_general(columns, right, (((0,), (0,)), ((), ())), preferred_element_type=f32).astype(bf16)

    def near(j):
        product(j)
        for i in range(width // 256):
            part = pl.ds(pl.multiple_of(h * width + i * 256, 256), 256)
            tb[j, part] = flipped(ms[j, :, i * 256:(i + 1) * 256], pb[j])
        for side in range(2):
            if live(caps[j], side):
                pl.when(h == side)(functools.partial(scatter, j, side, side))

    def far(j, s, after=None):
        o = 1 - s
        columns = live(caps[j], o)
        m_copy(j).wait_recv()
        if after is not None:
            m_copy(after).start()

        def tile(i, c):
            part = pl.ds(pl.multiple_of(i * 256, 256), 256)
            px[part, 0:columns] = jnp.dot(lf[part], mr[j, :, 0:columns], preferred_element_type=f32).astype(bf16)
            return c

        lax.fori_loop(0, span // 256, tile, 0)
        for i, n in turns(live(caps[j], s)):
            xb[j, i:i + n, 0:columns] = flipped(ms[j, :, i:i + n], px[:, 0:columns])
        x_copy(j).start()
        for i, n in turns(columns):
            tb[j, o * width + i:o * width + i + n] = flipped(mr[j, :, i:i + n], pb[j])
        scatter(j, o, s)

    hosts = [[j for j in wide if HOST[j] == s] for s in range(2)]

    for s in range(2):
        if hosts[1 - s]:
            pl.when(h == s)(lambda s=s: m_copy(hosts[1 - s][0]).start())
    for j in range(states):
        if j in wide:
            near(j)
        else:
            pl.when(h == 0)(functools.partial(near, j))
    w0[:, empty] = jnp.zeros((half, rows, width), bf16)
    w1[:, empty] = jnp.zeros((half, rows, width), bf16)

    def pass_on(s, part, slots, some):
        @pl.when(own == 1 - part)
        def _():
            for j in slots:
                arrive(j, part, s, 1)
            for k in some:
                relay(k, part, s)

    def course(s):
        for j in range(states - 1):
            pass_on(s, s, [j], [j])
        mine, theirs = hosts[s], hosts[1 - s]
        done = 0
        for n, j in enumerate(mine):
            far(j, s, theirs[n + 1] if n + 1 < len(theirs) else None)
            if n == 0:
                pass_on(s, s, [states - 1], range(states - 1, sectors))
                if j == 0:
                    pass_on(s, 1 - s, [0], [0])
                    done = 1
        for n in range(len(mine) + 1, len(theirs)):
            m_copy(theirs[n]).start()
        for j in theirs:
            x_copy(j).wait_recv()
            scatter(j, 1 - s, s)
        for j in range(done, states - 1):
            pass_on(s, 1 - s, [j], [j])
        pass_on(s, 1 - s, [states - 1], range(states - 1, sectors))
        for part in range(2):
            @pl.when(own == part)
            def _():
                for j in range(states):
                    arrive(j, part, s, 0)

    for s in range(2):
        pl.when(h == s)(functools.partial(course, s))

    def gather(r, c):
        total = w0[0, inv_ref[0, r]].astype(f32)
        for source in range(1, half):
            total = total + w0[source, inv_ref[source, r]].astype(f32)
        o_ref[r] = total
        return c

    lax.fori_loop(0, sectors, gather, 0)

    def received(s):
        for part in range(2):
            @pl.when(own == part)
            def _():
                for k in range(sectors):
                    handed(k, part, s, lambda k=k: hand(k, s).wait_recv())

    for s in range(2):
        pl.when(h == s)(functools.partial(received, s))

    def add(r, c):
        size = meta_ref[rights + r]
        col_ids = lax.broadcasted_iota(jnp.int32, (rows, width), 1) + h * width
        limit = jnp.where(size > me * rows, size, 0)
        o_ref[r] = jnp.where(col_ids < limit, o_ref[r] + down[meta_ref[ranks + r]].astype(f32), 0.0)
        return c

    lax.fori_loop(0, sectors, add, 0)

    def settle(s):
        for j in hosts[1 - s]:
            m_copy(j).wait_send()
        for j in hosts[s]:
            x_copy(j).wait_send()
        for j in range(states):
            for part in range(2):
                sent(j, part, s)
        for part in range(2):
            @pl.when(own == 1 - part)
            def _():
                for k in range(sectors):
                    handed(k, part, s, lambda k=k: hand(k, s).wait_send())

    for s in range(2):
        pl.when(h == s)(functools.partial(settle, s))


def fused(at, inv, meta, whole, site):
    caps, crops = LADDER[at]
    states, span, width = site.shape
    devices, sectors = inv.shape
    rows, half = span // devices, devices // 2
    wide = max(j + 1 for j in range(states) if caps[j] > half)
    bf16 = jnp.bfloat16
    dma = pltpu.SemaphoreType.DMA
    return pl.pallas_call(
        functools.partial(kernel, caps, crops),
        out_shape=jax.ShapeDtypeStruct((sectors, rows, width), jnp.float32),
        in_specs=[pl.BlockSpec(memory_space=pltpu.SMEM)] * 2 + [pl.BlockSpec(memory_space=pltpu.VMEM)] * 2,
        out_specs=pl.BlockSpec(memory_space=pltpu.VMEM),
        scratch_shapes=[
            pltpu.VMEM((wide, span, width), bf16),
            pltpu.VMEM((states, span, width), bf16),
            pltpu.VMEM((span, width), bf16),
            pltpu.VMEM((wide, width, width), bf16),
            pltpu.VMEM((states, span, width), bf16),
            pltpu.VMEM((half, states + 1, rows, width), bf16),
            pltpu.VMEM((half, states + 1, rows, width), bf16),
            pltpu.VMEM((sectors, rows, width), bf16),
            pltpu.VMEM((sectors, rows, width), bf16),
            dma((wide,)), dma((wide,)), dma((wide,)), dma((wide,)),
            dma((states, devices)), dma((2, half, states)),
            dma((sectors,)), dma((sectors,)),
        ],
        compiler_params=pltpu.CompilerParams(
            collective_id=1 + at, has_side_effects=True, vmem_limit_bytes=50 * 2**20),
        cost_estimate=pl.CostEstimate(
            flops=4 * states * span * span * width, bytes_accessed=16 * 2**20, transcendentals=0),
    )(inv, meta, whole, site)


def body(groups, devices, left_env, site_tensor, left_sizes, right_sizes, targets):
    states = site_tensor.shape[1]
    sectors = right_sizes.shape[0]
    others = groups * devices
    i32 = jnp.int32
    dma = pltpu.SemaphoreType.DMA
    smem = pl.BlockSpec(memory_space=pltpu.SMEM)
    vmem = pl.BlockSpec(memory_space=pltpu.VMEM)
    inv, meta, pick, whole, masked = pl.pallas_call(
        agree,
        out_shape=[
            jax.ShapeDtypeStruct((devices, sectors), i32),
            jax.ShapeDtypeStruct((2 * states + 1 + 3 * sectors,), i32),
            jax.ShapeDtypeStruct((1,), i32),
            jax.ShapeDtypeStruct((site_tensor.shape[2],) * 2, jnp.bfloat16),
            jax.ShapeDtypeStruct(site_tensor.shape[1:], jnp.bfloat16),
        ],
        in_specs=[smem] * 3 + [pl.BlockSpec(memory_space=pltpu.HBM)] * 2,
        out_specs=[smem] * 3 + [vmem] * 2,
        scratch_shapes=[
            pltpu.VMEM((8, 128), i32), pltpu.VMEM((others, 8, 128), i32), pltpu.SMEM((others, 8, 128), i32),
            pltpu.VMEM(site_tensor.shape[1:], jnp.bfloat16),
            dma((others,)), dma((others,)), dma, dma, dma, dma, dma,
        ],
        compiler_params=pltpu.CompilerParams(collective_id=0, has_side_effects=True, vmem_limit_bytes=54 * 2**20),
    )(targets, left_sizes, right_sizes, left_env[0], site_tensor[0])
    branches = [functools.partial(fused, at) for at in range(len(LADDER))]
    return lax.switch(pick[0], branches, inv, meta, whole, masked)


def solution(mesh):
    in_specs = (
        P(("groups", "charge"), "split", None),
        P(("groups", "charge"), None, None, "split"),
        P(("groups", "charge")),
        P("groups"),
        P(("groups", "charge"), None),
    )
    out_specs = P("groups", "charge", "split")
    if mesh.shape["split"] == 2 and mesh.shape["charge"] == 8:
        inner = functools.partial(body, mesh.shape["groups"], mesh.shape["charge"])
    else:
        inner = gathered_body
    return jax.shard_map(inner, mesh=mesh, in_specs=in_specs, out_specs=out_specs, check_vma=False)
```

```python
import functools

import jax
import jax.numpy as jnp
from jax import lax
from jax.experimental import pallas as pl
from jax.experimental.pallas import tpu as pltpu
from jax.sharding import PartitionSpec as P

MESH = pl.DeviceIdType.MESH
HOST = (1, 0, 0, 0)
LADDER = (
    ((8, 8, 5, 4), (8, 8, 6, 5, 5, 3, 3, 3)),
    ((8, 8, 6, 5), (8, 8, 6, 6, 6, 4, 4, 4)),
    ((8, 8, 8, 8), (8, 8, 8, 8, 8, 8, 8, 8)),
)


def gathered_body(left_env, site_tensor, left_sizes, right_sizes, targets):
    states = site_tensor.shape[1]
    span = site_tensor.shape[2]
    width = site_tensor.shape[3]
    sectors = right_sizes.shape[0]
    column_base = lax.axis_index("split") * width
    row_ids = lax.broadcasted_iota(jnp.int32, (1, span, 1), 1)
    column_ids = lax.broadcasted_iota(jnp.int32, (1, 1, width), 2) + column_base
    slot_ids = lax.broadcasted_iota(jnp.int32, (states, sectors), 1)
    route = targets[0][:, None] == slot_ids
    live_cols = jnp.sum(jnp.where(route, right_sizes[None, :], 0), axis=1)
    keep = (row_ids < left_sizes[0]) & (column_ids < live_cols[:, None, None])
    masked = jnp.where(keep, site_tensor[0], jnp.zeros((), jnp.bfloat16))[None]
    product = jnp.einsum(
        "ik,skj->sij",
        lax.all_gather(left_env, "split", axis=1, tiled=True)[0],
        masked[0],
        preferred_element_type=jnp.float32,
    ).astype(jnp.bfloat16)
    terms = jnp.einsum(
        "ski,skj->sij",
        lax.all_gather(masked, "split", axis=3, tiled=True)[0],
        product,
        preferred_element_type=jnp.float32,
    ).astype(jnp.bfloat16)
    placed = jnp.einsum(
        "st,sij->tij", route.astype(jnp.bfloat16), terms, preferred_element_type=jnp.float32
    ).astype(jnp.bfloat16)
    return lax.psum_scatter(placed, "charge", scatter_dimension=1, tiled=True).astype(jnp.float32)


def agree(targets_ref, left_ref, right_ref, l_ref, m_ref, inv_ref, meta_ref, pick_ref, lf, ms,
          info, got, seen, site, send, recv, sem, lsend, lrecv, lown, mown):
    g = lax.axis_index("groups")
    me = lax.axis_index("charge")
    h = lax.axis_index("split")
    devices, sectors = inv_ref.shape[0], right_ref.shape[0]
    others = got.shape[0]
    states = targets_ref.shape[1]
    mine = g * devices + me
    rights = 2 * states + 1
    orders = rights + sectors
    ranks = orders + sectors

    barrier = pltpu.get_barrier_semaphore()

    def place(i):
        n = lax.rem(mine + i, others)
        return {"groups": n // devices, "charge": lax.rem(n, devices)}

    def greet(i, c):
        pl.semaphore_signal(barrier, inc=1, device_id=place(i), device_id_type=MESH)
        return c

    lax.fori_loop(1, others, greet, 0)
    pl.semaphore_signal(barrier, inc=1, device_id={"split": 1 - h}, device_id_type=MESH)

    span, width = ms.shape[1], ms.shape[2]
    half_rows = pl.ds(pl.multiple_of(h * width, width), width)
    m_own = pltpu.make_async_copy(m_ref, site, mown)
    m_own.start()
    l_own = pltpu.make_async_copy(l_ref, lf.at[half_rows], lown)
    l_own.start()
    every = [right_ref[r] for r in range(sectors)]
    place_of = []
    for r in range(sectors):
        ahead = jnp.int32(0)
        for k in range(sectors):
            if k != r:
                first = every[k] >= every[r] if k < r else every[k] > every[r]
                ahead = ahead + jnp.where(first, 1, 0)
        place_of.append(ahead)
        meta_ref[rights + r] = every[r]
        meta_ref[ranks + r] = ahead
    ordered = []
    for k in range(sectors):
        which, much = jnp.int32(0), jnp.int32(0)
        for r in range(sectors):
            which = jnp.where(place_of[r] == k, r, which)
            much = jnp.where(place_of[r] == k, every[r], much)
        meta_ref[orders + k] = which
        ordered.append(much)
    to = [targets_ref[0, j] for j in range(states)]
    size = [right_ref[t] for t in to]
    grade = [meta_ref[ranks + t] for t in to]
    rank = []
    for j in range(states):
        ahead = jnp.int32(0)
        for k in range(states):
            if k != j:
                ahead = ahead + jnp.where(grade[k] < grade[j], 1, 0)
        rank.append(ahead)
    lane = lax.broadcasted_iota(jnp.int32, info.shape, 1)
    packed = jnp.zeros(info.shape, jnp.int32)
    for slot in range(states):
        state, live, target = jnp.int32(0), jnp.int32(0), jnp.int32(0)
        for j in range(states):
            here = rank[j] == slot
            state = jnp.where(here, j, state)
            live = jnp.where(here, size[j], live)
            target = jnp.where(here, to[j], target)
        meta_ref[slot] = state
        meta_ref[states + slot] = live
        packed = jnp.where(lane == slot, target, packed)
        packed = jnp.where(lane == states + slot, live, packed)
    for k in range(sectors):
        packed = jnp.where(lane == 2 * states + k, ordered[k], packed)
    meta_ref[2 * states] = left_ref[0]
    info[...] = packed
    got[mine] = packed
    pl.semaphore_wait(barrier, others)
    l_copy = pltpu.make_async_remote_copy(
        src_ref=l_ref, dst_ref=lf.at[half_rows], send_sem=lsend, recv_sem=lrecv,
        device_id={"split": 1 - h}, device_id_type=MESH)
    l_copy.start()

    def copy(i):
        return pltpu.make_async_remote_copy(
            src_ref=info, dst_ref=got.at[mine], send_sem=send.at[i], recv_sem=recv.at[mine],
            device_id=place(i), device_id_type=MESH)

    def start(i, c):
        copy(i).start()
        return c

    def finish(i, c):
        n = lax.rem(mine + i, others)
        copy(i).wait_send()
        pltpu.make_async_remote_copy(
            src_ref=info, dst_ref=got.at[n], send_sem=send.at[i], recv_sem=recv.at[n],
            device_id=place(i), device_id_type=MESH).wait_recv()
        return c

    lax.fori_loop(1, others, start, 0)
    m_own.wait()

    def mask(j, c):
        state, live, deep = meta_ref[j], meta_ref[states + j], meta_ref[2 * states]

        def tile(i, c):
            part = pl.ds(pl.multiple_of(i * 128, 128), 128)
            row_ids = lax.broadcasted_iota(jnp.int32, (128, width), 0) + i * 128
            col_ids = lax.broadcasted_iota(jnp.int32, (128, width), 1) + h * width
            keep = (row_ids < deep) & (col_ids < live)
            ms[j, part] = jnp.where(keep, site[state, part].astype(jnp.float32), 0.0).astype(jnp.bfloat16)
            return c

        return lax.fori_loop(0, span // 128, tile, c)

    lax.fori_loop(0, states, mask, 0)
    lax.fori_loop(1, others, finish, 0)
    local = pltpu.make_async_copy(got, seen, sem)
    local.start()
    local.wait()

    half = devices // 2
    rows = span // devices
    side, seat = lax.div(me, half), lax.rem(me, half)
    for kind in range(2):
        block = (side if kind == 0 else 1 - side) * half + seat
        wants = [every[r] > jnp.maximum(block * rows, h * width) for r in range(sectors)]

        def route(s, c):
            reached = [seen[mine - seat + s, 0, j] for j in range(states)]
            for r in range(sectors):
                slot = jnp.int32(states)
                for j in range(states):
                    slot = jnp.where(reached[j] == r, j, slot)
                inv_ref[kind * half + s, r] = jnp.where(wants[r], slot, states)
            return c

        lax.fori_loop(0, half, route, 0)

    def widest(n, most):
        return tuple(jnp.maximum(m, seen[n, 0, states + j]) for j, m in enumerate(most))

    most = lax.fori_loop(0, others, widest, (jnp.int32(0),) * (states + sectors))
    pick = jnp.int32(len(LADDER) - 1)
    for at in range(len(LADDER) - 2, -1, -1):
        caps = LADDER[at][0] + LADDER[at][1]
        fits = most[0] <= caps[0] * rows
        for j in range(1, states + sectors):
            fits = fits & (most[j] <= caps[j] * rows)
        pick = jnp.where(fits, at, pick)
    pick_ref[0] = pick
    l_own.wait()
    l_copy.wait()


def kernel(caps, crops, inv_ref, meta_ref, lf, ms, o_ref, mr, pb, px, xb, tb, w0, w1, up, down,
           msend, mrecv, xsend, xrecv, zsend, zrecv, usend, drecv):
    me = lax.axis_index("charge")
    h = lax.axis_index("split")
    states, span, width = ms.shape
    sectors, rows = o_ref.shape[0], o_ref.shape[1]
    devices = span // rows
    half = devices // 2
    empty = states
    f32, bf16 = jnp.float32, jnp.bfloat16
    own, seat = lax.div(me, half), lax.rem(me, half)
    partner = {"charge": lax.rem(me + half, devices)}
    wide = [j for j in range(states) if caps[j] > half]
    rights, orders, ranks = 2 * states + 1, 2 * states + 1 + sectors, 2 * states + 1 + 2 * sectors

    def blocks(cap, side):
        return min(cap, half) if side == 0 else max(cap - half, 0)

    def live(cap, side):
        return blocks(cap, side) * rows

    barrier = pltpu.get_barrier_semaphore()
    pl.semaphore_signal(barrier, inc=1, device_id={"split": 1 - h}, device_id_type=MESH)
    pl.semaphore_signal(barrier, inc=1, device_id=partner, device_id_type=MESH)
    for i in range(1, half):
        pl.semaphore_signal(
            barrier, inc=1, device_id={"charge": own * half + lax.rem(seat + i, half)}, device_id_type=MESH)
    pl.semaphore_wait(barrier, half + 1)

    def m_copy(j):
        columns = pl.ds(0, live(caps[j], 1 - HOST[j]))
        return pltpu.make_async_remote_copy(
            src_ref=ms.at[j, :, columns], dst_ref=mr.at[j, :, columns], send_sem=msend.at[j],
            recv_sem=mrecv.at[j], device_id={"split": 1 - h}, device_id_type=MESH)

    def x_copy(j, b):
        s = HOST[j]
        columns = pl.ds(0, live(caps[j], 1 - s))
        here, there = (pl.ds(pl.multiple_of((n + b) * rows, rows), rows) for n in (0, s * half))
        return pltpu.make_async_remote_copy(
            src_ref=xb.at[j, here, columns], dst_ref=tb.at[j, there, columns],
            send_sem=xsend.at[j, b], recv_sem=xrecv.at[j, b], device_id={"split": 1 - h}, device_id_type=MESH)

    def chunk(j, part, side, to, source, kind):
        w = (w0, w1)[kind]
        columns = pl.ds(0, live(caps[j], side))
        from_rows = pl.ds(pl.multiple_of((part * half + to) * rows, rows), rows)
        return pltpu.make_async_remote_copy(
            src_ref=tb.at[j, from_rows, columns], dst_ref=w.at[source, j, :, columns],
            send_sem=zsend.at[j, part * half + to], recv_sem=zrecv.at[kind, source, j],
            device_id={"charge": own * half + to}, device_id_type=MESH)

    def forward(j, part, side, to):
        columns = live(caps[j], side)
        for kind in range(2):
            w = (w0, w1)[kind]

            @pl.when((own == part ^ kind) & (to != seat))
            def _():
                chunk(j, part, side, to, seat, kind).start()

            @pl.when((own == part ^ kind) & (to == seat))
            def _():
                def move(i, c):
                    here = pl.ds(pl.multiple_of((part * half + to) * rows + i * 32, 32), 32)
                    w[seat, j, pl.ds(pl.multiple_of(i * 32, 32), 32), 0:columns] = tb[j, here, 0:columns]
                    return c

                lax.fori_loop(0, rows // 32, move, 0)

    def scatter(j, part, side):
        count = blocks(caps[j], part)

        def one(i, c):
            forward(j, part, side, lax.rem(seat + 1 + i, count))
            return c

        lax.fori_loop(0, count, one, 0)

    def arrive(j, part, side, kind):
        if live(caps[j], side) == 0 or blocks(caps[j], part) == 0:
            return

        @pl.when(seat < blocks(caps[j], part))
        def _():
            def one(i, c):
                chunk(j, part, side, seat, lax.rem(seat + i, half), kind).wait_recv()
                return c

            lax.fori_loop(1, half, one, 0)

    def sent(j, part, side):
        count = blocks(caps[j], part)
        if live(caps[j], side) == 0 or count == 0:
            return

        def one(to, c):
            pl.when(to != seat)(lambda: chunk(j, part, side, to, seat, 0).wait_send())
            return c

        lax.fori_loop(0, count, one, 0)

    def hand(k, side):
        columns = pl.ds(0, live(crops[k], side))
        return pltpu.make_async_remote_copy(
            src_ref=up.at[k, :, columns], dst_ref=down.at[k, :, columns], send_sem=usend.at[k],
            recv_sem=drecv.at[k], device_id=partner, device_id_type=MESH)

    def handed(k, part, side, act):
        if live(crops[k], side) and blocks(crops[k], part):
            pl.when(seat < blocks(crops[k], part))(act)

    def relay(k, part, side, full):
        def act():
            columns = live(crops[k], side)
            r = meta_ref[orders + k]
            slots = [inv_ref[half + source, r] for source in range(half)]

            def tile(i, c):
                at = pl.ds(pl.multiple_of(i * 32, 32), 32)
                total = jnp.zeros((32, columns), f32)
                for source in range(half):
                    if full:
                        total = total + w1[source, slots[source], at, 0:columns].astype(f32)
                    else:
                        for j in range(k + 1):
                            part = w1[source, j, at, 0:columns].astype(f32)
                            total = total + jnp.where(slots[source] == j, part, 0.0)
                up[k, at, 0:columns] = total.astype(bf16)
                return c

            lax.fori_loop(0, rows // 32, tile, 0)
            hand(k, side).start()

        handed(k, part, side, act)

    def product(j):
        def tile(i, c):
            part = pl.ds(pl.multiple_of(i * 256, 256), 256)
            pb[j, part] = jnp.dot(lf[part], ms[j], preferred_element_type=f32).astype(bf16)
            return c

        lax.fori_loop(0, span // 256, tile, 0)

    def flipped(columns, right):
        return lax.dot_general(columns, right, (((0,), (0,)), ((), ())), preferred_element_type=f32).astype(bf16)

    def near(j):
        product(j)

        def tile(i, c):
            part = pl.ds(pl.multiple_of(h * width + i * 256, 256), 256)
            tb[j, part] = flipped(ms[j, :, pl.ds(pl.multiple_of(i * 256, 256), 256)], pb[j])
            return c

        lax.fori_loop(0, width // 256, tile, 0)
        for side in range(2):
            if live(caps[j], side):
                pl.when(h == side)(functools.partial(scatter, j, side, side))

    def far(j, s):
        o = 1 - s
        columns = live(caps[j], o)
        m_copy(j).wait_recv()

        def tile(i, c):
            part = pl.ds(pl.multiple_of(i * 256, 256), 256)
            px[part, 0:columns] = jnp.dot(lf[part], mr[j, :, 0:columns], preferred_element_type=f32).astype(bf16)
            return c

        lax.fori_loop(0, span // 256, tile, 0)

        def back(i, c):
            part = pl.ds(pl.multiple_of(i * rows, rows), rows)
            xb[j, part, 0:columns] = flipped(ms[j, :, part], px[:, 0:columns])
            x_copy(j, i).start()
            return c

        lax.fori_loop(0, blocks(caps[j], s), back, 0)

        def there(i, c):
            part = pl.ds(pl.multiple_of(o * width + i * rows, rows), rows)
            tb[j, part] = flipped(mr[j, :, pl.ds(pl.multiple_of(i * rows, rows), rows)], pb[j])
            return c

        lax.fori_loop(0, blocks(caps[j], o), there, 0)
        scatter(j, o, s)

    hosts = [[j for j in reversed(wide) if HOST[j] == s] for s in range(2)]
    for s in range(2):
        @pl.when(h == s)
        def _():
            for j in hosts[1 - s]:
                m_copy(j).start()
    for j in range(states):
        if j in wide:
            near(j)
        else:
            pl.when(h == 0)(functools.partial(near, j))
    w0[:, empty] = jnp.zeros((half, rows, width), bf16)
    w1[:, empty] = jnp.zeros((half, rows, width), bf16)

    def pass_on(s, part, slots, some, full):
        @pl.when(own == 1 - part)
        def _():
            for j in slots:
                arrive(j, part, s, 1)
            for k in some:
                relay(k, part, s, full)

    def course(s):
        for j in range(states - 1):
            pass_on(s, s, [j], [j], False)
        last = functools.partial(pass_on, s, s, [states - 1], range(states - 1, sectors), True)
        mine, theirs = hosts[s], hosts[1 - s]
        done = int(mine == [0])
        for j in mine[:-1]:
            far(j, s)
        far(mine[-1], s)
        if done:
            last()
            pass_on(s, 1 - s, [0], [0], False)
        for j in theirs[:-1]:
            def step(b, c, j=j):
                x_copy(j, b).wait_recv()
                forward(j, 1 - s, s, b)
                return c

            lax.fori_loop(0, blocks(caps[j], 1 - s), step, 0)
        j = theirs[-1]
        count = blocks(caps[j], 1 - s)

        def step(b, c):
            x_copy(j, b).wait_recv()
            forward(j, 1 - s, s, b)
            return c

        lax.fori_loop(0, count, step, 0)
        pass_on(s, 1 - s, range(done, states), range(done, sectors), True)
        if not done:
            last()
        for part in range(2):
            @pl.when(own == part)
            def _():
                for j in range(states):
                    arrive(j, part, s, 0)

    for s in range(2):
        pl.when(h == s)(functools.partial(course, s))

    def gather(r, c):
        total = w0[0, inv_ref[0, r]].astype(f32)
        for source in range(1, half):
            total = total + w0[source, inv_ref[source, r]].astype(f32)
        o_ref[r] = total
        return c

    lax.fori_loop(0, sectors, gather, 0)

    def received(s):
        for part in range(2):
            @pl.when(own == part)
            def _():
                for k in range(sectors):
                    handed(k, part, s, lambda k=k: hand(k, s).wait_recv())

    for s in range(2):
        pl.when(h == s)(functools.partial(received, s))

    def add(r, c):
        size = meta_ref[rights + r]
        col_ids = lax.broadcasted_iota(jnp.int32, (rows, width), 1) + h * width
        limit = jnp.where(size > me * rows, size, 0)
        o_ref[r] = jnp.where(col_ids < limit, o_ref[r] + down[meta_ref[ranks + r]].astype(f32), 0.0)
        return c

    lax.fori_loop(0, sectors, add, 0)

    def settle(s):
        for j in hosts[1 - s]:
            m_copy(j).wait_send()
        for j in hosts[s]:
            def left(b, c, j=j):
                x_copy(j, b).wait_send()
                return c

            lax.fori_loop(0, blocks(caps[j], s), left, 0)
        for j in range(states):
            for part in range(2):
                sent(j, part, s)
        for part in range(2):
            @pl.when(own == 1 - part)
            def _():
                for k in range(sectors):
                    handed(k, part, s, lambda k=k: hand(k, s).wait_send())

    for s in range(2):
        pl.when(h == s)(functools.partial(settle, s))


def fused(at, inv, meta, whole, site):
    caps, crops = LADDER[at]
    states, span, width = site.shape
    devices, sectors = inv.shape
    rows, half = span // devices, devices // 2
    wide = max(j + 1 for j in range(states) if caps[j] > half)
    bf16 = jnp.bfloat16
    dma = pltpu.SemaphoreType.DMA
    return pl.pallas_call(
        functools.partial(kernel, caps, crops),
        out_shape=jax.ShapeDtypeStruct((sectors, rows, width), jnp.float32),
        in_specs=[pl.BlockSpec(memory_space=pltpu.SMEM)] * 2 + [pl.BlockSpec(memory_space=pltpu.VMEM)] * 2,
        out_specs=pl.BlockSpec(memory_space=pltpu.VMEM),
        scratch_shapes=[
            pltpu.VMEM((wide, span, width), bf16),
            pltpu.VMEM((states, span, width), bf16),
            pltpu.VMEM((span, width), bf16),
            pltpu.VMEM((wide, width, width), bf16),
            pltpu.VMEM((states, span, width), bf16),
            pltpu.VMEM((half, states + 1, rows, width), bf16),
            pltpu.VMEM((half, states + 1, rows, width), bf16),
            pltpu.VMEM((sectors, rows, width), bf16),
            pltpu.VMEM((sectors, rows, width), bf16),
            dma((wide,)), dma((wide,)), dma((wide, half)), dma((wide, half)),
            dma((states, devices)), dma((2, half, states)),
            dma((sectors,)), dma((sectors,)),
        ],
        compiler_params=pltpu.CompilerParams(
            collective_id=1 + at, has_side_effects=True, vmem_limit_bytes=50 * 2**20),
        cost_estimate=pl.CostEstimate(
            flops=4 * states * span * span * width, bytes_accessed=16 * 2**20, transcendentals=0),
    )(inv, meta, whole, site)


def body(groups, devices, left_env, site_tensor, left_sizes, right_sizes, targets):
    states = site_tensor.shape[1]
    sectors = right_sizes.shape[0]
    others = groups * devices
    i32 = jnp.int32
    dma = pltpu.SemaphoreType.DMA
    smem = pl.BlockSpec(memory_space=pltpu.SMEM)
    vmem = pl.BlockSpec(memory_space=pltpu.VMEM)
    inv, meta, pick, whole, masked = pl.pallas_call(
        agree,
        out_shape=[
            jax.ShapeDtypeStruct((devices, sectors), i32),
            jax.ShapeDtypeStruct((2 * states + 1 + 3 * sectors,), i32),
            jax.ShapeDtypeStruct((1,), i32),
            jax.ShapeDtypeStruct((site_tensor.shape[2],) * 2, jnp.bfloat16),
            jax.ShapeDtypeStruct(site_tensor.shape[1:], jnp.bfloat16),
        ],
        in_specs=[smem] * 3 + [pl.BlockSpec(memory_space=pltpu.HBM)] * 2,
        out_specs=[smem] * 3 + [vmem] * 2,
        scratch_shapes=[
            pltpu.VMEM((8, 128), i32), pltpu.VMEM((others, 8, 128), i32), pltpu.SMEM((others, 8, 128), i32),
            pltpu.VMEM(site_tensor.shape[1:], jnp.bfloat16),
            dma((others,)), dma((others,)), dma, dma, dma, dma, dma,
        ],
        compiler_params=pltpu.CompilerParams(collective_id=0, has_side_effects=True, vmem_limit_bytes=54 * 2**20),
    )(targets, left_sizes, right_sizes, left_env[0], site_tensor[0])
    branches = [functools.partial(fused, at) for at in range(len(LADDER))]
    return lax.switch(pick[0], branches, inv, meta, whole, masked)


def solution(mesh):
    in_specs = (
        P(("groups", "charge"), "split", None),
        P(("groups", "charge"), None, None, "split"),
        P(("groups", "charge")),
        P("groups"),
        P(("groups", "charge"), None),
    )
    out_specs = P("groups", "charge", "split")
    if mesh.shape["split"] == 2 and mesh.shape["charge"] == 8:
        inner = functools.partial(body, mesh.shape["groups"], mesh.shape["charge"])
    else:
        inner = gathered_body
    return jax.shard_map(inner, mesh=mesh, in_specs=in_specs, out_specs=out_specs, check_vma=False)
```

```python
import functools

import jax
import jax.numpy as jnp
from jax import lax
from jax.experimental import pallas as pl
from jax.experimental.pallas import tpu as pltpu
from jax.sharding import PartitionSpec as P

MESH = pl.DeviceIdType.MESH
HOST = (1, 0, 0, 0)
AROUND = 5
LADDER = (
    ((8, 8, 5, 4), (8, 8, 5, 5, 4, 3, 3, 3)),
    ((8, 8, 6, 4), (8, 8, 6, 6, 5, 3, 3, 3)),
    ((8, 8, 6, 5), (8, 8, 6, 6, 6, 4, 4, 4)),
    ((8, 8, 8, 8), (8, 8, 8, 8, 8, 8, 8, 8)),
)


def gathered_body(left_env, site_tensor, left_sizes, right_sizes, targets):
    states = site_tensor.shape[1]
    span = site_tensor.shape[2]
    width = site_tensor.shape[3]
    sectors = right_sizes.shape[0]
    column_base = lax.axis_index("split") * width
    row_ids = lax.broadcasted_iota(jnp.int32, (1, span, 1), 1)
    column_ids = lax.broadcasted_iota(jnp.int32, (1, 1, width), 2) + column_base
    slot_ids = lax.broadcasted_iota(jnp.int32, (states, sectors), 1)
    route = targets[0][:, None] == slot_ids
    live_cols = jnp.sum(jnp.where(route, right_sizes[None, :], 0), axis=1)
    keep = (row_ids < left_sizes[0]) & (column_ids < live_cols[:, None, None])
    masked = jnp.where(keep, site_tensor[0], jnp.zeros((), jnp.bfloat16))[None]
    product = jnp.einsum(
        "ik,skj->sij",
        lax.all_gather(left_env, "split", axis=1, tiled=True)[0],
        masked[0],
        preferred_element_type=jnp.float32,
    ).astype(jnp.bfloat16)
    terms = jnp.einsum(
        "ski,skj->sij",
        lax.all_gather(masked, "split", axis=3, tiled=True)[0],
        product,
        preferred_element_type=jnp.float32,
    ).astype(jnp.bfloat16)
    placed = jnp.einsum(
        "st,sij->tij", route.astype(jnp.bfloat16), terms, preferred_element_type=jnp.float32
    ).astype(jnp.bfloat16)
    return lax.psum_scatter(placed, "charge", scatter_dimension=1, tiled=True).astype(jnp.float32)


def agree(targets_ref, left_ref, right_ref, l_ref, m_ref, inv_ref, meta_ref, pick_ref, lf, ms,
          info, got, seen, site, send, recv, sem, lsend, lrecv, lown, mown):
    g = lax.axis_index("groups")
    me = lax.axis_index("charge")
    h = lax.axis_index("split")
    devices, sectors = inv_ref.shape[0], right_ref.shape[0]
    others = got.shape[0]
    states = targets_ref.shape[1]
    mine = g * devices + me
    rights = 2 * states + 1
    orders = rights + sectors
    ranks = orders + sectors

    barrier = pltpu.get_barrier_semaphore()

    def place(i):
        n = lax.rem(mine + i, others)
        return {"groups": n // devices, "charge": lax.rem(n, devices)}

    def greet(i, c):
        pl.semaphore_signal(barrier, inc=1, device_id=place(i), device_id_type=MESH)
        return c

    lax.fori_loop(1, others, greet, 0)
    pl.semaphore_signal(barrier, inc=1, device_id={"split": 1 - h}, device_id_type=MESH)

    span, width = ms.shape[1], ms.shape[2]
    half_rows = pl.ds(pl.multiple_of(h * width, width), width)
    m_own = pltpu.make_async_copy(m_ref, site, mown)
    m_own.start()
    l_own = pltpu.make_async_copy(l_ref, lf.at[half_rows], lown)
    l_own.start()
    every = [right_ref[r] for r in range(sectors)]
    place_of = []
    for r in range(sectors):
        ahead = jnp.int32(0)
        for k in range(sectors):
            if k != r:
                first = every[k] >= every[r] if k < r else every[k] > every[r]
                ahead = ahead + jnp.where(first, 1, 0)
        place_of.append(ahead)
        meta_ref[rights + r] = every[r]
        meta_ref[ranks + r] = ahead
    ordered = []
    for k in range(sectors):
        which, much = jnp.int32(0), jnp.int32(0)
        for r in range(sectors):
            which = jnp.where(place_of[r] == k, r, which)
            much = jnp.where(place_of[r] == k, every[r], much)
        meta_ref[orders + k] = which
        ordered.append(much)
    to = [targets_ref[0, j] for j in range(states)]
    size = [right_ref[t] for t in to]
    grade = [meta_ref[ranks + t] for t in to]
    rank = []
    for j in range(states):
        ahead = jnp.int32(0)
        for k in range(states):
            if k != j:
                ahead = ahead + jnp.where(grade[k] < grade[j], 1, 0)
        rank.append(ahead)
    lane = lax.broadcasted_iota(jnp.int32, info.shape, 1)
    packed = jnp.zeros(info.shape, jnp.int32)
    for slot in range(states):
        state, live, target = jnp.int32(0), jnp.int32(0), jnp.int32(0)
        for j in range(states):
            here = rank[j] == slot
            state = jnp.where(here, j, state)
            live = jnp.where(here, size[j], live)
            target = jnp.where(here, to[j], target)
        meta_ref[slot] = state
        meta_ref[states + slot] = live
        packed = jnp.where(lane == slot, target, packed)
        packed = jnp.where(lane == states + slot, live, packed)
    for k in range(sectors):
        packed = jnp.where(lane == 2 * states + k, ordered[k], packed)
    meta_ref[2 * states] = left_ref[0]
    info[...] = packed
    got[mine] = packed
    pl.semaphore_wait(barrier, others)
    l_copy = pltpu.make_async_remote_copy(
        src_ref=l_ref, dst_ref=lf.at[half_rows], send_sem=lsend, recv_sem=lrecv,
        device_id={"split": 1 - h}, device_id_type=MESH)
    l_copy.start()

    def copy(i):
        return pltpu.make_async_remote_copy(
            src_ref=info, dst_ref=got.at[mine], send_sem=send.at[i], recv_sem=recv.at[mine],
            device_id=place(i), device_id_type=MESH)

    def start(i, c):
        copy(i).start()
        return c

    def finish(i, c):
        n = lax.rem(mine + i, others)
        copy(i).wait_send()
        pltpu.make_async_remote_copy(
            src_ref=info, dst_ref=got.at[n], send_sem=send.at[i], recv_sem=recv.at[n],
            device_id=place(i), device_id_type=MESH).wait_recv()
        return c

    lax.fori_loop(1, others, start, 0)
    m_own.wait()

    def mask(j, c):
        state, live, deep = meta_ref[j], meta_ref[states + j], meta_ref[2 * states]

        def tile(i, c):
            part = pl.ds(pl.multiple_of(i * 128, 128), 128)
            row_ids = lax.broadcasted_iota(jnp.int32, (128, width), 0) + i * 128
            col_ids = lax.broadcasted_iota(jnp.int32, (128, width), 1) + h * width
            keep = (row_ids < deep) & (col_ids < live)
            ms[j, part] = jnp.where(keep, site[state, part].astype(jnp.float32), 0.0).astype(jnp.bfloat16)
            return c

        return lax.fori_loop(0, span // 128, tile, c)

    lax.fori_loop(0, states, mask, 0)
    lax.fori_loop(1, others, finish, 0)
    local = pltpu.make_async_copy(got, seen, sem)
    local.start()
    local.wait()

    half = devices // 2
    rows = span // devices
    side, seat = lax.div(me, half), lax.rem(me, half)
    for kind in range(2):
        block = (side if kind == 0 else 1 - side) * half + seat
        wants = [every[r] > jnp.maximum(block * rows, h * width) for r in range(sectors)]

        def route(s, c):
            reached = [seen[mine - seat + s, 0, j] for j in range(states)]
            for r in range(sectors):
                slot = jnp.int32(states)
                for j in range(states):
                    slot = jnp.where(reached[j] == r, j, slot)
                inv_ref[kind * half + s, r] = jnp.where(wants[r], slot, states)
            return c

        lax.fori_loop(0, half, route, 0)

    def widest(n, most):
        return tuple(jnp.maximum(m, seen[n, 0, states + j]) for j, m in enumerate(most))

    most = lax.fori_loop(0, others, widest, (jnp.int32(0),) * (states + sectors))
    pick = jnp.int32(len(LADDER) - 1)
    for at in range(len(LADDER) - 2, -1, -1):
        caps = LADDER[at][0] + LADDER[at][1]
        fits = most[0] <= caps[0] * rows
        for j in range(1, states + sectors):
            fits = fits & (most[j] <= caps[j] * rows)
        pick = jnp.where(fits, at, pick)
    pick_ref[0] = pick
    l_own.wait()
    l_copy.wait()


def kernel(caps, crops, inv_ref, meta_ref, lf, ms, o_ref, mr, pb, px, xb, tb, w0, w1, up, down, via,
           msend, mrecv, xsend, xrecv, zsend, zrecv, usend, drecv, vsend, vrecv, fsend):
    me = lax.axis_index("charge")
    h = lax.axis_index("split")
    states, span, width = ms.shape
    sectors, rows = o_ref.shape[0], o_ref.shape[1]
    devices = span // rows
    half = devices // 2
    empty = states
    f32, bf16 = jnp.float32, jnp.bfloat16
    own, seat = lax.div(me, half), lax.rem(me, half)
    partner = {"charge": lax.rem(me + half, devices)}
    wide = [j for j in range(states) if caps[j] > half]
    rights, orders, ranks = 2 * states + 1, 2 * states + 1 + sectors, 2 * states + 1 + 2 * sectors

    def blocks(cap, side):
        return min(cap, half) if side == 0 else max(cap - half, 0)

    def live(cap, side):
        return blocks(cap, side) * rows

    barrier = pltpu.get_barrier_semaphore()
    pl.semaphore_signal(barrier, inc=1, device_id={"split": 1 - h}, device_id_type=MESH)
    pl.semaphore_signal(barrier, inc=1, device_id=partner, device_id_type=MESH)
    across = {"charge": lax.rem(me + half, devices), "split": 1 - h}
    pl.semaphore_signal(barrier, inc=1, device_id=across, device_id_type=MESH)
    for i in range(1, half):
        pl.semaphore_signal(
            barrier, inc=1, device_id={"charge": own * half + lax.rem(seat + i, half)}, device_id_type=MESH)
    pl.semaphore_wait(barrier, half + 2)

    def m_copy(j):
        columns = pl.ds(0, live(caps[j], 1 - HOST[j]))
        return pltpu.make_async_remote_copy(
            src_ref=ms.at[j, :, columns], dst_ref=mr.at[j, :, columns], send_sem=msend.at[j],
            recv_sem=mrecv.at[j], device_id={"split": 1 - h}, device_id_type=MESH)

    def x_copy(j, b):
        s = HOST[j]
        columns = pl.ds(0, live(caps[j], 1 - s))
        here, there = (pl.ds(pl.multiple_of((n + b) * rows, rows), rows) for n in (0, s * half))
        return pltpu.make_async_remote_copy(
            src_ref=xb.at[j, here, columns], dst_ref=tb.at[j, there, columns],
            send_sem=xsend.at[j, b], recv_sem=xrecv.at[j, b], device_id={"split": 1 - h}, device_id_type=MESH)

    def chunk(j, part, side, to, source, kind):
        w = (w0, w1)[kind]
        columns = pl.ds(0, live(caps[j], side))
        from_rows = pl.ds(pl.multiple_of((part * half + to) * rows, rows), rows)
        return pltpu.make_async_remote_copy(
            src_ref=tb.at[j, from_rows, columns], dst_ref=w.at[source, j, :, columns],
            send_sem=zsend.at[j, part * half + to], recv_sem=zrecv.at[kind, source, j],
            device_id={"charge": own * half + to}, device_id_type=MESH)

    def forward(j, part, side, to):
        columns = live(caps[j], side)
        for kind in range(2):
            w = (w0, w1)[kind]

            @pl.when((own == part ^ kind) & (to != seat))
            def _():
                chunk(j, part, side, to, seat, kind).start()

            @pl.when((own == part ^ kind) & (to == seat))
            def _():
                def move(i, c):
                    here = pl.ds(pl.multiple_of((part * half + to) * rows + i * 32, 32), 32)
                    w[seat, j, pl.ds(pl.multiple_of(i * 32, 32), 32), 0:columns] = tb[j, here, 0:columns]
                    return c

                lax.fori_loop(0, rows // 32, move, 0)

    def scatter(j, part, side):
        count = blocks(caps[j], part)

        def one(i, c):
            forward(j, part, side, lax.rem(seat + 1 + i, count))
            return c

        lax.fori_loop(0, count, one, 0)

    def arrive(j, part, side, kind):
        if live(caps[j], side) == 0 or blocks(caps[j], part) == 0:
            return

        @pl.when(seat < blocks(caps[j], part))
        def _():
            def one(i, c):
                chunk(j, part, side, seat, lax.rem(seat + i, half), kind).wait_recv()
                return c

            lax.fori_loop(1, half, one, 0)

    def sent(j, part, side):
        count = blocks(caps[j], part)
        if live(caps[j], side) == 0 or count == 0:
            return

        def one(to, c):
            pl.when(to != seat)(lambda: chunk(j, part, side, to, seat, 0).wait_send())
            return c

        lax.fori_loop(0, count, one, 0)

    def hand(k, side):
        columns = pl.ds(0, live(crops[k], side))
        return pltpu.make_async_remote_copy(
            src_ref=up.at[k, :, columns], dst_ref=down.at[k, :, columns], send_sem=usend.at[k],
            recv_sem=drecv.at[k], device_id=partner, device_id_type=MESH)

    def aside(k):
        columns = pl.ds(0, live(crops[k], 0))
        return pltpu.make_async_remote_copy(
            src_ref=up.at[k, :, columns], dst_ref=via.at[k - AROUND, :, columns], send_sem=vsend.at[k - AROUND],
            recv_sem=vrecv.at[k - AROUND], device_id={"split": 1 - h}, device_id_type=MESH)

    def diagonal(k):
        columns = pl.ds(0, live(crops[k], 0))
        return pltpu.make_async_remote_copy(
            src_ref=via.at[k - AROUND, :, columns], dst_ref=down.at[k, :, columns], send_sem=fsend.at[k - AROUND],
            recv_sem=drecv.at[k], device_id=across, device_id_type=MESH)

    def handed(k, part, side, act):
        if live(crops[k], side) and blocks(crops[k], part):
            pl.when(seat < blocks(crops[k], part))(act)

    def relay(k, part, side, full):
        def act():
            columns = live(crops[k], side)
            r = meta_ref[orders + k]
            slots = [inv_ref[half + source, r] for source in range(half)]

            def tile(i, c):
                at = pl.ds(pl.multiple_of(i * 32, 32), 32)
                total = jnp.zeros((32, columns), f32)
                for source in range(half):
                    if full:
                        total = total + w1[source, slots[source], at, 0:columns].astype(f32)
                    else:
                        for j in range(k + 1):
                            one = w1[source, j, at, 0:columns].astype(f32)
                            total = total + jnp.where(slots[source] == j, one, 0.0)
                up[k, at, 0:columns] = total.astype(bf16)
                return c

            lax.fori_loop(0, rows // 32, tile, 0)
            (aside(k) if part == side == 0 and k >= AROUND else hand(k, side)).start()

        handed(k, part, side, act)

    def product(j):
        def tile(i, c):
            part = pl.ds(pl.multiple_of(i * 256, 256), 256)
            pb[j, part] = jnp.dot(lf[part], ms[j], preferred_element_type=f32).astype(bf16)
            return c

        lax.fori_loop(0, span // 256, tile, 0)

    def flipped(columns, right):
        return lax.dot_general(columns, right, (((0,), (0,)), ((), ())), preferred_element_type=f32).astype(bf16)

    def near(j):
        product(j)

        def tile(i, c):
            part = pl.ds(pl.multiple_of(h * width + i * 256, 256), 256)
            tb[j, part] = flipped(ms[j, :, pl.ds(pl.multiple_of(i * 256, 256), 256)], pb[j])
            return c

        lax.fori_loop(0, width // 256, tile, 0)
        for side in range(2):
            if live(caps[j], side):
                pl.when(h == side)(functools.partial(scatter, j, side, side))

    def far(j, s):
        o = 1 - s
        columns = live(caps[j], o)
        m_copy(j).wait_recv()

        def tile(i, c):
            part = pl.ds(pl.multiple_of(i * 256, 256), 256)
            px[part, 0:columns] = jnp.dot(lf[part], mr[j, :, 0:columns], preferred_element_type=f32).astype(bf16)
            return c

        lax.fori_loop(0, span // 256, tile, 0)

        def back(i, c):
            part = pl.ds(pl.multiple_of(i * rows, rows), rows)
            xb[j, part, 0:columns] = flipped(ms[j, :, part], px[:, 0:columns])
            x_copy(j, i).start()
            return c

        lax.fori_loop(0, blocks(caps[j], s), back, 0)

        def there(i, c):
            part = pl.ds(pl.multiple_of(o * width + i * rows, rows), rows)
            tb[j, part] = flipped(mr[j, :, pl.ds(pl.multiple_of(i * rows, rows), rows)], pb[j])
            return c

        lax.fori_loop(0, blocks(caps[j], o), there, 0)
        scatter(j, o, s)

    hosts = [[j for j in reversed(wide) if HOST[j] == s] for s in range(2)]
    for s in range(2):
        @pl.when(h == s)
        def _():
            for j in hosts[1 - s]:
                m_copy(j).start()
    for j in range(states):
        if j in wide:
            near(j)
        else:
            pl.when(h == 0)(functools.partial(near, j))
    w0[:, empty] = jnp.zeros((half, rows, width), bf16)
    w1[:, empty] = jnp.zeros((half, rows, width), bf16)

    def pass_on(s, part, slots, some, full):
        @pl.when(own == 1 - part)
        def _():
            for j in slots:
                arrive(j, part, s, 1)
            for k in some:
                relay(k, part, s, full)

    def turn_over():
        @pl.when(own == 1)
        def _():
            for k in range(AROUND, sectors):
                def act(k=k):
                    aside(k).wait_recv()
                    diagonal(k).start()

                handed(k, 0, 0, act)

    def course(s):
        for j in range(states - 1):
            pass_on(s, s, [j], [j], False)
        last = functools.partial(pass_on, s, s, [states - 1], range(states - 1, sectors), True)
        mine, theirs = hosts[s], hosts[1 - s]
        done = int(mine == [0])
        for j in mine[:-1]:
            far(j, s)
        if not done:
            last()
        far(mine[-1], s)
        if done:
            last()
            pass_on(s, 1 - s, [0], [0], False)
        if s == 1:
            turn_over()
        for j in theirs[:-1]:
            def step(b, c, j=j):
                x_copy(j, b).wait_recv()
                forward(j, 1 - s, s, b)
                return c

            lax.fori_loop(0, blocks(caps[j], 1 - s), step, 0)
        j = theirs[-1]
        count = blocks(caps[j], 1 - s)

        def step(b, c):
            x_copy(j, b).wait_recv()
            forward(j, 1 - s, s, b)
            return c

        lax.fori_loop(0, count, step, 0)
        pass_on(s, 1 - s, range(done, states), range(done, sectors), True)
        for part in range(2):
            @pl.when(own == part)
            def _():
                for j in range(states):
                    arrive(j, part, s, 0)

    for s in range(2):
        pl.when(h == s)(functools.partial(course, s))

    def gather(r, c):
        total = w0[0, inv_ref[0, r]].astype(f32)
        for source in range(1, half):
            total = total + w0[source, inv_ref[source, r]].astype(f32)
        o_ref[r] = total
        return c

    lax.fori_loop(0, sectors, gather, 0)

    def received(s):
        for part in range(2):
            @pl.when(own == part)
            def _():
                for k in range(sectors):
                    handed(k, part, s, lambda k=k: hand(k, s).wait_recv())

    for s in range(2):
        pl.when(h == s)(functools.partial(received, s))

    def add(r, c):
        size = meta_ref[rights + r]
        col_ids = lax.broadcasted_iota(jnp.int32, (rows, width), 1) + h * width
        limit = jnp.where(size > me * rows, size, 0)
        o_ref[r] = jnp.where(col_ids < limit, o_ref[r] + down[meta_ref[ranks + r]].astype(f32), 0.0)
        return c

    lax.fori_loop(0, sectors, add, 0)

    def settle(s):
        for j in hosts[1 - s]:
            m_copy(j).wait_send()
        for j in hosts[s]:
            def left(b, c, j=j):
                x_copy(j, b).wait_send()
                return c

            lax.fori_loop(0, blocks(caps[j], s), left, 0)
        for j in range(states):
            for part in range(2):
                sent(j, part, s)
        for part in range(2):
            @pl.when(own == 1 - part)
            def _():
                for k in range(sectors):
                    if part == s == 0 and k >= AROUND:
                        handed(k, part, s, lambda k=k: aside(k).wait_send())
                    else:
                        handed(k, part, s, lambda k=k: hand(k, s).wait_send())
        if s == 1:
            @pl.when(own == 1)
            def _():
                for k in range(AROUND, sectors):
                    handed(k, 0, 0, lambda k=k: diagonal(k).wait_send())

    for s in range(2):
        pl.when(h == s)(functools.partial(settle, s))


def fused(at, inv, meta, whole, site):
    caps, crops = LADDER[at]
    states, span, width = site.shape
    devices, sectors = inv.shape
    rows, half = span // devices, devices // 2
    wide = max(j + 1 for j in range(states) if caps[j] > half)
    bf16 = jnp.bfloat16
    dma = pltpu.SemaphoreType.DMA
    return pl.pallas_call(
        functools.partial(kernel, caps, crops),
        out_shape=jax.ShapeDtypeStruct((sectors, rows, width), jnp.float32),
        in_specs=[pl.BlockSpec(memory_space=pltpu.SMEM)] * 2 + [pl.BlockSpec(memory_space=pltpu.VMEM)] * 2,
        out_specs=pl.BlockSpec(memory_space=pltpu.VMEM),
        scratch_shapes=[
            pltpu.VMEM((wide, span, width), bf16),
            pltpu.VMEM((states, span, width), bf16),
            pltpu.VMEM((span, width), bf16),
            pltpu.VMEM((wide, width, width), bf16),
            pltpu.VMEM((states, span, width), bf16),
            pltpu.VMEM((half, states + 1, rows, width), bf16),
            pltpu.VMEM((half, states + 1, rows, width), bf16),
            pltpu.VMEM((sectors, rows, width), bf16),
            pltpu.VMEM((sectors, rows, width), bf16),
            pltpu.VMEM((sectors - AROUND, rows, width), bf16),
            dma((wide,)), dma((wide,)), dma((wide, half)), dma((wide, half)),
            dma((states, devices)), dma((2, half, states)),
            dma((sectors,)), dma((sectors,)),
            dma((sectors - AROUND,)), dma((sectors - AROUND,)), dma((sectors - AROUND,)),
        ],
        compiler_params=pltpu.CompilerParams(
            collective_id=1 + at, has_side_effects=True, vmem_limit_bytes=50 * 2**20),
        cost_estimate=pl.CostEstimate(
            flops=4 * states * span * span * width, bytes_accessed=16 * 2**20, transcendentals=0),
    )(inv, meta, whole, site)


def body(groups, devices, left_env, site_tensor, left_sizes, right_sizes, targets):
    states = site_tensor.shape[1]
    sectors = right_sizes.shape[0]
    others = groups * devices
    i32 = jnp.int32
    dma = pltpu.SemaphoreType.DMA
    smem = pl.BlockSpec(memory_space=pltpu.SMEM)
    vmem = pl.BlockSpec(memory_space=pltpu.VMEM)
    inv, meta, pick, whole, masked = pl.pallas_call(
        agree,
        out_shape=[
            jax.ShapeDtypeStruct((devices, sectors), i32),
            jax.ShapeDtypeStruct((2 * states + 1 + 3 * sectors,), i32),
            jax.ShapeDtypeStruct((1,), i32),
            jax.ShapeDtypeStruct((site_tensor.shape[2],) * 2, jnp.bfloat16),
            jax.ShapeDtypeStruct(site_tensor.shape[1:], jnp.bfloat16),
        ],
        in_specs=[smem] * 3 + [pl.BlockSpec(memory_space=pltpu.HBM)] * 2,
        out_specs=[smem] * 3 + [vmem] * 2,
        scratch_shapes=[
            pltpu.VMEM((8, 128), i32), pltpu.VMEM((others, 8, 128), i32), pltpu.SMEM((others, 8, 128), i32),
            pltpu.VMEM(site_tensor.shape[1:], jnp.bfloat16),
            dma((others,)), dma((others,)), dma, dma, dma, dma, dma,
        ],
        compiler_params=pltpu.CompilerParams(collective_id=0, has_side_effects=True, vmem_limit_bytes=54 * 2**20),
    )(targets, left_sizes, right_sizes, left_env[0], site_tensor[0])
    branches = [functools.partial(fused, at) for at in range(len(LADDER))]
    return lax.switch(pick[0], branches, inv, meta, whole, masked)


def solution(mesh):
    in_specs = (
        P(("groups", "charge"), "split", None),
        P(("groups", "charge"), None, None, "split"),
        P(("groups", "charge")),
        P("groups"),
        P(("groups", "charge"), None),
    )
    out_specs = P("groups", "charge", "split")
    if mesh.shape["split"] == 2 and mesh.shape["charge"] == 8:
        inner = functools.partial(body, mesh.shape["groups"], mesh.shape["charge"])
    else:
        inner = gathered_body
    return jax.shard_map(inner, mesh=mesh, in_specs=in_specs, out_specs=out_specs, check_vma=False)
```

```python
import functools

import jax
import jax.numpy as jnp
from jax import lax
from jax.experimental import pallas as pl
from jax.experimental.pallas import tpu as pltpu
from jax.sharding import PartitionSpec as P

MESH = pl.DeviceIdType.MESH
HOST = (1, 0, 0, 0)
AROUND = 5
LADDER = (
    ((8, 8, 5, 4), (8, 8, 5, 5, 4, 3, 3, 3)),
    ((8, 8, 6, 4), (8, 8, 6, 6, 5, 3, 3, 3)),
    ((8, 8, 6, 5), (8, 8, 6, 6, 6, 4, 4, 4)),
    ((8, 8, 8, 8), (8, 8, 8, 8, 8, 8, 8, 8)),
)


def gathered_body(left_env, site_tensor, left_sizes, right_sizes, targets):
    states = site_tensor.shape[1]
    span = site_tensor.shape[2]
    width = site_tensor.shape[3]
    sectors = right_sizes.shape[0]
    column_base = lax.axis_index("split") * width
    row_ids = lax.broadcasted_iota(jnp.int32, (1, span, 1), 1)
    column_ids = lax.broadcasted_iota(jnp.int32, (1, 1, width), 2) + column_base
    slot_ids = lax.broadcasted_iota(jnp.int32, (states, sectors), 1)
    route = targets[0][:, None] == slot_ids
    live_cols = jnp.sum(jnp.where(route, right_sizes[None, :], 0), axis=1)
    keep = (row_ids < left_sizes[0]) & (column_ids < live_cols[:, None, None])
    masked = jnp.where(keep, site_tensor[0], jnp.zeros((), jnp.bfloat16))[None]
    product = jnp.einsum(
        "ik,skj->sij",
        lax.all_gather(left_env, "split", axis=1, tiled=True)[0],
        masked[0],
        preferred_element_type=jnp.float32,
    ).astype(jnp.bfloat16)
    terms = jnp.einsum(
        "ski,skj->sij",
        lax.all_gather(masked, "split", axis=3, tiled=True)[0],
        product,
        preferred_element_type=jnp.float32,
    ).astype(jnp.bfloat16)
    placed = jnp.einsum(
        "st,sij->tij", route.astype(jnp.bfloat16), terms, preferred_element_type=jnp.float32
    ).astype(jnp.bfloat16)
    return lax.psum_scatter(placed, "charge", scatter_dimension=1, tiled=True).astype(jnp.float32)


def agree(targets_ref, left_ref, right_ref, l_ref, m_ref, inv_ref, meta_ref, pick_ref, lf, ms,
          info, got, seen, site, send, recv, sem, lsend, lrecv, lown, mown):
    g = lax.axis_index("groups")
    me = lax.axis_index("charge")
    h = lax.axis_index("split")
    devices, sectors = inv_ref.shape[0], right_ref.shape[0]
    others = got.shape[0]
    states = targets_ref.shape[1]
    mine = g * devices + me
    rights = 2 * states + 1
    orders = rights + sectors
    ranks = orders + sectors

    barrier = pltpu.get_barrier_semaphore()

    def place(i):
        n = lax.rem(mine + i, others)
        return {"groups": n // devices, "charge": lax.rem(n, devices)}

    def greet(i, c):
        pl.semaphore_signal(barrier, inc=1, device_id=place(i), device_id_type=MESH)
        return c

    lax.fori_loop(1, others, greet, 0)
    pl.semaphore_signal(barrier, inc=1, device_id={"split": 1 - h}, device_id_type=MESH)

    span, width = ms.shape[1], ms.shape[2]
    half_rows = pl.ds(pl.multiple_of(h * width, width), width)
    m_own = pltpu.make_async_copy(m_ref, site, mown)
    m_own.start()
    l_own = pltpu.make_async_copy(l_ref, lf.at[half_rows], lown)
    l_own.start()
    every = [right_ref[r] for r in range(sectors)]
    place_of = []
    for r in range(sectors):
        ahead = jnp.int32(0)
        for k in range(sectors):
            if k != r:
                first = every[k] >= every[r] if k < r else every[k] > every[r]
                ahead = ahead + jnp.where(first, 1, 0)
        place_of.append(ahead)
        meta_ref[rights + r] = every[r]
        meta_ref[ranks + r] = ahead
    ordered = []
    for k in range(sectors):
        which, much = jnp.int32(0), jnp.int32(0)
        for r in range(sectors):
            which = jnp.where(place_of[r] == k, r, which)
            much = jnp.where(place_of[r] == k, every[r], much)
        meta_ref[orders + k] = which
        ordered.append(much)
    to = [targets_ref[0, j] for j in range(states)]
    size = [right_ref[t] for t in to]
    grade = [meta_ref[ranks + t] for t in to]
    rank = []
    for j in range(states):
        ahead = jnp.int32(0)
        for k in range(states):
            if k != j:
                ahead = ahead + jnp.where(grade[k] < grade[j], 1, 0)
        rank.append(ahead)
    lane = lax.broadcasted_iota(jnp.int32, info.shape, 1)
    packed = jnp.zeros(info.shape, jnp.int32)
    for slot in range(states):
        state, live, target = jnp.int32(0), jnp.int32(0), jnp.int32(0)
        for j in range(states):
            here = rank[j] == slot
            state = jnp.where(here, j, state)
            live = jnp.where(here, size[j], live)
            target = jnp.where(here, to[j], target)
        meta_ref[slot] = state
        meta_ref[states + slot] = live
        packed = jnp.where(lane == slot, target, packed)
        packed = jnp.where(lane == states + slot, live, packed)
    for k in range(sectors):
        packed = jnp.where(lane == 2 * states + k, ordered[k], packed)
    meta_ref[2 * states] = left_ref[0]
    info[...] = packed
    got[mine] = packed
    pl.semaphore_wait(barrier, others)
    l_copy = pltpu.make_async_remote_copy(
        src_ref=l_ref, dst_ref=lf.at[half_rows], send_sem=lsend, recv_sem=lrecv,
        device_id={"split": 1 - h}, device_id_type=MESH)
    l_copy.start()

    def copy(i):
        return pltpu.make_async_remote_copy(
            src_ref=info, dst_ref=got.at[mine], send_sem=send.at[i], recv_sem=recv.at[mine],
            device_id=place(i), device_id_type=MESH)

    def start(i, c):
        copy(i).start()
        return c

    def finish(i, c):
        n = lax.rem(mine + i, others)
        copy(i).wait_send()
        pltpu.make_async_remote_copy(
            src_ref=info, dst_ref=got.at[n], send_sem=send.at[i], recv_sem=recv.at[n],
            device_id=place(i), device_id_type=MESH).wait_recv()
        return c

    lax.fori_loop(1, others, start, 0)
    m_own.wait()

    def mask(j, c):
        state, live, deep = meta_ref[j], meta_ref[states + j], meta_ref[2 * states]

        def tile(i, c):
            part = pl.ds(pl.multiple_of(i * 128, 128), 128)
            row_ids = lax.broadcasted_iota(jnp.int32, (128, width), 0) + i * 128
            col_ids = lax.broadcasted_iota(jnp.int32, (128, width), 1) + h * width
            keep = (row_ids < deep) & (col_ids < live)
            ms[j, part] = jnp.where(keep, site[state, part].astype(jnp.float32), 0.0).astype(jnp.bfloat16)
            return c

        return lax.fori_loop(0, span // 128, tile, c)

    lax.fori_loop(0, states, mask, 0)
    lax.fori_loop(1, others, finish, 0)
    local = pltpu.make_async_copy(got, seen, sem)
    local.start()
    local.wait()

    half = devices // 2
    rows = span // devices
    side, seat = lax.div(me, half), lax.rem(me, half)
    for kind in range(2):
        block = (side if kind == 0 else 1 - side) * half + seat
        wants = [every[r] > jnp.maximum(block * rows, h * width) for r in range(sectors)]

        def route(s, c):
            reached = [seen[mine - seat + s, 0, j] for j in range(states)]
            for r in range(sectors):
                slot = jnp.int32(states)
                for j in range(states):
                    slot = jnp.where(reached[j] == r, j, slot)
                inv_ref[kind * half + s, r] = jnp.where(wants[r], slot, states)
            return c

        lax.fori_loop(0, half, route, 0)

    def widest(n, most):
        return tuple(jnp.maximum(m, seen[n, 0, states + j]) for j, m in enumerate(most))

    most = lax.fori_loop(0, others, widest, (jnp.int32(0),) * (states + sectors))
    pick = jnp.int32(len(LADDER) - 1)
    for at in range(len(LADDER) - 2, -1, -1):
        caps = LADDER[at][0] + LADDER[at][1]
        fits = most[0] <= caps[0] * rows
        for j in range(1, states + sectors):
            fits = fits & (most[j] <= caps[j] * rows)
        pick = jnp.where(fits, at, pick)
    pick_ref[0] = pick
    l_own.wait()
    l_copy.wait()


def kernel(caps, crops, inv_ref, meta_ref, lf, ms, o_ref, mr, pb, px, xb, tb, w0, w1, up, down, via,
           msend, mrecv, xsend, xrecv, zsend, zrecv, usend, drecv, vsend, vrecv, fsend):
    me = lax.axis_index("charge")
    h = lax.axis_index("split")
    states, span, width = ms.shape
    sectors, rows = o_ref.shape[0], o_ref.shape[1]
    devices = span // rows
    half = devices // 2
    empty = states
    f32, bf16 = jnp.float32, jnp.bfloat16
    own, seat = lax.div(me, half), lax.rem(me, half)
    partner = {"charge": lax.rem(me + half, devices)}
    wide = [j for j in range(states) if caps[j] > half]
    rights, orders, ranks = 2 * states + 1, 2 * states + 1 + sectors, 2 * states + 1 + 2 * sectors

    def blocks(cap, side):
        return min(cap, half) if side == 0 else max(cap - half, 0)

    def live(cap, side):
        return blocks(cap, side) * rows

    barrier = pltpu.get_barrier_semaphore()
    pl.semaphore_signal(barrier, inc=1, device_id={"split": 1 - h}, device_id_type=MESH)
    pl.semaphore_signal(barrier, inc=1, device_id=partner, device_id_type=MESH)
    across = {"charge": lax.rem(me + half, devices), "split": 1 - h}
    pl.semaphore_signal(barrier, inc=1, device_id=across, device_id_type=MESH)
    for i in range(1, half):
        pl.semaphore_signal(
            barrier, inc=1, device_id={"charge": own * half + lax.rem(seat + i, half)}, device_id_type=MESH)
    pl.semaphore_wait(barrier, half + 2)

    def m_copy(j):
        columns = pl.ds(0, live(caps[j], 1 - HOST[j]))
        return pltpu.make_async_remote_copy(
            src_ref=ms.at[j, :, columns], dst_ref=mr.at[j, :, columns], send_sem=msend.at[j],
            recv_sem=mrecv.at[j], device_id={"split": 1 - h}, device_id_type=MESH)

    def x_copy(j, b):
        s = HOST[j]
        columns = pl.ds(0, live(caps[j], 1 - s))
        here, there = (pl.ds(pl.multiple_of((n + b) * rows, rows), rows) for n in (0, s * half))
        return pltpu.make_async_remote_copy(
            src_ref=xb.at[j, here, columns], dst_ref=tb.at[j, there, columns],
            send_sem=xsend.at[j, b], recv_sem=xrecv.at[j, b], device_id={"split": 1 - h}, device_id_type=MESH)

    def chunk(j, part, side, to, source, kind):
        w = (w0, w1)[kind]
        columns = pl.ds(0, live(caps[j], side))
        from_rows = pl.ds(pl.multiple_of((part * half + to) * rows, rows), rows)
        return pltpu.make_async_remote_copy(
            src_ref=tb.at[j, from_rows, columns], dst_ref=w.at[source, j, :, columns],
            send_sem=zsend.at[j, part * half + to], recv_sem=zrecv.at[kind, source, j],
            device_id={"charge": own * half + to}, device_id_type=MESH)

    def forward(j, part, side, to):
        columns = live(caps[j], side)
        for kind in range(2):
            w = (w0, w1)[kind]

            @pl.when((own == part ^ kind) & (to != seat))
            def _():
                chunk(j, part, side, to, seat, kind).start()

            @pl.when((own == part ^ kind) & (to == seat))
            def _():
                def move(i, c):
                    here = pl.ds(pl.multiple_of((part * half + to) * rows + i * 32, 32), 32)
                    w[seat, j, pl.ds(pl.multiple_of(i * 32, 32), 32), 0:columns] = tb[j, here, 0:columns]
                    return c

                lax.fori_loop(0, rows // 32, move, 0)

    def scatter(j, part, side):
        count = blocks(caps[j], part)

        def one(i, c):
            forward(j, part, side, lax.rem(seat + 1 + i, count))
            return c

        lax.fori_loop(0, count, one, 0)

    def arrive(j, part, side, kind):
        if live(caps[j], side) == 0 or blocks(caps[j], part) == 0:
            return

        @pl.when(seat < blocks(caps[j], part))
        def _():
            def one(i, c):
                chunk(j, part, side, seat, lax.rem(seat + i, half), kind).wait_recv()
                return c

            lax.fori_loop(1, half, one, 0)

    def sent(j, part, side):
        count = blocks(caps[j], part)
        if live(caps[j], side) == 0 or count == 0:
            return

        def one(to, c):
            pl.when(to != seat)(lambda: chunk(j, part, side, to, seat, 0).wait_send())
            return c

        lax.fori_loop(0, count, one, 0)

    def hand(k, side):
        columns = pl.ds(0, live(crops[k], side))
        return pltpu.make_async_remote_copy(
            src_ref=up.at[k, :, columns], dst_ref=down.at[k, :, columns], send_sem=usend.at[k],
            recv_sem=drecv.at[k], device_id=partner, device_id_type=MESH)

    def aside(k):
        columns = pl.ds(0, live(crops[k], 0))
        return pltpu.make_async_remote_copy(
            src_ref=up.at[k, :, columns], dst_ref=via.at[k - AROUND, :, columns], send_sem=vsend.at[k - AROUND],
            recv_sem=vrecv.at[k - AROUND], device_id={"split": 1 - h}, device_id_type=MESH)

    def diagonal(k):
        columns = pl.ds(0, live(crops[k], 0))
        return pltpu.make_async_remote_copy(
            src_ref=via.at[k - AROUND, :, columns], dst_ref=down.at[k, :, columns], send_sem=fsend.at[k - AROUND],
            recv_sem=drecv.at[k], device_id=across, device_id_type=MESH)

    def handed(k, part, side, act):
        if live(crops[k], side) and blocks(crops[k], part):
            pl.when(seat < blocks(crops[k], part))(act)

    def relay(k, part, side, full):
        def act():
            columns = live(crops[k], side)
            r = meta_ref[orders + k]
            slots = [inv_ref[half + source, r] for source in range(half)]

            def tile(i, c):
                at = pl.ds(pl.multiple_of(i * 32, 32), 32)
                total = jnp.zeros((32, columns), f32)
                for source in range(half):
                    if full:
                        total = total + w1[source, slots[source], at, 0:columns].astype(f32)
                    else:
                        for j in range(k + 1):
                            one = w1[source, j, at, 0:columns].astype(f32)
                            total = total + jnp.where(slots[source] == j, one, 0.0)
                up[k, at, 0:columns] = total.astype(bf16)
                return c

            lax.fori_loop(0, rows // 32, tile, 0)
            (aside(k) if part == side == 0 and k >= AROUND else hand(k, side)).start()

        handed(k, part, side, act)

    def product(j):
        def tile(i, c):
            part = pl.ds(pl.multiple_of(i * 256, 256), 256)
            pb[j, part] = jnp.dot(lf[part], ms[j], preferred_element_type=f32).astype(bf16)
            return c

        lax.fori_loop(0, span // 256, tile, 0)

    def flipped(columns, right):
        return lax.dot_general(columns, right, (((0,), (0,)), ((), ())), preferred_element_type=f32).astype(bf16)

    def near(j):
        product(j)

        def tile(i, c):
            part = pl.ds(pl.multiple_of(h * width + i * 256, 256), 256)
            tb[j, part] = flipped(ms[j, :, pl.ds(pl.multiple_of(i * 256, 256), 256)], pb[j])
            return c

        lax.fori_loop(0, width // 256, tile, 0)
        for side in range(2):
            if live(caps[j], side):
                pl.when(h == side)(functools.partial(scatter, j, side, side))

    def turned(i, s, count):
        return count - 1 - i if s else i

    def far(j, s):
        o = 1 - s
        columns = live(caps[j], o)
        m_copy(j).wait_recv()

        def tile(i, c):
            part = pl.ds(pl.multiple_of(i * 256, 256), 256)
            px[part, 0:columns] = jnp.dot(lf[part], mr[j, :, 0:columns], preferred_element_type=f32).astype(bf16)
            return c

        lax.fori_loop(0, span // 256, tile, 0)

        def back(i, c):
            i = turned(i, s, blocks(caps[j], s))
            part = pl.ds(pl.multiple_of(i * rows, rows), rows)
            xb[j, part, 0:columns] = flipped(ms[j, :, part], px[:, 0:columns])
            x_copy(j, i).start()
            return c

        lax.fori_loop(0, blocks(caps[j], s), back, 0)

        def there(i, c):
            part = pl.ds(pl.multiple_of(o * width + i * rows, rows), rows)
            tb[j, part] = flipped(mr[j, :, pl.ds(pl.multiple_of(i * rows, rows), rows)], pb[j])
            return c

        lax.fori_loop(0, blocks(caps[j], o), there, 0)
        scatter(j, o, s)

    hosts = [[j for j in reversed(wide) if HOST[j] == s] for s in range(2)]
    for s in range(2):
        @pl.when(h == s)
        def _():
            for j in hosts[1 - s]:
                m_copy(j).start()
    for j in range(states):
        if j in wide:
            near(j)
        else:
            pl.when(h == 0)(functools.partial(near, j))
    w0[:, empty] = jnp.zeros((half, rows, width), bf16)
    w1[:, empty] = jnp.zeros((half, rows, width), bf16)

    def pass_on(s, part, slots, some, full):
        @pl.when(own == 1 - part)
        def _():
            for j in slots:
                arrive(j, part, s, 1)
            for k in some:
                relay(k, part, s, full)

    def turn_over():
        @pl.when(own == 1)
        def _():
            for k in range(AROUND, sectors):
                def act(k=k):
                    aside(k).wait_recv()
                    diagonal(k).start()

                handed(k, 0, 0, act)

    def course(s):
        for j in range(states - 1):
            pass_on(s, s, [j], [j], False)
        last = functools.partial(pass_on, s, s, [states - 1], range(states - 1, sectors), True)
        mine, theirs = hosts[s], hosts[1 - s]
        done = int(mine == [0])
        for j in mine[:-1]:
            far(j, s)
        if not done:
            last()
        far(mine[-1], s)
        if done:
            last()
            pass_on(s, 1 - s, [0], [0], False)
        if s == 1:
            turn_over()
        for j in theirs[:-1]:
            def step(b, c, j=j):
                x_copy(j, b).wait_recv()
                forward(j, 1 - s, s, b)
                return c

            lax.fori_loop(0, blocks(caps[j], 1 - s), step, 0)
        j = theirs[-1]
        count = blocks(caps[j], 1 - s)

        def step(b, c):
            b = turned(b, 1 - s, count)
            x_copy(j, b).wait_recv()
            forward(j, 1 - s, s, b)
            return c

        lax.fori_loop(0, count, step, 0)
        pass_on(s, 1 - s, range(done, states), range(done, sectors), True)
        for part in range(2):
            @pl.when(own == part)
            def _():
                for j in range(states):
                    arrive(j, part, s, 0)

    for s in range(2):
        pl.when(h == s)(functools.partial(course, s))

    def gather(r, c):
        total = w0[0, inv_ref[0, r]].astype(f32)
        for source in range(1, half):
            total = total + w0[source, inv_ref[source, r]].astype(f32)
        o_ref[r] = total
        return c

    lax.fori_loop(0, sectors, gather, 0)

    def received(s):
        for part in range(2):
            @pl.when(own == part)
            def _():
                for k in range(sectors):
                    handed(k, part, s, lambda k=k: hand(k, s).wait_recv())

    for s in range(2):
        pl.when(h == s)(functools.partial(received, s))

    def add(r, c):
        size = meta_ref[rights + r]
        col_ids = lax.broadcasted_iota(jnp.int32, (rows, width), 1) + h * width
        limit = jnp.where(size > me * rows, size, 0)
        o_ref[r] = jnp.where(col_ids < limit, o_ref[r] + down[meta_ref[ranks + r]].astype(f32), 0.0)
        return c

    lax.fori_loop(0, sectors, add, 0)

    def settle(s):
        for j in hosts[1 - s]:
            m_copy(j).wait_send()
        for j in hosts[s]:
            def left(b, c, j=j):
                x_copy(j, b).wait_send()
                return c

            lax.fori_loop(0, blocks(caps[j], s), left, 0)
        for j in range(states):
            for part in range(2):
                sent(j, part, s)
        for part in range(2):
            @pl.when(own == 1 - part)
            def _():
                for k in range(sectors):
                    if part == s == 0 and k >= AROUND:
                        handed(k, part, s, lambda k=k: aside(k).wait_send())
                    else:
                        handed(k, part, s, lambda k=k: hand(k, s).wait_send())
        if s == 1:
            @pl.when(own == 1)
            def _():
                for k in range(AROUND, sectors):
                    handed(k, 0, 0, lambda k=k: diagonal(k).wait_send())

    for s in range(2):
        pl.when(h == s)(functools.partial(settle, s))


def fused(at, inv, meta, whole, site):
    caps, crops = LADDER[at]
    states, span, width = site.shape
    devices, sectors = inv.shape
    rows, half = span // devices, devices // 2
    wide = max(j + 1 for j in range(states) if caps[j] > half)
    bf16 = jnp.bfloat16
    dma = pltpu.SemaphoreType.DMA
    return pl.pallas_call(
        functools.partial(kernel, caps, crops),
        out_shape=jax.ShapeDtypeStruct((sectors, rows, width), jnp.float32),
        in_specs=[pl.BlockSpec(memory_space=pltpu.SMEM)] * 2 + [pl.BlockSpec(memory_space=pltpu.VMEM)] * 2,
        out_specs=pl.BlockSpec(memory_space=pltpu.VMEM),
        scratch_shapes=[
            pltpu.VMEM((wide, span, width), bf16),
            pltpu.VMEM((states, span, width), bf16),
            pltpu.VMEM((span, width), bf16),
            pltpu.VMEM((wide, width, width), bf16),
            pltpu.VMEM((states, span, width), bf16),
            pltpu.VMEM((half, states + 1, rows, width), bf16),
            pltpu.VMEM((half, states + 1, rows, width), bf16),
            pltpu.VMEM((sectors, rows, width), bf16),
            pltpu.VMEM((sectors, rows, width), bf16),
            pltpu.VMEM((sectors - AROUND, rows, width), bf16),
            dma((wide,)), dma((wide,)), dma((wide, half)), dma((wide, half)),
            dma((states, devices)), dma((2, half, states)),
            dma((sectors,)), dma((sectors,)),
            dma((sectors - AROUND,)), dma((sectors - AROUND,)), dma((sectors - AROUND,)),
        ],
        compiler_params=pltpu.CompilerParams(
            collective_id=1 + at, has_side_effects=True, vmem_limit_bytes=50 * 2**20),
        cost_estimate=pl.CostEstimate(
            flops=4 * states * span * span * width, bytes_accessed=16 * 2**20, transcendentals=0),
    )(inv, meta, whole, site)


def body(groups, devices, left_env, site_tensor, left_sizes, right_sizes, targets):
    states = site_tensor.shape[1]
    sectors = right_sizes.shape[0]
    others = groups * devices
    i32 = jnp.int32
    dma = pltpu.SemaphoreType.DMA
    smem = pl.BlockSpec(memory_space=pltpu.SMEM)
    vmem = pl.BlockSpec(memory_space=pltpu.VMEM)
    inv, meta, pick, whole, masked = pl.pallas_call(
        agree,
        out_shape=[
            jax.ShapeDtypeStruct((devices, sectors), i32),
            jax.ShapeDtypeStruct((2 * states + 1 + 3 * sectors,), i32),
            jax.ShapeDtypeStruct((1,), i32),
            jax.ShapeDtypeStruct((site_tensor.shape[2],) * 2, jnp.bfloat16),
            jax.ShapeDtypeStruct(site_tensor.shape[1:], jnp.bfloat16),
        ],
        in_specs=[smem] * 3 + [pl.BlockSpec(memory_space=pltpu.HBM)] * 2,
        out_specs=[smem] * 3 + [vmem] * 2,
        scratch_shapes=[
            pltpu.VMEM((8, 128), i32), pltpu.VMEM((others, 8, 128), i32), pltpu.SMEM((others, 8, 128), i32),
            pltpu.VMEM(site_tensor.shape[1:], jnp.bfloat16),
            dma((others,)), dma((others,)), dma, dma, dma, dma, dma,
        ],
        compiler_params=pltpu.CompilerParams(collective_id=0, has_side_effects=True, vmem_limit_bytes=54 * 2**20),
    )(targets, left_sizes, right_sizes, left_env[0], site_tensor[0])
    branches = [functools.partial(fused, at) for at in range(len(LADDER))]
    return lax.switch(pick[0], branches, inv, meta, whole, masked)


def solution(mesh):
    in_specs = (
        P(("groups", "charge"), "split", None),
        P(("groups", "charge"), None, None, "split"),
        P(("groups", "charge")),
        P("groups"),
        P(("groups", "charge"), None),
    )
    out_specs = P("groups", "charge", "split")
    if mesh.shape["split"] == 2 and mesh.shape["charge"] == 8:
        inner = functools.partial(body, mesh.shape["groups"], mesh.shape["charge"])
    else:
        inner = gathered_body
    return jax.shard_map(inner, mesh=mesh, in_specs=in_specs, out_specs=out_specs, check_vma=False)
```

```python
import functools

import jax
import jax.numpy as jnp
from jax import lax
from jax.experimental import pallas as pl
from jax.experimental.pallas import tpu as pltpu
from jax.sharding import PartitionSpec as P

MESH = pl.DeviceIdType.MESH
HOST = (1, 0, 0, 0)
AROUND = 5
LADDER = (
    ((8, 8, 5, 4), (8, 8, 5, 5, 4, 3, 3, 2)),
    ((8, 8, 5, 4), (8, 8, 6, 5, 4, 3, 3, 3)),
    ((8, 8, 6, 4), (8, 8, 6, 5, 4, 3, 3, 2)),
    ((8, 8, 6, 4), (8, 8, 6, 6, 5, 3, 3, 3)),
    ((8, 8, 6, 5), (8, 8, 6, 6, 5, 3, 3, 3)),
    ((8, 8, 8, 8), (8, 8, 8, 8, 8, 8, 8, 8)),
)


def gathered_body(left_env, site_tensor, left_sizes, right_sizes, targets):
    states = site_tensor.shape[1]
    span = site_tensor.shape[2]
    width = site_tensor.shape[3]
    sectors = right_sizes.shape[0]
    column_base = lax.axis_index("split") * width
    row_ids = lax.broadcasted_iota(jnp.int32, (1, span, 1), 1)
    column_ids = lax.broadcasted_iota(jnp.int32, (1, 1, width), 2) + column_base
    slot_ids = lax.broadcasted_iota(jnp.int32, (states, sectors), 1)
    route = targets[0][:, None] == slot_ids
    live_cols = jnp.sum(jnp.where(route, right_sizes[None, :], 0), axis=1)
    keep = (row_ids < left_sizes[0]) & (column_ids < live_cols[:, None, None])
    masked = jnp.where(keep, site_tensor[0], jnp.zeros((), jnp.bfloat16))[None]
    product = jnp.einsum(
        "ik,skj->sij",
        lax.all_gather(left_env, "split", axis=1, tiled=True)[0],
        masked[0],
        preferred_element_type=jnp.float32,
    ).astype(jnp.bfloat16)
    terms = jnp.einsum(
        "ski,skj->sij",
        lax.all_gather(masked, "split", axis=3, tiled=True)[0],
        product,
        preferred_element_type=jnp.float32,
    ).astype(jnp.bfloat16)
    placed = jnp.einsum(
        "st,sij->tij", route.astype(jnp.bfloat16), terms, preferred_element_type=jnp.float32
    ).astype(jnp.bfloat16)
    return lax.psum_scatter(placed, "charge", scatter_dimension=1, tiled=True).astype(jnp.float32)


def agree(targets_ref, left_ref, right_ref, l_ref, m_ref, inv_ref, meta_ref, pick_ref, lf, ms,
          info, got, seen, site, send, recv, sem, lsend, lrecv, lown, mown):
    g = lax.axis_index("groups")
    me = lax.axis_index("charge")
    h = lax.axis_index("split")
    devices, sectors = inv_ref.shape[0], right_ref.shape[0]
    others = got.shape[0]
    states = targets_ref.shape[1]
    mine = g * devices + me
    rights = 2 * states + 1
    orders = rights + sectors
    ranks = orders + sectors

    barrier = pltpu.get_barrier_semaphore()

    def place(i):
        n = lax.rem(mine + i, others)
        return {"groups": n // devices, "charge": lax.rem(n, devices)}

    def greet(i, c):
        pl.semaphore_signal(barrier, inc=1, device_id=place(i), device_id_type=MESH)
        return c

    lax.fori_loop(1, others, greet, 0)
    pl.semaphore_signal(barrier, inc=1, device_id={"split": 1 - h}, device_id_type=MESH)

    span, width = ms.shape[1], ms.shape[2]
    half_rows = pl.ds(pl.multiple_of(h * width, width), width)
    m_own = pltpu.make_async_copy(m_ref, site, mown)
    m_own.start()
    l_own = pltpu.make_async_copy(l_ref, lf.at[half_rows], lown)
    l_own.start()
    every = [right_ref[r] for r in range(sectors)]
    place_of = []
    for r in range(sectors):
        ahead = jnp.int32(0)
        for k in range(sectors):
            if k != r:
                first = every[k] >= every[r] if k < r else every[k] > every[r]
                ahead = ahead + jnp.where(first, 1, 0)
        place_of.append(ahead)
        meta_ref[rights + r] = every[r]
        meta_ref[ranks + r] = ahead
    ordered = []
    for k in range(sectors):
        which, much = jnp.int32(0), jnp.int32(0)
        for r in range(sectors):
            which = jnp.where(place_of[r] == k, r, which)
            much = jnp.where(place_of[r] == k, every[r], much)
        meta_ref[orders + k] = which
        ordered.append(much)
    to = [targets_ref[0, j] for j in range(states)]
    size = [right_ref[t] for t in to]
    grade = [meta_ref[ranks + t] for t in to]
    rank = []
    for j in range(states):
        ahead = jnp.int32(0)
        for k in range(states):
            if k != j:
                ahead = ahead + jnp.where(grade[k] < grade[j], 1, 0)
        rank.append(ahead)
    lane = lax.broadcasted_iota(jnp.int32, info.shape, 1)
    packed = jnp.zeros(info.shape, jnp.int32)
    for slot in range(states):
        state, live, target = jnp.int32(0), jnp.int32(0), jnp.int32(0)
        for j in range(states):
            here = rank[j] == slot
            state = jnp.where(here, j, state)
            live = jnp.where(here, size[j], live)
            target = jnp.where(here, to[j], target)
        meta_ref[slot] = state
        meta_ref[states + slot] = live
        packed = jnp.where(lane == slot, target, packed)
        packed = jnp.where(lane == states + slot, live, packed)
    for k in range(sectors):
        packed = jnp.where(lane == 2 * states + k, ordered[k], packed)
    meta_ref[2 * states] = left_ref[0]
    info[...] = packed
    got[mine] = packed
    pl.semaphore_wait(barrier, others)
    l_copy = pltpu.make_async_remote_copy(
        src_ref=l_ref, dst_ref=lf.at[half_rows], send_sem=lsend, recv_sem=lrecv,
        device_id={"split": 1 - h}, device_id_type=MESH)
    l_copy.start()

    def copy(i):
        return pltpu.make_async_remote_copy(
            src_ref=info, dst_ref=got.at[mine], send_sem=send.at[i], recv_sem=recv.at[mine],
            device_id=place(i), device_id_type=MESH)

    def start(i, c):
        copy(i).start()
        return c

    def finish(i, c):
        n = lax.rem(mine + i, others)
        copy(i).wait_send()
        pltpu.make_async_remote_copy(
            src_ref=info, dst_ref=got.at[n], send_sem=send.at[i], recv_sem=recv.at[n],
            device_id=place(i), device_id_type=MESH).wait_recv()
        return c

    lax.fori_loop(1, others, start, 0)
    m_own.wait()

    def mask(j, c):
        state, live, deep = meta_ref[j], meta_ref[states + j], meta_ref[2 * states]

        def tile(i, c):
            part = pl.ds(pl.multiple_of(i * 128, 128), 128)
            row_ids = lax.broadcasted_iota(jnp.int32, (128, width), 0) + i * 128
            col_ids = lax.broadcasted_iota(jnp.int32, (128, width), 1) + h * width
            keep = (row_ids < deep) & (col_ids < live)
            ms[j, part] = jnp.where(keep, site[state, part].astype(jnp.float32), 0.0).astype(jnp.bfloat16)
            return c

        return lax.fori_loop(0, span // 128, tile, c)

    lax.fori_loop(0, states, mask, 0)
    lax.fori_loop(1, others, finish, 0)
    local = pltpu.make_async_copy(got, seen, sem)
    local.start()
    local.wait()

    half = devices // 2
    rows = span // devices
    side, seat = lax.div(me, half), lax.rem(me, half)
    for kind in range(2):
        block = (side if kind == 0 else 1 - side) * half + seat
        wants = [every[r] > jnp.maximum(block * rows, h * width) for r in range(sectors)]

        def route(s, c):
            reached = [seen[mine - seat + s, 0, j] for j in range(states)]
            for r in range(sectors):
                slot = jnp.int32(states)
                for j in range(states):
                    slot = jnp.where(reached[j] == r, j, slot)
                inv_ref[kind * half + s, r] = jnp.where(wants[r], slot, states)
            return c

        lax.fori_loop(0, half, route, 0)

    def widest(n, most):
        return tuple(jnp.maximum(m, seen[n, 0, states + j]) for j, m in enumerate(most))

    most = lax.fori_loop(0, others, widest, (jnp.int32(0),) * (states + sectors))
    pick = jnp.int32(len(LADDER) - 1)
    for at in range(len(LADDER) - 2, -1, -1):
        caps = LADDER[at][0] + LADDER[at][1]
        fits = most[0] <= caps[0] * rows
        for j in range(1, states + sectors):
            fits = fits & (most[j] <= caps[j] * rows)
        pick = jnp.where(fits, at, pick)
    pick_ref[0] = pick
    l_own.wait()
    l_copy.wait()


def kernel(caps, crops, inv_ref, meta_ref, lf, ms, o_ref, mr, pb, px, xb, tb, w0, w1, up, down, via,
           msend, mrecv, xsend, xrecv, zsend, zrecv, usend, drecv, vsend, vrecv, fsend):
    me = lax.axis_index("charge")
    h = lax.axis_index("split")
    states, span, width = ms.shape
    sectors, rows = o_ref.shape[0], o_ref.shape[1]
    devices = span // rows
    half = devices // 2
    empty = states
    f32, bf16 = jnp.float32, jnp.bfloat16
    own, seat = lax.div(me, half), lax.rem(me, half)
    partner = {"charge": lax.rem(me + half, devices)}
    wide = [j for j in range(states) if caps[j] > half]
    rights, orders, ranks = 2 * states + 1, 2 * states + 1 + sectors, 2 * states + 1 + 2 * sectors

    def blocks(cap, side):
        return min(cap, half) if side == 0 else max(cap - half, 0)

    def live(cap, side):
        return blocks(cap, side) * rows

    barrier = pltpu.get_barrier_semaphore()
    pl.semaphore_signal(barrier, inc=1, device_id={"split": 1 - h}, device_id_type=MESH)
    pl.semaphore_signal(barrier, inc=1, device_id=partner, device_id_type=MESH)
    across = {"charge": lax.rem(me + half, devices), "split": 1 - h}
    pl.semaphore_signal(barrier, inc=1, device_id=across, device_id_type=MESH)
    for i in range(1, half):
        pl.semaphore_signal(
            barrier, inc=1, device_id={"charge": own * half + lax.rem(seat + i, half)}, device_id_type=MESH)
    pl.semaphore_wait(barrier, half + 2)

    def m_copy(j):
        columns = pl.ds(0, live(caps[j], 1 - HOST[j]))
        return pltpu.make_async_remote_copy(
            src_ref=ms.at[j, :, columns], dst_ref=mr.at[j, :, columns], send_sem=msend.at[j],
            recv_sem=mrecv.at[j], device_id={"split": 1 - h}, device_id_type=MESH)

    def x_copy(j, b):
        s = HOST[j]
        columns = pl.ds(0, live(caps[j], 1 - s))
        here, there = (pl.ds(pl.multiple_of((n + b) * rows, rows), rows) for n in (0, s * half))
        return pltpu.make_async_remote_copy(
            src_ref=xb.at[j, here, columns], dst_ref=tb.at[j, there, columns],
            send_sem=xsend.at[j, b], recv_sem=xrecv.at[j, b], device_id={"split": 1 - h}, device_id_type=MESH)

    def chunk(j, part, side, to, source, kind):
        w = (w0, w1)[kind]
        columns = pl.ds(0, live(caps[j], side))
        from_rows = pl.ds(pl.multiple_of((part * half + to) * rows, rows), rows)
        return pltpu.make_async_remote_copy(
            src_ref=tb.at[j, from_rows, columns], dst_ref=w.at[source, j, :, columns],
            send_sem=zsend.at[j, part * half + to], recv_sem=zrecv.at[kind, source, j],
            device_id={"charge": own * half + to}, device_id_type=MESH)

    def forward(j, part, side, to):
        columns = live(caps[j], side)
        for kind in range(2):
            w = (w0, w1)[kind]

            @pl.when((own == part ^ kind) & (to != seat))
            def _():
                chunk(j, part, side, to, seat, kind).start()

            @pl.when((own == part ^ kind) & (to == seat))
            def _():
                def move(i, c):
                    here = pl.ds(pl.multiple_of((part * half + to) * rows + i * 32, 32), 32)
                    w[seat, j, pl.ds(pl.multiple_of(i * 32, 32), 32), 0:columns] = tb[j, here, 0:columns]
                    return c

                lax.fori_loop(0, rows // 32, move, 0)

    def scatter(j, part, side):
        count = blocks(caps[j], part)

        def one(i, c):
            forward(j, part, side, lax.rem(seat + 1 + i, count))
            return c

        lax.fori_loop(0, count, one, 0)

    def arrive(j, part, side, kind):
        if live(caps[j], side) == 0 or blocks(caps[j], part) == 0:
            return

        @pl.when(seat < blocks(caps[j], part))
        def _():
            def one(i, c):
                chunk(j, part, side, seat, lax.rem(seat + i, half), kind).wait_recv()
                return c

            lax.fori_loop(1, half, one, 0)

    def sent(j, part, side):
        count = blocks(caps[j], part)
        if live(caps[j], side) == 0 or count == 0:
            return

        def one(to, c):
            pl.when(to != seat)(lambda: chunk(j, part, side, to, seat, 0).wait_send())
            return c

        lax.fori_loop(0, count, one, 0)

    def hand(k, side):
        columns = pl.ds(0, live(crops[k], side))
        return pltpu.make_async_remote_copy(
            src_ref=up.at[k, :, columns], dst_ref=down.at[k, :, columns], send_sem=usend.at[k],
            recv_sem=drecv.at[k], device_id=partner, device_id_type=MESH)

    def aside(k):
        columns = pl.ds(0, live(crops[k], 0))
        return pltpu.make_async_remote_copy(
            src_ref=up.at[k, :, columns], dst_ref=via.at[k - AROUND, :, columns], send_sem=vsend.at[k - AROUND],
            recv_sem=vrecv.at[k - AROUND], device_id={"split": 1 - h}, device_id_type=MESH)

    def diagonal(k):
        columns = pl.ds(0, live(crops[k], 0))
        return pltpu.make_async_remote_copy(
            src_ref=via.at[k - AROUND, :, columns], dst_ref=down.at[k, :, columns], send_sem=fsend.at[k - AROUND],
            recv_sem=drecv.at[k], device_id=across, device_id_type=MESH)

    def handed(k, part, side, act):
        if live(crops[k], side) and blocks(crops[k], part):
            pl.when(seat < blocks(crops[k], part))(act)

    def relay(k, part, side, full):
        def act():
            columns = live(crops[k], side)
            r = meta_ref[orders + k]
            slots = [inv_ref[half + source, r] for source in range(half)]

            def tile(i, c):
                at = pl.ds(pl.multiple_of(i * 32, 32), 32)
                total = jnp.zeros((32, columns), f32)
                for source in range(half):
                    if full:
                        total = total + w1[source, slots[source], at, 0:columns].astype(f32)
                    else:
                        for j in range(k + 1):
                            one = w1[source, j, at, 0:columns].astype(f32)
                            total = total + jnp.where(slots[source] == j, one, 0.0)
                up[k, at, 0:columns] = total.astype(bf16)
                return c

            lax.fori_loop(0, rows // 32, tile, 0)
            (aside(k) if part == side == 0 and k >= AROUND else hand(k, side)).start()

        handed(k, part, side, act)

    def product(j):
        def tile(i, c):
            part = pl.ds(pl.multiple_of(i * 256, 256), 256)
            pb[j, part] = jnp.dot(lf[part], ms[j], preferred_element_type=f32).astype(bf16)
            return c

        lax.fori_loop(0, span // 256, tile, 0)

    def flipped(columns, right):
        return lax.dot_general(columns, right, (((0,), (0,)), ((), ())), preferred_element_type=f32).astype(bf16)

    def near(j, c):
        @pl.when((j < len(wide)) | (h == 0))
        def _():
            product(j)

            def tile(i, c):
                part = pl.ds(pl.multiple_of(h * width + i * 256, 256), 256)
                tb[j, part] = flipped(ms[j, :, pl.ds(pl.multiple_of(i * 256, 256), 256)], pb[j])
                return c

            lax.fori_loop(0, width // 256, tile, 0)

        for slot in range(states):
            for side in range(2):
                if live(caps[slot], side):
                    pl.when((h == side) & (j == slot))(functools.partial(scatter, slot, side, side))
        return c

    def turned(i, s, count):
        return count - 1 - i if s else i

    def far(j, s):
        o = 1 - s
        columns = live(caps[j], o)
        m_copy(j).wait_recv()

        def tile(i, c):
            part = pl.ds(pl.multiple_of(i * 256, 256), 256)
            px[part, 0:columns] = jnp.dot(lf[part], mr[j, :, 0:columns], preferred_element_type=f32).astype(bf16)
            return c

        lax.fori_loop(0, span // 256, tile, 0)

        def back(i, c):
            i = turned(i, s, blocks(caps[j], s))
            part = pl.ds(pl.multiple_of(i * rows, rows), rows)
            xb[j, part, 0:columns] = flipped(ms[j, :, part], px[:, 0:columns])
            x_copy(j, i).start()
            return c

        lax.fori_loop(0, blocks(caps[j], s), back, 0)

        def there(i, c):
            part = pl.ds(pl.multiple_of(o * width + i * rows, rows), rows)
            tb[j, part] = flipped(mr[j, :, pl.ds(pl.multiple_of(i * rows, rows), rows)], pb[j])
            return c

        lax.fori_loop(0, blocks(caps[j], o), there, 0)
        scatter(j, o, s)

    hosts = [[j for j in reversed(wide) if HOST[j] == s] for s in range(2)]
    for s in range(2):
        @pl.when(h == s)
        def _():
            for j in hosts[1 - s]:
                m_copy(j).start()
    lax.fori_loop(0, states, near, 0)
    w0[:, empty] = jnp.zeros((half, rows, width), bf16)
    w1[:, empty] = jnp.zeros((half, rows, width), bf16)

    def pass_on(s, part, slots, some, full):
        @pl.when(own == 1 - part)
        def _():
            for j in slots:
                arrive(j, part, s, 1)
            for k in some:
                relay(k, part, s, full)

    def turn_over():
        @pl.when(own == 1)
        def _():
            for k in range(AROUND, sectors):
                def act(k=k):
                    aside(k).wait_recv()
                    diagonal(k).start()

                handed(k, 0, 0, act)

    def course(s):
        for j in range(states - 1):
            pass_on(s, s, [j], [j], False)
        last = functools.partial(pass_on, s, s, [states - 1], range(states - 1, sectors), True)
        mine, theirs = hosts[s], hosts[1 - s]
        done = int(mine == [0])
        for j in mine[:-1]:
            far(j, s)
        if not done:
            last()
        far(mine[-1], s)
        if done:
            last()
            pass_on(s, 1 - s, [0], [0], False)
        if s == 1:
            turn_over()
        for j in theirs[:-1]:
            def step(b, c, j=j):
                x_copy(j, b).wait_recv()
                forward(j, 1 - s, s, b)
                return c

            lax.fori_loop(0, blocks(caps[j], 1 - s), step, 0)
        j = theirs[-1]
        count = blocks(caps[j], 1 - s)

        def step(b, c):
            b = turned(b, 1 - s, count)
            x_copy(j, b).wait_recv()
            forward(j, 1 - s, s, b)
            return c

        lax.fori_loop(0, count, step, 0)
        pass_on(s, 1 - s, range(done, states), range(done, sectors), True)
        for part in range(2):
            @pl.when(own == part)
            def _():
                for j in range(states):
                    arrive(j, part, s, 0)

    for s in range(2):
        pl.when(h == s)(functools.partial(course, s))

    def gather(r, c):
        total = w0[0, inv_ref[0, r]].astype(f32)
        for source in range(1, half):
            total = total + w0[source, inv_ref[source, r]].astype(f32)
        o_ref[r] = total
        return c

    lax.fori_loop(0, sectors, gather, 0)

    def received(s):
        for part in range(2):
            @pl.when(own == part)
            def _():
                for k in range(sectors):
                    handed(k, part, s, lambda k=k: hand(k, s).wait_recv())

    for s in range(2):
        pl.when(h == s)(functools.partial(received, s))

    def add(r, c):
        size = meta_ref[rights + r]
        col_ids = lax.broadcasted_iota(jnp.int32, (rows, width), 1) + h * width
        limit = jnp.where(size > me * rows, size, 0)
        o_ref[r] = jnp.where(col_ids < limit, o_ref[r] + down[meta_ref[ranks + r]].astype(f32), 0.0)
        return c

    lax.fori_loop(0, sectors, add, 0)

    def settle(s):
        for j in hosts[1 - s]:
            m_copy(j).wait_send()
        for j in hosts[s]:
            def left(b, c, j=j):
                x_copy(j, b).wait_send()
                return c

            lax.fori_loop(0, blocks(caps[j], s), left, 0)
        for j in range(states):
            for part in range(2):
                sent(j, part, s)
        for part in range(2):
            @pl.when(own == 1 - part)
            def _():
                for k in range(sectors):
                    if part == s == 0 and k >= AROUND:
                        handed(k, part, s, lambda k=k: aside(k).wait_send())
                    else:
                        handed(k, part, s, lambda k=k: hand(k, s).wait_send())
        if s == 1:
            @pl.when(own == 1)
            def _():
                for k in range(AROUND, sectors):
                    handed(k, 0, 0, lambda k=k: diagonal(k).wait_send())

    for s in range(2):
        pl.when(h == s)(functools.partial(settle, s))


def fused(at, inv, meta, whole, site):
    caps, crops = LADDER[at]
    states, span, width = site.shape
    devices, sectors = inv.shape
    rows, half = span // devices, devices // 2
    wide = max(j + 1 for j in range(states) if caps[j] > half)
    bf16 = jnp.bfloat16
    dma = pltpu.SemaphoreType.DMA
    return pl.pallas_call(
        functools.partial(kernel, caps, crops),
        out_shape=jax.ShapeDtypeStruct((sectors, rows, width), jnp.float32),
        in_specs=[pl.BlockSpec(memory_space=pltpu.SMEM)] * 2 + [pl.BlockSpec(memory_space=pltpu.VMEM)] * 2,
        out_specs=pl.BlockSpec(memory_space=pltpu.VMEM),
        scratch_shapes=[
            pltpu.VMEM((wide, span, width), bf16),
            pltpu.VMEM((states, span, width), bf16),
            pltpu.VMEM((span, width), bf16),
            pltpu.VMEM((wide, width, width), bf16),
            pltpu.VMEM((states, span, width), bf16),
            pltpu.VMEM((half, states + 1, rows, width), bf16),
            pltpu.VMEM((half, states + 1, rows, width), bf16),
            pltpu.VMEM((sectors, rows, width), bf16),
            pltpu.VMEM((sectors, rows, width), bf16),
            pltpu.VMEM((sectors - AROUND, rows, width), bf16),
            dma((wide,)), dma((wide,)), dma((wide, half)), dma((wide, half)),
            dma((states, devices)), dma((2, half, states)),
            dma((sectors,)), dma((sectors,)),
            dma((sectors - AROUND,)), dma((sectors - AROUND,)), dma((sectors - AROUND,)),
        ],
        compiler_params=pltpu.CompilerParams(
            collective_id=1 + at, has_side_effects=True, vmem_limit_bytes=50 * 2**20),
        cost_estimate=pl.CostEstimate(
            flops=4 * states * span * span * width, bytes_accessed=16 * 2**20, transcendentals=0),
    )(inv, meta, whole, site)


def body(groups, devices, left_env, site_tensor, left_sizes, right_sizes, targets):
    states = site_tensor.shape[1]
    sectors = right_sizes.shape[0]
    others = groups * devices
    i32 = jnp.int32
    dma = pltpu.SemaphoreType.DMA
    smem = pl.BlockSpec(memory_space=pltpu.SMEM)
    vmem = pl.BlockSpec(memory_space=pltpu.VMEM)
    inv, meta, pick, whole, masked = pl.pallas_call(
        agree,
        out_shape=[
            jax.ShapeDtypeStruct((devices, sectors), i32),
            jax.ShapeDtypeStruct((2 * states + 1 + 3 * sectors,), i32),
            jax.ShapeDtypeStruct((1,), i32),
            jax.ShapeDtypeStruct((site_tensor.shape[2],) * 2, jnp.bfloat16),
            jax.ShapeDtypeStruct(site_tensor.shape[1:], jnp.bfloat16),
        ],
        in_specs=[smem] * 3 + [pl.BlockSpec(memory_space=pltpu.HBM)] * 2,
        out_specs=[smem] * 3 + [vmem] * 2,
        scratch_shapes=[
            pltpu.VMEM((8, 128), i32), pltpu.VMEM((others, 8, 128), i32), pltpu.SMEM((others, 8, 128), i32),
            pltpu.VMEM(site_tensor.shape[1:], jnp.bfloat16),
            dma((others,)), dma((others,)), dma, dma, dma, dma, dma,
        ],
        compiler_params=pltpu.CompilerParams(collective_id=0, has_side_effects=True, vmem_limit_bytes=54 * 2**20),
    )(targets, left_sizes, right_sizes, left_env[0], site_tensor[0])
    branches = [functools.partial(fused, at) for at in range(len(LADDER))]
    return lax.switch(pick[0], branches, inv, meta, whole, masked)


def solution(mesh):
    in_specs = (
        P(("groups", "charge"), "split", None),
        P(("groups", "charge"), None, None, "split"),
        P(("groups", "charge")),
        P("groups"),
        P(("groups", "charge"), None),
    )
    out_specs = P("groups", "charge", "split")
    if mesh.shape["split"] == 2 and mesh.shape["charge"] == 8:
        inner = functools.partial(body, mesh.shape["groups"], mesh.shape["charge"])
    else:
        inner = gathered_body
    return jax.shard_map(inner, mesh=mesh, in_specs=in_specs, out_specs=out_specs, check_vma=False)
```

```python
import functools

import jax
import jax.numpy as jnp
from jax import lax
from jax.experimental import pallas as pl
from jax.experimental.pallas import tpu as pltpu
from jax.sharding import PartitionSpec as P

MESH = pl.DeviceIdType.MESH
HOST = (1, 0, 0, 0)
AROUND = 4
LADDER = (
    ((8, 8, 5, 4), (8, 8, 5, 5, 4, 3, 3, 2)),
    ((8, 8, 5, 4), (8, 8, 6, 5, 4, 3, 3, 3)),
    ((8, 8, 6, 4), (8, 8, 6, 5, 4, 3, 3, 2)),
    ((8, 8, 6, 4), (8, 8, 6, 6, 5, 3, 3, 3)),
    ((8, 8, 6, 5), (8, 8, 6, 6, 5, 3, 3, 3)),
    ((8, 8, 8, 8), (8, 8, 8, 8, 8, 8, 8, 8)),
)


def gathered_body(left_env, site_tensor, left_sizes, right_sizes, targets):
    states = site_tensor.shape[1]
    span = site_tensor.shape[2]
    width = site_tensor.shape[3]
    sectors = right_sizes.shape[0]
    column_base = lax.axis_index("split") * width
    row_ids = lax.broadcasted_iota(jnp.int32, (1, span, 1), 1)
    column_ids = lax.broadcasted_iota(jnp.int32, (1, 1, width), 2) + column_base
    slot_ids = lax.broadcasted_iota(jnp.int32, (states, sectors), 1)
    route = targets[0][:, None] == slot_ids
    live_cols = jnp.sum(jnp.where(route, right_sizes[None, :], 0), axis=1)
    keep = (row_ids < left_sizes[0]) & (column_ids < live_cols[:, None, None])
    masked = jnp.where(keep, site_tensor[0], jnp.zeros((), jnp.bfloat16))[None]
    product = jnp.einsum(
        "ik,skj->sij",
        lax.all_gather(left_env, "split", axis=1, tiled=True)[0],
        masked[0],
        preferred_element_type=jnp.float32,
    ).astype(jnp.bfloat16)
    terms = jnp.einsum(
        "ski,skj->sij",
        lax.all_gather(masked, "split", axis=3, tiled=True)[0],
        product,
        preferred_element_type=jnp.float32,
    ).astype(jnp.bfloat16)
    placed = jnp.einsum(
        "st,sij->tij", route.astype(jnp.bfloat16), terms, preferred_element_type=jnp.float32
    ).astype(jnp.bfloat16)
    return lax.psum_scatter(placed, "charge", scatter_dimension=1, tiled=True).astype(jnp.float32)


def agree(targets_ref, left_ref, right_ref, l_ref, m_ref, inv_ref, meta_ref, pick_ref, lf, ms,
          info, got, seen, site, send, recv, sem, lsend, lrecv, lown, mown):
    g = lax.axis_index("groups")
    me = lax.axis_index("charge")
    h = lax.axis_index("split")
    devices, sectors = inv_ref.shape[0], right_ref.shape[0]
    others = got.shape[0]
    states = targets_ref.shape[1]
    mine = g * devices + me
    rights = 2 * states + 1
    orders = rights + sectors
    ranks = orders + sectors

    barrier = pltpu.get_barrier_semaphore()

    def place(i):
        n = lax.rem(mine + i, others)
        return {"groups": n // devices, "charge": lax.rem(n, devices)}

    def greet(i, c):
        pl.semaphore_signal(barrier, inc=1, device_id=place(i), device_id_type=MESH)
        return c

    lax.fori_loop(1, others, greet, 0)
    pl.semaphore_signal(barrier, inc=1, device_id={"split": 1 - h}, device_id_type=MESH)

    span, width = ms.shape[1], ms.shape[2]
    half_rows = pl.ds(pl.multiple_of(h * width, width), width)
    m_own = pltpu.make_async_copy(m_ref, site, mown)
    m_own.start()
    l_own = pltpu.make_async_copy(l_ref, lf.at[half_rows], lown)
    l_own.start()
    every = [right_ref[r] for r in range(sectors)]
    place_of = []
    for r in range(sectors):
        ahead = jnp.int32(0)
        for k in range(sectors):
            if k != r:
                first = every[k] >= every[r] if k < r else every[k] > every[r]
                ahead = ahead + jnp.where(first, 1, 0)
        place_of.append(ahead)
        meta_ref[rights + r] = every[r]
        meta_ref[ranks + r] = ahead
    ordered = []
    for k in range(sectors):
        which, much = jnp.int32(0), jnp.int32(0)
        for r in range(sectors):
            which = jnp.where(place_of[r] == k, r, which)
            much = jnp.where(place_of[r] == k, every[r], much)
        meta_ref[orders + k] = which
        ordered.append(much)
    to = [targets_ref[0, j] for j in range(states)]
    size = [right_ref[t] for t in to]
    grade = [meta_ref[ranks + t] for t in to]
    rank = []
    for j in range(states):
        ahead = jnp.int32(0)
        for k in range(states):
            if k != j:
                ahead = ahead + jnp.where(grade[k] < grade[j], 1, 0)
        rank.append(ahead)
    lane = lax.broadcasted_iota(jnp.int32, info.shape, 1)
    packed = jnp.zeros(info.shape, jnp.int32)
    for slot in range(states):
        state, live, target = jnp.int32(0), jnp.int32(0), jnp.int32(0)
        for j in range(states):
            here = rank[j] == slot
            state = jnp.where(here, j, state)
            live = jnp.where(here, size[j], live)
            target = jnp.where(here, to[j], target)
        meta_ref[slot] = state
        meta_ref[states + slot] = live
        packed = jnp.where(lane == slot, target, packed)
        packed = jnp.where(lane == states + slot, live, packed)
    for k in range(sectors):
        packed = jnp.where(lane == 2 * states + k, ordered[k], packed)
    meta_ref[2 * states] = left_ref[0]
    info[...] = packed
    got[mine] = packed
    pl.semaphore_wait(barrier, others)
    l_copy = pltpu.make_async_remote_copy(
        src_ref=l_ref, dst_ref=lf.at[half_rows], send_sem=lsend, recv_sem=lrecv,
        device_id={"split": 1 - h}, device_id_type=MESH)
    l_copy.start()

    def copy(i):
        return pltpu.make_async_remote_copy(
            src_ref=info, dst_ref=got.at[mine], send_sem=send.at[i], recv_sem=recv.at[mine],
            device_id=place(i), device_id_type=MESH)

    def start(i, c):
        copy(i).start()
        return c

    def finish(i, c):
        n = lax.rem(mine + i, others)
        copy(i).wait_send()
        pltpu.make_async_remote_copy(
            src_ref=info, dst_ref=got.at[n], send_sem=send.at[i], recv_sem=recv.at[n],
            device_id=place(i), device_id_type=MESH).wait_recv()
        return c

    lax.fori_loop(1, others, start, 0)
    m_own.wait()

    def mask(j, c):
        state, live, deep = meta_ref[j], meta_ref[states + j], meta_ref[2 * states]

        def tile(i, c):
            part = pl.ds(pl.multiple_of(i * 128, 128), 128)
            row_ids = lax.broadcasted_iota(jnp.int32, (128, width), 0) + i * 128
            col_ids = lax.broadcasted_iota(jnp.int32, (128, width), 1) + h * width
            keep = (row_ids < deep) & (col_ids < live)
            ms[j, part] = jnp.where(keep, site[state, part].astype(jnp.float32), 0.0).astype(jnp.bfloat16)
            return c

        return lax.fori_loop(0, span // 128, tile, c)

    lax.fori_loop(0, states, mask, 0)
    lax.fori_loop(1, others, finish, 0)
    local = pltpu.make_async_copy(got, seen, sem)
    local.start()
    local.wait()

    half = devices // 2
    rows = span // devices
    side, seat = lax.div(me, half), lax.rem(me, half)
    for kind in range(2):
        block = (side if kind == 0 else 1 - side) * half + seat
        wants = [every[r] > jnp.maximum(block * rows, h * width) for r in range(sectors)]

        def route(s, c):
            reached = [seen[mine - seat + s, 0, j] for j in range(states)]
            for r in range(sectors):
                slot = jnp.int32(states)
                for j in range(states):
                    slot = jnp.where(reached[j] == r, j, slot)
                inv_ref[kind * half + s, r] = jnp.where(wants[r], slot, states)
            return c

        lax.fori_loop(0, half, route, 0)

    def widest(n, most):
        return tuple(jnp.maximum(m, seen[n, 0, states + j]) for j, m in enumerate(most))

    most = lax.fori_loop(0, others, widest, (jnp.int32(0),) * (states + sectors))
    pick = jnp.int32(len(LADDER) - 1)
    for at in range(len(LADDER) - 2, -1, -1):
        caps = LADDER[at][0] + LADDER[at][1]
        fits = most[0] <= caps[0] * rows
        for j in range(1, states + sectors):
            fits = fits & (most[j] <= caps[j] * rows)
        pick = jnp.where(fits, at, pick)
    pick_ref[0] = pick
    l_own.wait()
    l_copy.wait()


def kernel(caps, crops, inv_ref, meta_ref, lf, ms, o_ref, mr, pb, px, xb, tb, w0, w1, up, down, via,
           msend, mrecv, xsend, xrecv, zsend, zrecv, usend, drecv, vsend, vrecv, fsend):
    me = lax.axis_index("charge")
    h = lax.axis_index("split")
    states, span, width = ms.shape
    sectors, rows = o_ref.shape[0], o_ref.shape[1]
    devices = span // rows
    half = devices // 2
    empty = states
    f32, bf16 = jnp.float32, jnp.bfloat16
    own, seat = lax.div(me, half), lax.rem(me, half)
    partner = {"charge": lax.rem(me + half, devices)}
    wide = [j for j in range(states) if caps[j] > half]
    rights, orders, ranks = 2 * states + 1, 2 * states + 1 + sectors, 2 * states + 1 + 2 * sectors

    def blocks(cap, side):
        return min(cap, half) if side == 0 else max(cap - half, 0)

    def live(cap, side):
        return blocks(cap, side) * rows

    barrier = pltpu.get_barrier_semaphore()
    pl.semaphore_signal(barrier, inc=1, device_id={"split": 1 - h}, device_id_type=MESH)
    pl.semaphore_signal(barrier, inc=1, device_id=partner, device_id_type=MESH)
    across = {"charge": lax.rem(me + half, devices), "split": 1 - h}
    pl.semaphore_signal(barrier, inc=1, device_id=across, device_id_type=MESH)
    for i in range(1, half):
        pl.semaphore_signal(
            barrier, inc=1, device_id={"charge": own * half + lax.rem(seat + i, half)}, device_id_type=MESH)
    pl.semaphore_wait(barrier, half + 2)

    def m_copy(j):
        columns = pl.ds(0, live(caps[j], 1 - HOST[j]))
        return pltpu.make_async_remote_copy(
            src_ref=ms.at[j, :, columns], dst_ref=mr.at[j, :, columns], send_sem=msend.at[j],
            recv_sem=mrecv.at[j], device_id={"split": 1 - h}, device_id_type=MESH)

    def x_copy(j, b):
        s = HOST[j]
        columns = pl.ds(0, live(caps[j], 1 - s))
        here, there = (pl.ds(pl.multiple_of((n + b) * rows, rows), rows) for n in (0, s * half))
        return pltpu.make_async_remote_copy(
            src_ref=xb.at[j, here, columns], dst_ref=tb.at[j, there, columns],
            send_sem=xsend.at[j, b], recv_sem=xrecv.at[j, b], device_id={"split": 1 - h}, device_id_type=MESH)

    def chunk(j, part, side, to, source, kind):
        w = (w0, w1)[kind]
        columns = pl.ds(0, live(caps[j], side))
        from_rows = pl.ds(pl.multiple_of((part * half + to) * rows, rows), rows)
        return pltpu.make_async_remote_copy(
            src_ref=tb.at[j, from_rows, columns], dst_ref=w.at[source, j, :, columns],
            send_sem=zsend.at[j, part * half + to], recv_sem=zrecv.at[kind, source, j],
            device_id={"charge": own * half + to}, device_id_type=MESH)

    def forward(j, part, side, to):
        columns = live(caps[j], side)
        for kind in range(2):
            w = (w0, w1)[kind]

            @pl.when((own == part ^ kind) & (to != seat))
            def _():
                chunk(j, part, side, to, seat, kind).start()

            @pl.when((own == part ^ kind) & (to == seat))
            def _():
                def move(i, c):
                    here = pl.ds(pl.multiple_of((part * half + to) * rows + i * 32, 32), 32)
                    w[seat, j, pl.ds(pl.multiple_of(i * 32, 32), 32), 0:columns] = tb[j, here, 0:columns]
                    return c

                lax.fori_loop(0, rows // 32, move, 0)

    def scatter(j, part, side):
        count = blocks(caps[j], part)

        def one(i, c):
            forward(j, part, side, lax.rem(seat + 1 + i, count))
            return c

        lax.fori_loop(0, count, one, 0)

    def arrive(j, part, side, kind):
        if live(caps[j], side) == 0 or blocks(caps[j], part) == 0:
            return

        @pl.when(seat < blocks(caps[j], part))
        def _():
            def one(i, c):
                chunk(j, part, side, seat, lax.rem(seat + i, half), kind).wait_recv()
                return c

            lax.fori_loop(1, half, one, 0)

    def sent(j, part, side):
        count = blocks(caps[j], part)
        if live(caps[j], side) == 0 or count == 0:
            return

        def one(to, c):
            pl.when(to != seat)(lambda: chunk(j, part, side, to, seat, 0).wait_send())
            return c

        lax.fori_loop(0, count, one, 0)

    def hand(k, side):
        columns = pl.ds(0, live(crops[k], side))
        return pltpu.make_async_remote_copy(
            src_ref=up.at[k, :, columns], dst_ref=down.at[k, :, columns], send_sem=usend.at[k],
            recv_sem=drecv.at[k], device_id=partner, device_id_type=MESH)

    def aside(k):
        columns = pl.ds(0, live(crops[k], 0))
        return pltpu.make_async_remote_copy(
            src_ref=up.at[k, :, columns], dst_ref=via.at[k - AROUND, :, columns], send_sem=vsend.at[k - AROUND],
            recv_sem=vrecv.at[k - AROUND], device_id={"split": 1 - h}, device_id_type=MESH)

    def diagonal(k):
        columns = pl.ds(0, live(crops[k], 0))
        return pltpu.make_async_remote_copy(
            src_ref=via.at[k - AROUND, :, columns], dst_ref=down.at[k, :, columns], send_sem=fsend.at[k - AROUND],
            recv_sem=drecv.at[k], device_id=across, device_id_type=MESH)

    def split_up(k, part, side, around, across):
        if part != 0 or side != 0 or k < AROUND:
            across()
        elif k > AROUND:
            around()
        else:
            pl.when(seat < half // 2)(around)
            pl.when(seat >= half // 2)(across)

    def handed(k, part, side, act):
        if live(crops[k], side) and blocks(crops[k], part):
            pl.when(seat < blocks(crops[k], part))(act)

    def relay(k, part, side, full):
        def act():
            columns = live(crops[k], side)
            r = meta_ref[orders + k]
            slots = [inv_ref[half + source, r] for source in range(half)]

            def tile(i, c):
                at = pl.ds(pl.multiple_of(i * 32, 32), 32)
                total = jnp.zeros((32, columns), f32)
                for source in range(half):
                    if full:
                        total = total + w1[source, slots[source], at, 0:columns].astype(f32)
                    else:
                        for j in range(k + 1):
                            one = w1[source, j, at, 0:columns].astype(f32)
                            total = total + jnp.where(slots[source] == j, one, 0.0)
                up[k, at, 0:columns] = total.astype(bf16)
                return c

            lax.fori_loop(0, rows // 32, tile, 0)
            split_up(k, part, side, lambda: aside(k).start(), lambda: hand(k, side).start())

        handed(k, part, side, act)

    def product(j):
        def tile(i, c):
            part = pl.ds(pl.multiple_of(i * 256, 256), 256)
            pb[j, part] = jnp.dot(lf[part], ms[j], preferred_element_type=f32).astype(bf16)
            return c

        lax.fori_loop(0, span // 256, tile, 0)

    def flipped(columns, right):
        return lax.dot_general(columns, right, (((0,), (0,)), ((), ())), preferred_element_type=f32).astype(bf16)

    def near(j, c):
        @pl.when((j < len(wide)) | (h == 0))
        def _():
            product(j)

            def tile(i, c):
                part = pl.ds(pl.multiple_of(h * width + i * 256, 256), 256)
                tb[j, part] = flipped(ms[j, :, pl.ds(pl.multiple_of(i * 256, 256), 256)], pb[j])
                return c

            lax.fori_loop(0, width // 256, tile, 0)

        for slot in range(states):
            for side in range(2):
                if live(caps[slot], side):
                    pl.when((h == side) & (j == slot))(functools.partial(scatter, slot, side, side))
        return c

    def turned(i, s, count):
        return count - 1 - i

    def far(j, s):
        o = 1 - s
        columns = live(caps[j], o)
        m_copy(j).wait_recv()

        def tile(i, c):
            part = pl.ds(pl.multiple_of(i * 256, 256), 256)
            px[part, 0:columns] = jnp.dot(lf[part], mr[j, :, 0:columns], preferred_element_type=f32).astype(bf16)
            return c

        lax.fori_loop(0, span // 256, tile, 0)

        def back(i, c):
            i = turned(i, s, blocks(caps[j], s))
            part = pl.ds(pl.multiple_of(i * rows, rows), rows)
            xb[j, part, 0:columns] = flipped(ms[j, :, part], px[:, 0:columns])
            x_copy(j, i).start()
            return c

        lax.fori_loop(0, blocks(caps[j], s), back, 0)

        def there(i, c):
            part = pl.ds(pl.multiple_of(o * width + i * rows, rows), rows)
            tb[j, part] = flipped(mr[j, :, pl.ds(pl.multiple_of(i * rows, rows), rows)], pb[j])
            return c

        lax.fori_loop(0, blocks(caps[j], o), there, 0)
        scatter(j, o, s)

    hosts = [[j for j in reversed(wide) if HOST[j] == s] for s in range(2)]
    for s in range(2):
        @pl.when(h == s)
        def _():
            for j in hosts[1 - s]:
                m_copy(j).start()
    lax.fori_loop(0, states, near, 0)
    w0[:, empty] = jnp.zeros((half, rows, width), bf16)
    w1[:, empty] = jnp.zeros((half, rows, width), bf16)

    def pass_on(s, part, slots, some, full):
        @pl.when(own == 1 - part)
        def _():
            for j in slots:
                arrive(j, part, s, 1)
            for k in some:
                relay(k, part, s, full)

    def turn_over():
        @pl.when(own == 1)
        def _():
            for k in range(AROUND, sectors):
                def act(k=k):
                    aside(k).wait_recv()
                    diagonal(k).start()

                handed(k, 0, 0, lambda k=k, act=act: split_up(k, 0, 0, act, lambda: None))

    def course(s):
        for j in range(states - 1):
            pass_on(s, s, [j], [j], False)
        last = functools.partial(pass_on, s, s, [states - 1], range(states - 1, sectors), True)
        mine, theirs = hosts[s], hosts[1 - s]
        done = int(mine == [0])
        for j in mine[:-1]:
            far(j, s)
        if not done:
            last()
        far(mine[-1], s)
        if done:
            last()
            pass_on(s, 1 - s, [0], [0], False)
        for j in theirs[:-1]:
            def step(b, c, j=j):
                x_copy(j, b).wait_recv()
                forward(j, 1 - s, s, b)
                return c

            lax.fori_loop(0, blocks(caps[j], 1 - s), step, 0)
        if s == 1:
            turn_over()
        j = theirs[-1]
        count = blocks(caps[j], 1 - s)

        def step(b, c):
            b = turned(b, 1 - s, count)
            x_copy(j, b).wait_recv()
            forward(j, 1 - s, s, b)
            return c

        lax.fori_loop(0, count, step, 0)
        pass_on(s, 1 - s, range(done, states), range(done, sectors), True)
        for part in range(2):
            @pl.when(own == part)
            def _():
                for j in range(states):
                    arrive(j, part, s, 0)

    for s in range(2):
        pl.when(h == s)(functools.partial(course, s))

    def gather(r, c):
        total = w0[0, inv_ref[0, r]].astype(f32)
        for source in range(1, half):
            total = total + w0[source, inv_ref[source, r]].astype(f32)
        o_ref[r] = total
        return c

    lax.fori_loop(0, sectors, gather, 0)

    def received(s):
        for part in range(2):
            @pl.when(own == part)
            def _():
                for k in range(sectors):
                    handed(k, part, s, lambda k=k: hand(k, s).wait_recv())

    for s in range(2):
        pl.when(h == s)(functools.partial(received, s))

    def add(r, c):
        size = meta_ref[rights + r]
        col_ids = lax.broadcasted_iota(jnp.int32, (rows, width), 1) + h * width
        limit = jnp.where(size > me * rows, size, 0)
        o_ref[r] = jnp.where(col_ids < limit, o_ref[r] + down[meta_ref[ranks + r]].astype(f32), 0.0)
        return c

    lax.fori_loop(0, sectors, add, 0)

    def settle(s):
        for j in hosts[1 - s]:
            m_copy(j).wait_send()
        for j in hosts[s]:
            def left(b, c, j=j):
                x_copy(j, b).wait_send()
                return c

            lax.fori_loop(0, blocks(caps[j], s), left, 0)
        for j in range(states):
            for part in range(2):
                sent(j, part, s)
        for part in range(2):
            @pl.when(own == 1 - part)
            def _():
                for k in range(sectors):
                    handed(k, part, s, lambda k=k, part=part: split_up(
                        k, part, s, lambda: aside(k).wait_send(), lambda: hand(k, s).wait_send()))
        if s == 1:
            @pl.when(own == 1)
            def _():
                for k in range(AROUND, sectors):
                    handed(k, 0, 0, lambda k=k: split_up(
                        k, 0, 0, lambda: diagonal(k).wait_send(), lambda: None))

    for s in range(2):
        pl.when(h == s)(functools.partial(settle, s))


def fused(at, inv, meta, whole, site):
    caps, crops = LADDER[at]
    states, span, width = site.shape
    devices, sectors = inv.shape
    rows, half = span // devices, devices // 2
    wide = max(j + 1 for j in range(states) if caps[j] > half)
    bf16 = jnp.bfloat16
    dma = pltpu.SemaphoreType.DMA
    return pl.pallas_call(
        functools.partial(kernel, caps, crops),
        out_shape=jax.ShapeDtypeStruct((sectors, rows, width), jnp.float32),
        in_specs=[pl.BlockSpec(memory_space=pltpu.SMEM)] * 2 + [pl.BlockSpec(memory_space=pltpu.VMEM)] * 2,
        out_specs=pl.BlockSpec(memory_space=pltpu.VMEM),
        scratch_shapes=[
            pltpu.VMEM((wide, span, width), bf16),
            pltpu.VMEM((states, span, width), bf16),
            pltpu.VMEM((span, width), bf16),
            pltpu.VMEM((wide, width, width), bf16),
            pltpu.VMEM((states, span, width), bf16),
            pltpu.VMEM((half, states + 1, rows, width), bf16),
            pltpu.VMEM((half, states + 1, rows, width), bf16),
            pltpu.VMEM((sectors, rows, width), bf16),
            pltpu.VMEM((sectors, rows, width), bf16),
            pltpu.VMEM((sectors - AROUND, rows, width), bf16),
            dma((wide,)), dma((wide,)), dma((wide, half)), dma((wide, half)),
            dma((states, devices)), dma((2, half, states)),
            dma((sectors,)), dma((sectors,)),
            dma((sectors - AROUND,)), dma((sectors - AROUND,)), dma((sectors - AROUND,)),
        ],
        compiler_params=pltpu.CompilerParams(
            collective_id=1 + at, has_side_effects=True, vmem_limit_bytes=50 * 2**20),
        cost_estimate=pl.CostEstimate(
            flops=4 * states * span * span * width, bytes_accessed=16 * 2**20, transcendentals=0),
    )(inv, meta, whole, site)


def body(groups, devices, left_env, site_tensor, left_sizes, right_sizes, targets):
    states = site_tensor.shape[1]
    sectors = right_sizes.shape[0]
    others = groups * devices
    i32 = jnp.int32
    dma = pltpu.SemaphoreType.DMA
    smem = pl.BlockSpec(memory_space=pltpu.SMEM)
    vmem = pl.BlockSpec(memory_space=pltpu.VMEM)
    inv, meta, pick, whole, masked = pl.pallas_call(
        agree,
        out_shape=[
            jax.ShapeDtypeStruct((devices, sectors), i32),
            jax.ShapeDtypeStruct((2 * states + 1 + 3 * sectors,), i32),
            jax.ShapeDtypeStruct((1,), i32),
            jax.ShapeDtypeStruct((site_tensor.shape[2],) * 2, jnp.bfloat16),
            jax.ShapeDtypeStruct(site_tensor.shape[1:], jnp.bfloat16),
        ],
        in_specs=[smem] * 3 + [pl.BlockSpec(memory_space=pltpu.HBM)] * 2,
        out_specs=[smem] * 3 + [vmem] * 2,
        scratch_shapes=[
            pltpu.VMEM((8, 128), i32), pltpu.VMEM((others, 8, 128), i32), pltpu.SMEM((others, 8, 128), i32),
            pltpu.VMEM(site_tensor.shape[1:], jnp.bfloat16),
            dma((others,)), dma((others,)), dma, dma, dma, dma, dma,
        ],
        compiler_params=pltpu.CompilerParams(collective_id=0, has_side_effects=True, vmem_limit_bytes=54 * 2**20),
    )(targets, left_sizes, right_sizes, left_env[0], site_tensor[0])
    branches = [functools.partial(fused, at) for at in range(len(LADDER))]
    return lax.switch(pick[0], branches, inv, meta, whole, masked)


def solution(mesh):
    in_specs = (
        P(("groups", "charge"), "split", None),
        P(("groups", "charge"), None, None, "split"),
        P(("groups", "charge")),
        P("groups"),
        P(("groups", "charge"), None),
    )
    out_specs = P("groups", "charge", "split")
    if mesh.shape["split"] == 2 and mesh.shape["charge"] == 8:
        inner = functools.partial(body, mesh.shape["groups"], mesh.shape["charge"])
    else:
        inner = gathered_body
    return jax.shard_map(inner, mesh=mesh, in_specs=in_specs, out_specs=out_specs, check_vma=False)
```

```python
import functools

import jax
import jax.numpy as jnp
from jax import lax
from jax.experimental import pallas as pl
from jax.experimental.pallas import tpu as pltpu
from jax.sharding import PartitionSpec as P

MESH = pl.DeviceIdType.MESH
HOST = (1, 0, 0, 0)
AROUND = 4
LADDER = (
    ((8, 8, 5, 4), (8, 8, 5, 5, 4, 3, 3, 2)),
    ((8, 8, 5, 4), (8, 8, 6, 5, 4, 3, 3, 3)),
    ((8, 8, 6, 4), (8, 8, 6, 5, 4, 3, 3, 2)),
    ((8, 8, 6, 4), (8, 8, 6, 6, 5, 3, 3, 3)),
    ((8, 8, 6, 5), (8, 8, 6, 6, 5, 3, 3, 3)),
    ((8, 8, 8, 8), (8, 8, 8, 8, 8, 8, 8, 8)),
)


def gathered_body(left_env, site_tensor, left_sizes, right_sizes, targets):
    states = site_tensor.shape[1]
    span = site_tensor.shape[2]
    width = site_tensor.shape[3]
    sectors = right_sizes.shape[0]
    column_base = lax.axis_index("split") * width
    row_ids = lax.broadcasted_iota(jnp.int32, (1, span, 1), 1)
    column_ids = lax.broadcasted_iota(jnp.int32, (1, 1, width), 2) + column_base
    slot_ids = lax.broadcasted_iota(jnp.int32, (states, sectors), 1)
    route = targets[0][:, None] == slot_ids
    live_cols = jnp.sum(jnp.where(route, right_sizes[None, :], 0), axis=1)
    keep = (row_ids < left_sizes[0]) & (column_ids < live_cols[:, None, None])
    masked = jnp.where(keep, site_tensor[0], jnp.zeros((), jnp.bfloat16))[None]
    product = jnp.einsum(
        "ik,skj->sij",
        lax.all_gather(left_env, "split", axis=1, tiled=True)[0],
        masked[0],
        preferred_element_type=jnp.float32,
    ).astype(jnp.bfloat16)
    terms = jnp.einsum(
        "ski,skj->sij",
        lax.all_gather(masked, "split", axis=3, tiled=True)[0],
        product,
        preferred_element_type=jnp.float32,
    ).astype(jnp.bfloat16)
    placed = jnp.einsum(
        "st,sij->tij", route.astype(jnp.bfloat16), terms, preferred_element_type=jnp.float32
    ).astype(jnp.bfloat16)
    return lax.psum_scatter(placed, "charge", scatter_dimension=1, tiled=True).astype(jnp.float32)


def agree(targets_ref, left_ref, right_ref, l_ref, m_ref, inv_ref, meta_ref, pick_ref, lf, ms,
          info, got, seen, site, send, recv, sem, lsend, lrecv, lown, mown):
    g = lax.axis_index("groups")
    me = lax.axis_index("charge")
    h = lax.axis_index("split")
    devices, sectors = inv_ref.shape[0], right_ref.shape[0]
    others = got.shape[0]
    states = targets_ref.shape[1]
    mine = g * devices + me
    rights = 2 * states + 1
    orders = rights + sectors
    ranks = orders + sectors

    barrier = pltpu.get_barrier_semaphore()

    def place(i):
        n = lax.rem(mine + i, others)
        return {"groups": n // devices, "charge": lax.rem(n, devices)}

    def greet(i, c):
        pl.semaphore_signal(barrier, inc=1, device_id=place(i), device_id_type=MESH)
        return c

    lax.fori_loop(1, others, greet, 0)
    pl.semaphore_signal(barrier, inc=1, device_id={"split": 1 - h}, device_id_type=MESH)

    span, width = ms.shape[1], ms.shape[2]
    half_rows = pl.ds(pl.multiple_of(h * width, width), width)
    m_own = pltpu.make_async_copy(m_ref, site, mown)
    m_own.start()
    l_own = pltpu.make_async_copy(l_ref, lf.at[half_rows], lown)
    l_own.start()
    every = [right_ref[r] for r in range(sectors)]
    place_of = []
    for r in range(sectors):
        ahead = jnp.int32(0)
        for k in range(sectors):
            if k != r:
                first = every[k] >= every[r] if k < r else every[k] > every[r]
                ahead = ahead + jnp.where(first, 1, 0)
        place_of.append(ahead)
        meta_ref[rights + r] = every[r]
        meta_ref[ranks + r] = ahead
    ordered = []
    for k in range(sectors):
        which, much = jnp.int32(0), jnp.int32(0)
        for r in range(sectors):
            which = jnp.where(place_of[r] == k, r, which)
            much = jnp.where(place_of[r] == k, every[r], much)
        meta_ref[orders + k] = which
        ordered.append(much)
    to = [targets_ref[0, j] for j in range(states)]
    size = [right_ref[t] for t in to]
    grade = [meta_ref[ranks + t] for t in to]
    rank = []
    for j in range(states):
        ahead = jnp.int32(0)
        for k in range(states):
            if k != j:
                ahead = ahead + jnp.where(grade[k] < grade[j], 1, 0)
        rank.append(ahead)
    lane = lax.broadcasted_iota(jnp.int32, info.shape, 1)
    packed = jnp.zeros(info.shape, jnp.int32)
    for slot in range(states):
        state, live, target = jnp.int32(0), jnp.int32(0), jnp.int32(0)
        for j in range(states):
            here = rank[j] == slot
            state = jnp.where(here, j, state)
            live = jnp.where(here, size[j], live)
            target = jnp.where(here, to[j], target)
        meta_ref[slot] = state
        meta_ref[states + slot] = live
        packed = jnp.where(lane == slot, target, packed)
        packed = jnp.where(lane == states + slot, live, packed)
    for k in range(sectors):
        packed = jnp.where(lane == 2 * states + k, ordered[k], packed)
    meta_ref[2 * states] = left_ref[0]
    info[...] = packed
    got[mine] = packed
    pl.semaphore_wait(barrier, others)
    l_copy = pltpu.make_async_remote_copy(
        src_ref=l_ref, dst_ref=lf.at[half_rows], send_sem=lsend, recv_sem=lrecv,
        device_id={"split": 1 - h}, device_id_type=MESH)
    l_copy.start()

    def copy(i):
        return pltpu.make_async_remote_copy(
            src_ref=info, dst_ref=got.at[mine], send_sem=send.at[i], recv_sem=recv.at[mine],
            device_id=place(i), device_id_type=MESH)

    def start(i, c):
        copy(i).start()
        return c

    def finish(i, c):
        n = lax.rem(mine + i, others)
        copy(i).wait_send()
        pltpu.make_async_remote_copy(
            src_ref=info, dst_ref=got.at[n], send_sem=send.at[i], recv_sem=recv.at[n],
            device_id=place(i), device_id_type=MESH).wait_recv()
        return c

    lax.fori_loop(1, others, start, 0)
    m_own.wait()

    def mask(j, c):
        state, live, deep = meta_ref[j], meta_ref[states + j], meta_ref[2 * states]

        def tile(i, c):
            part = pl.ds(pl.multiple_of(i * 128, 128), 128)
            row_ids = lax.broadcasted_iota(jnp.int32, (128, width), 0) + i * 128
            col_ids = lax.broadcasted_iota(jnp.int32, (128, width), 1) + h * width
            keep = (row_ids < deep) & (col_ids < live)
            ms[j, part] = jnp.where(keep, site[state, part].astype(jnp.float32), 0.0).astype(jnp.bfloat16)
            return c

        return lax.fori_loop(0, span // 128, tile, c)

    lax.fori_loop(0, states, mask, 0)
    lax.fori_loop(1, others, finish, 0)
    local = pltpu.make_async_copy(got, seen, sem)
    local.start()
    local.wait()

    half = devices // 2
    rows = span // devices
    side, seat = lax.div(me, half), lax.rem(me, half)
    for kind in range(2):
        block = (side if kind == 0 else 1 - side) * half + seat
        wants = [every[r] > jnp.maximum(block * rows, h * width) for r in range(sectors)]

        def route(s, c):
            reached = [seen[mine - seat + s, 0, j] for j in range(states)]
            for r in range(sectors):
                slot = jnp.int32(states)
                for j in range(states):
                    slot = jnp.where(reached[j] == r, j, slot)
                inv_ref[kind * half + s, r] = jnp.where(wants[r], slot, states)
            return c

        lax.fori_loop(0, half, route, 0)

    def widest(n, most):
        return tuple(jnp.maximum(m, seen[n, 0, states + j]) for j, m in enumerate(most))

    most = lax.fori_loop(0, others, widest, (jnp.int32(0),) * (states + sectors))
    pick = jnp.int32(len(LADDER) - 1)
    for at in range(len(LADDER) - 2, -1, -1):
        caps = LADDER[at][0] + LADDER[at][1]
        fits = most[0] <= caps[0] * rows
        for j in range(1, states + sectors):
            fits = fits & (most[j] <= caps[j] * rows)
        pick = jnp.where(fits, at, pick)
    pick_ref[0] = pick
    l_own.wait()
    l_copy.wait()


def kernel(caps, crops, inv_ref, meta_ref, lf, ms, o_ref, mr, pb, px, xb, tb, w0, w1, up, down, via,
           msend, mrecv, xsend, xrecv, zsend, zrecv, usend, drecv, vsend, vrecv, fsend):
    me = lax.axis_index("charge")
    h = lax.axis_index("split")
    states, span, width = ms.shape
    sectors, rows = o_ref.shape[0], o_ref.shape[1]
    devices = span // rows
    half = devices // 2
    empty = states
    f32, bf16 = jnp.float32, jnp.bfloat16
    own, seat = lax.div(me, half), lax.rem(me, half)
    partner = {"charge": lax.rem(me + half, devices)}
    wide = [j for j in range(states) if caps[j] > half]
    rights, orders, ranks = 2 * states + 1, 2 * states + 1 + sectors, 2 * states + 1 + 2 * sectors

    def blocks(cap, side):
        return min(cap, half) if side == 0 else max(cap - half, 0)

    def live(cap, side):
        return blocks(cap, side) * rows

    barrier = pltpu.get_barrier_semaphore()
    pl.semaphore_signal(barrier, inc=1, device_id={"split": 1 - h}, device_id_type=MESH)
    pl.semaphore_signal(barrier, inc=1, device_id=partner, device_id_type=MESH)
    across = {"charge": lax.rem(me + half, devices), "split": 1 - h}
    pl.semaphore_signal(barrier, inc=1, device_id=across, device_id_type=MESH)
    for i in range(1, half):
        pl.semaphore_signal(
            barrier, inc=1, device_id={"charge": own * half + lax.rem(seat + i, half)}, device_id_type=MESH)
    pl.semaphore_wait(barrier, half + 2)

    def m_copy(j):
        columns = pl.ds(0, live(caps[j], 1 - HOST[j]))
        return pltpu.make_async_remote_copy(
            src_ref=ms.at[j, :, columns], dst_ref=mr.at[j, :, columns], send_sem=msend.at[j],
            recv_sem=mrecv.at[j], device_id={"split": 1 - h}, device_id_type=MESH)

    def x_copy(j, b):
        s = HOST[j]
        columns = pl.ds(0, live(caps[j], 1 - s))
        here, there = (pl.ds(pl.multiple_of((n + b) * rows, rows), rows) for n in (0, s * half))
        return pltpu.make_async_remote_copy(
            src_ref=xb.at[j, here, columns], dst_ref=tb.at[j, there, columns],
            send_sem=xsend.at[j, b], recv_sem=xrecv.at[j, b], device_id={"split": 1 - h}, device_id_type=MESH)

    def chunk(j, part, side, to, source, kind):
        w = (w0, w1)[kind]
        columns = pl.ds(0, live(caps[j], side))
        from_rows = pl.ds(pl.multiple_of((part * half + to) * rows, rows), rows)
        return pltpu.make_async_remote_copy(
            src_ref=tb.at[j, from_rows, columns], dst_ref=w.at[source, j, :, columns],
            send_sem=zsend.at[j, part * half + to], recv_sem=zrecv.at[kind, source, j],
            device_id={"charge": own * half + to}, device_id_type=MESH)

    def forward(j, part, side, to):
        columns = live(caps[j], side)
        for kind in range(2):
            w = (w0, w1)[kind]

            @pl.when((own == part ^ kind) & (to != seat))
            def _():
                chunk(j, part, side, to, seat, kind).start()

            @pl.when((own == part ^ kind) & (to == seat))
            def _():
                def move(i, c):
                    here = pl.ds(pl.multiple_of((part * half + to) * rows + i * 32, 32), 32)
                    w[seat, j, pl.ds(pl.multiple_of(i * 32, 32), 32), 0:columns] = tb[j, here, 0:columns]
                    return c

                lax.fori_loop(0, rows // 32, move, 0)

    def scatter(j, part, side):
        count = blocks(caps[j], part)

        def one(i, c):
            forward(j, part, side, lax.rem(seat + 1 + i, count))
            return c

        lax.fori_loop(0, count, one, 0)

    def arrive(j, part, side, kind):
        if live(caps[j], side) == 0 or blocks(caps[j], part) == 0:
            return

        @pl.when(seat < blocks(caps[j], part))
        def _():
            def one(i, c):
                chunk(j, part, side, seat, lax.rem(seat + i, half), kind).wait_recv()
                return c

            lax.fori_loop(1, half, one, 0)

    def sent(j, part, side):
        count = blocks(caps[j], part)
        if live(caps[j], side) == 0 or count == 0:
            return

        def one(to, c):
            pl.when(to != seat)(lambda: chunk(j, part, side, to, seat, 0).wait_send())
            return c

        lax.fori_loop(0, count, one, 0)

    def hand(k, side):
        columns = pl.ds(0, live(crops[k], side))
        return pltpu.make_async_remote_copy(
            src_ref=up.at[k, :, columns], dst_ref=down.at[k, :, columns], send_sem=usend.at[k],
            recv_sem=drecv.at[k], device_id=partner, device_id_type=MESH)

    def aside(k):
        columns = pl.ds(0, live(crops[k], 0))
        return pltpu.make_async_remote_copy(
            src_ref=up.at[k, :, columns], dst_ref=via.at[k - AROUND, :, columns], send_sem=vsend.at[k - AROUND],
            recv_sem=vrecv.at[k - AROUND], device_id={"split": 1 - h}, device_id_type=MESH)

    def diagonal(k):
        columns = pl.ds(0, live(crops[k], 0))
        return pltpu.make_async_remote_copy(
            src_ref=via.at[k - AROUND, :, columns], dst_ref=down.at[k, :, columns], send_sem=fsend.at[k - AROUND],
            recv_sem=drecv.at[k], device_id=across, device_id_type=MESH)

    def split_up(k, part, side, around, across):
        if part != 0 or side != 0 or k < AROUND:
            across()
        elif k > AROUND:
            around()
        else:
            pl.when(seat < half // 2)(around)
            pl.when(seat >= half // 2)(across)

    def handed(k, part, side, act):
        if live(crops[k], side) and blocks(crops[k], part):
            pl.when(seat < blocks(crops[k], part))(act)

    def relay(k, part, side, full):
        def act():
            columns = live(crops[k], side)
            r = meta_ref[orders + k]
            slots = [inv_ref[half + source, r] for source in range(half)]

            def tile(i, c):
                at = pl.ds(pl.multiple_of(i * 32, 32), 32)
                total = jnp.zeros((32, columns), f32)
                for source in range(half):
                    if full:
                        total = total + w1[source, slots[source], at, 0:columns].astype(f32)
                    else:
                        for j in range(k + 1):
                            one = w1[source, j, at, 0:columns].astype(f32)
                            total = total + jnp.where(slots[source] == j, one, 0.0)
                up[k, at, 0:columns] = total.astype(bf16)
                return c

            lax.fori_loop(0, rows // 32, tile, 0)
            split_up(k, part, side, lambda: aside(k).start(), lambda: hand(k, side).start())

        handed(k, part, side, act)

    def product(j):
        def tile(i, c):
            part = pl.ds(pl.multiple_of(i * 256, 256), 256)
            pb[j, part] = jnp.dot(lf[part], ms[j], preferred_element_type=f32).astype(bf16)
            return c

        lax.fori_loop(0, span // 256, tile, 0)

    def flipped(columns, right):
        return lax.dot_general(columns, right, (((0,), (0,)), ((), ())), preferred_element_type=f32).astype(bf16)

    def near(j, c):
        @pl.when((j < len(wide)) | (h == 0))
        def _():
            product(j)

            def tile(i, c):
                part = pl.ds(pl.multiple_of(h * width + i * 256, 256), 256)
                tb[j, part] = flipped(ms[j, :, pl.ds(pl.multiple_of(i * 256, 256), 256)], pb[j])
                return c

            lax.fori_loop(0, width // 256, tile, 0)

        for slot in range(states):
            for side in range(2):
                if live(caps[slot], side):
                    pl.when((h == side) & (j == slot))(functools.partial(scatter, slot, side, side))
        return c

    def turned(i, s, count):
        return count - 1 - i

    def far(j, s):
        o = 1 - s
        columns = live(caps[j], o)
        m_copy(j).wait_recv()

        def tile(i, c):
            part = pl.ds(pl.multiple_of(i * 256, 256), 256)
            px[part, 0:columns] = jnp.dot(lf[part], mr[j, :, 0:columns], preferred_element_type=f32).astype(bf16)
            return c

        lax.fori_loop(0, span // 256, tile, 0)

        def back(i, c):
            i = turned(i, s, blocks(caps[j], s))
            part = pl.ds(pl.multiple_of(i * rows, rows), rows)
            xb[j, part, 0:columns] = flipped(ms[j, :, part], px[:, 0:columns])
            x_copy(j, i).start()
            return c

        lax.fori_loop(0, blocks(caps[j], s), back, 0)

        def there(i, c):
            part = pl.ds(pl.multiple_of(o * width + i * rows, rows), rows)
            tb[j, part] = flipped(mr[j, :, pl.ds(pl.multiple_of(i * rows, rows), rows)], pb[j])
            return c

        lax.fori_loop(0, blocks(caps[j], o), there, 0)
        scatter(j, o, s)

    hosts = [[j for j in reversed(wide) if HOST[j] == s] for s in range(2)]
    if sum(caps[j] - half for j in wide[2:]) > 1:
        hosts[0].sort(key=lambda j: (j != 1, -j))
    for s in range(2):
        @pl.when(h == s)
        def _():
            for j in hosts[1 - s]:
                m_copy(j).start()
    lax.fori_loop(0, states, near, 0)
    w0[:, empty] = jnp.zeros((half, rows, width), bf16)
    w1[:, empty] = jnp.zeros((half, rows, width), bf16)

    def pass_on(s, part, slots, some, full):
        @pl.when(own == 1 - part)
        def _():
            for j in slots:
                arrive(j, part, s, 1)
            for k in some:
                relay(k, part, s, full)

    def turn_over():
        @pl.when(own == 1)
        def _():
            for k in range(AROUND, sectors):
                def act(k=k):
                    aside(k).wait_recv()
                    diagonal(k).start()

                handed(k, 0, 0, lambda k=k, act=act: split_up(k, 0, 0, act, lambda: None))

    def course(s):
        for j in range(states - 1):
            pass_on(s, s, [j], [j], False)
        last = functools.partial(pass_on, s, s, [states - 1], range(states - 1, sectors), True)
        mine, theirs = hosts[s], hosts[1 - s]
        done = int(mine == [0])
        for j in mine[:-1]:
            far(j, s)
        if not done:
            last()
        far(mine[-1], s)
        if done:
            last()
            pass_on(s, 1 - s, [0], [0], False)
        for j in theirs[:-1]:
            def step(b, c, j=j):
                x_copy(j, b).wait_recv()
                forward(j, 1 - s, s, b)
                return c

            lax.fori_loop(0, blocks(caps[j], 1 - s), step, 0)
        if s == 1:
            turn_over()
        j = theirs[-1]
        count = blocks(caps[j], 1 - s)

        def step(b, c):
            b = turned(b, 1 - s, count)
            x_copy(j, b).wait_recv()
            forward(j, 1 - s, s, b)
            return c

        lax.fori_loop(0, count, step, 0)
        pass_on(s, 1 - s, range(done, states), range(done, sectors), True)
        for part in range(2):
            @pl.when(own == part)
            def _():
                for j in range(states):
                    arrive(j, part, s, 0)

    for s in range(2):
        pl.when(h == s)(functools.partial(course, s))

    def gather(r, c):
        total = w0[0, inv_ref[0, r]].astype(f32)
        for source in range(1, half):
            total = total + w0[source, inv_ref[source, r]].astype(f32)
        o_ref[r] = total
        return c

    lax.fori_loop(0, sectors, gather, 0)

    def received(s):
        for part in range(2):
            @pl.when(own == part)
            def _():
                for k in range(sectors):
                    handed(k, part, s, lambda k=k: hand(k, s).wait_recv())

    for s in range(2):
        pl.when(h == s)(functools.partial(received, s))

    def add(r, c):
        size = meta_ref[rights + r]
        col_ids = lax.broadcasted_iota(jnp.int32, (rows, width), 1) + h * width
        limit = jnp.where(size > me * rows, size, 0)
        o_ref[r] = jnp.where(col_ids < limit, o_ref[r] + down[meta_ref[ranks + r]].astype(f32), 0.0)
        return c

    lax.fori_loop(0, sectors, add, 0)

    def settle(s):
        for j in hosts[1 - s]:
            m_copy(j).wait_send()
        for j in hosts[s]:
            def left(b, c, j=j):
                x_copy(j, b).wait_send()
                return c

            lax.fori_loop(0, blocks(caps[j], s), left, 0)
        for j in range(states):
            for part in range(2):
                sent(j, part, s)
        for part in range(2):
            @pl.when(own == 1 - part)
            def _():
                for k in range(sectors):
                    handed(k, part, s, lambda k=k, part=part: split_up(
                        k, part, s, lambda: aside(k).wait_send(), lambda: hand(k, s).wait_send()))
        if s == 1:
            @pl.when(own == 1)
            def _():
                for k in range(AROUND, sectors):
                    handed(k, 0, 0, lambda k=k: split_up(
                        k, 0, 0, lambda: diagonal(k).wait_send(), lambda: None))

    for s in range(2):
        pl.when(h == s)(functools.partial(settle, s))


def fused(at, inv, meta, whole, site):
    caps, crops = LADDER[at]
    states, span, width = site.shape
    devices, sectors = inv.shape
    rows, half = span // devices, devices // 2
    wide = max(j + 1 for j in range(states) if caps[j] > half)
    bf16 = jnp.bfloat16
    dma = pltpu.SemaphoreType.DMA
    return pl.pallas_call(
        functools.partial(kernel, caps, crops),
        out_shape=jax.ShapeDtypeStruct((sectors, rows, width), jnp.float32),
        in_specs=[pl.BlockSpec(memory_space=pltpu.SMEM)] * 2 + [pl.BlockSpec(memory_space=pltpu.VMEM)] * 2,
        out_specs=pl.BlockSpec(memory_space=pltpu.VMEM),
        scratch_shapes=[
            pltpu.VMEM((wide, span, width), bf16),
            pltpu.VMEM((states, span, width), bf16),
            pltpu.VMEM((span, width), bf16),
            pltpu.VMEM((wide, width, width), bf16),
            pltpu.VMEM((states, span, width), bf16),
            pltpu.VMEM((half, states + 1, rows, width), bf16),
            pltpu.VMEM((half, states + 1, rows, width), bf16),
            pltpu.VMEM((sectors, rows, width), bf16),
            pltpu.VMEM((sectors, rows, width), bf16),
            pltpu.VMEM((sectors - AROUND, rows, width), bf16),
            dma((wide,)), dma((wide,)), dma((wide, half)), dma((wide, half)),
            dma((states, devices)), dma((2, half, states)),
            dma((sectors,)), dma((sectors,)),
            dma((sectors - AROUND,)), dma((sectors - AROUND,)), dma((sectors - AROUND,)),
        ],
        compiler_params=pltpu.CompilerParams(
            collective_id=1 + at, has_side_effects=True, vmem_limit_bytes=50 * 2**20),
        cost_estimate=pl.CostEstimate(
            flops=4 * states * span * span * width, bytes_accessed=16 * 2**20, transcendentals=0),
    )(inv, meta, whole, site)


def body(groups, devices, left_env, site_tensor, left_sizes, right_sizes, targets):
    states = site_tensor.shape[1]
    sectors = right_sizes.shape[0]
    others = groups * devices
    i32 = jnp.int32
    dma = pltpu.SemaphoreType.DMA
    smem = pl.BlockSpec(memory_space=pltpu.SMEM)
    vmem = pl.BlockSpec(memory_space=pltpu.VMEM)
    inv, meta, pick, whole, masked = pl.pallas_call(
        agree,
        out_shape=[
            jax.ShapeDtypeStruct((devices, sectors), i32),
            jax.ShapeDtypeStruct((2 * states + 1 + 3 * sectors,), i32),
            jax.ShapeDtypeStruct((1,), i32),
            jax.ShapeDtypeStruct((site_tensor.shape[2],) * 2, jnp.bfloat16),
            jax.ShapeDtypeStruct(site_tensor.shape[1:], jnp.bfloat16),
        ],
        in_specs=[smem] * 3 + [pl.BlockSpec(memory_space=pltpu.HBM)] * 2,
        out_specs=[smem] * 3 + [vmem] * 2,
        scratch_shapes=[
            pltpu.VMEM((8, 128), i32), pltpu.VMEM((others, 8, 128), i32), pltpu.SMEM((others, 8, 128), i32),
            pltpu.VMEM(site_tensor.shape[1:], jnp.bfloat16),
            dma((others,)), dma((others,)), dma, dma, dma, dma, dma,
        ],
        compiler_params=pltpu.CompilerParams(collective_id=0, has_side_effects=True, vmem_limit_bytes=54 * 2**20),
    )(targets, left_sizes, right_sizes, left_env[0], site_tensor[0])
    branches = [functools.partial(fused, at) for at in range(len(LADDER))]
    return lax.switch(pick[0], branches, inv, meta, whole, masked)


def solution(mesh):
    in_specs = (
        P(("groups", "charge"), "split", None),
        P(("groups", "charge"), None, None, "split"),
        P(("groups", "charge")),
        P("groups"),
        P(("groups", "charge"), None),
    )
    out_specs = P("groups", "charge", "split")
    if mesh.shape["split"] == 2 and mesh.shape["charge"] == 8:
        inner = functools.partial(body, mesh.shape["groups"], mesh.shape["charge"])
    else:
        inner = gathered_body
    return jax.shard_map(inner, mesh=mesh, in_specs=in_specs, out_specs=out_specs, check_vma=False)
```

```python
import functools

import jax
import jax.numpy as jnp
from jax import lax
from jax.experimental import pallas as pl
from jax.experimental.pallas import tpu as pltpu
from jax.sharding import PartitionSpec as P

MESH = pl.DeviceIdType.MESH
HOST = (1, 0, 0, 0)
AROUND = 4
LADDER = (
    ((8, 8, 5, 4), (8, 8, 5, 5, 4, 3, 3, 2)),
    ((8, 8, 5, 4), (8, 8, 6, 5, 4, 3, 3, 3)),
    ((8, 8, 6, 4), (8, 8, 6, 5, 4, 3, 3, 2)),
    ((8, 8, 6, 4), (8, 8, 6, 6, 5, 3, 3, 3)),
    ((8, 8, 6, 5), (8, 8, 6, 6, 5, 3, 3, 3)),
    ((8, 8, 8, 8), (8, 8, 8, 8, 8, 8, 8, 8)),
)


def gathered_body(left_env, site_tensor, left_sizes, right_sizes, targets):
    states = site_tensor.shape[1]
    span = site_tensor.shape[2]
    width = site_tensor.shape[3]
    sectors = right_sizes.shape[0]
    column_base = lax.axis_index("split") * width
    row_ids = lax.broadcasted_iota(jnp.int32, (1, span, 1), 1)
    column_ids = lax.broadcasted_iota(jnp.int32, (1, 1, width), 2) + column_base
    slot_ids = lax.broadcasted_iota(jnp.int32, (states, sectors), 1)
    route = targets[0][:, None] == slot_ids
    live_cols = jnp.sum(jnp.where(route, right_sizes[None, :], 0), axis=1)
    keep = (row_ids < left_sizes[0]) & (column_ids < live_cols[:, None, None])
    masked = jnp.where(keep, site_tensor[0], jnp.zeros((), jnp.bfloat16))[None]
    product = jnp.einsum(
        "ik,skj->sij",
        lax.all_gather(left_env, "split", axis=1, tiled=True)[0],
        masked[0],
        preferred_element_type=jnp.float32,
    ).astype(jnp.bfloat16)
    terms = jnp.einsum(
        "ski,skj->sij",
        lax.all_gather(masked, "split", axis=3, tiled=True)[0],
        product,
        preferred_element_type=jnp.float32,
    ).astype(jnp.bfloat16)
    placed = jnp.einsum(
        "st,sij->tij", route.astype(jnp.bfloat16), terms, preferred_element_type=jnp.float32
    ).astype(jnp.bfloat16)
    return lax.psum_scatter(placed, "charge", scatter_dimension=1, tiled=True).astype(jnp.float32)


def agree(targets_ref, left_ref, right_ref, l_ref, m_ref, inv_ref, meta_ref, pick_ref, lf, ms,
          info, got, seen, site, send, recv, sem, lsend, lrecv, lown, mown):
    g = lax.axis_index("groups")
    me = lax.axis_index("charge")
    h = lax.axis_index("split")
    devices, sectors = inv_ref.shape[0], right_ref.shape[0]
    others = got.shape[0]
    states = targets_ref.shape[1]
    mine = g * devices + me
    rights = 2 * states + 1
    orders = rights + sectors
    ranks = orders + sectors

    barrier = pltpu.get_barrier_semaphore()

    def place(i):
        n = lax.rem(mine + i, others)
        return {"groups": n // devices, "charge": lax.rem(n, devices)}

    def greet(i, c):
        pl.semaphore_signal(barrier, inc=1, device_id=place(i), device_id_type=MESH)
        return c

    lax.fori_loop(1, others, greet, 0)
    pl.semaphore_signal(barrier, inc=1, device_id={"split": 1 - h}, device_id_type=MESH)

    span, width = ms.shape[1], ms.shape[2]
    half_rows = pl.ds(pl.multiple_of(h * width, width), width)
    m_own = pltpu.make_async_copy(m_ref, site, mown)
    m_own.start()
    l_own = pltpu.make_async_copy(l_ref, lf.at[half_rows], lown)
    l_own.start()
    every = [right_ref[r] for r in range(sectors)]
    place_of = []
    for r in range(sectors):
        ahead = jnp.int32(0)
        for k in range(sectors):
            if k != r:
                first = every[k] >= every[r] if k < r else every[k] > every[r]
                ahead = ahead + jnp.where(first, 1, 0)
        place_of.append(ahead)
        meta_ref[rights + r] = every[r]
        meta_ref[ranks + r] = ahead
    ordered = []
    for k in range(sectors):
        which, much = jnp.int32(0), jnp.int32(0)
        for r in range(sectors):
            which = jnp.where(place_of[r] == k, r, which)
            much = jnp.where(place_of[r] == k, every[r], much)
        meta_ref[orders + k] = which
        ordered.append(much)
    to = [targets_ref[0, j] for j in range(states)]
    size = [right_ref[t] for t in to]
    grade = [meta_ref[ranks + t] for t in to]
    rank = []
    for j in range(states):
        ahead = jnp.int32(0)
        for k in range(states):
            if k != j:
                ahead = ahead + jnp.where(grade[k] < grade[j], 1, 0)
        rank.append(ahead)
    lane = lax.broadcasted_iota(jnp.int32, info.shape, 1)
    packed = jnp.zeros(info.shape, jnp.int32)
    for slot in range(states):
        state, live, target = jnp.int32(0), jnp.int32(0), jnp.int32(0)
        for j in range(states):
            here = rank[j] == slot
            state = jnp.where(here, j, state)
            live = jnp.where(here, size[j], live)
            target = jnp.where(here, to[j], target)
        meta_ref[slot] = state
        meta_ref[states + slot] = live
        packed = jnp.where(lane == slot, target, packed)
        packed = jnp.where(lane == states + slot, live, packed)
    for k in range(sectors):
        packed = jnp.where(lane == 2 * states + k, ordered[k], packed)
    meta_ref[2 * states] = left_ref[0]
    info[...] = packed
    got[mine] = packed
    pl.semaphore_wait(barrier, others)
    l_copy = pltpu.make_async_remote_copy(
        src_ref=l_ref, dst_ref=lf.at[half_rows], send_sem=lsend, recv_sem=lrecv,
        device_id={"split": 1 - h}, device_id_type=MESH)
    l_copy.start()

    def copy(i):
        return pltpu.make_async_remote_copy(
            src_ref=info, dst_ref=got.at[mine], send_sem=send.at[i], recv_sem=recv.at[mine],
            device_id=place(i), device_id_type=MESH)

    def start(i, c):
        copy(i).start()
        return c

    def finish(i, c):
        n = lax.rem(mine + i, others)
        copy(i).wait_send()
        pltpu.make_async_remote_copy(
            src_ref=info, dst_ref=got.at[n], send_sem=send.at[i], recv_sem=recv.at[n],
            device_id=place(i), device_id_type=MESH).wait_recv()
        return c

    lax.fori_loop(1, others, start, 0)
    m_own.wait()

    def mask(j, c):
        state, live, deep = meta_ref[j], meta_ref[states + j], meta_ref[2 * states]

        def tile(i, c):
            part = pl.ds(pl.multiple_of(i * 128, 128), 128)
            row_ids = lax.broadcasted_iota(jnp.int32, (128, width), 0) + i * 128
            col_ids = lax.broadcasted_iota(jnp.int32, (128, width), 1) + h * width
            keep = (row_ids < deep) & (col_ids < live)
            ms[j, part] = jnp.where(keep, site[state, part].astype(jnp.float32), 0.0).astype(jnp.bfloat16)
            return c

        return lax.fori_loop(0, span // 128, tile, c)

    lax.fori_loop(0, states, mask, 0)
    lax.fori_loop(1, others, finish, 0)
    local = pltpu.make_async_copy(got, seen, sem)
    local.start()
    local.wait()

    half = devices // 2
    rows = span // devices
    side, seat = lax.div(me, half), lax.rem(me, half)
    for kind in range(2):
        block = (side if kind == 0 else 1 - side) * half + seat
        wants = [every[r] > jnp.maximum(block * rows, h * width) for r in range(sectors)]

        def route(s, c):
            reached = [seen[mine - seat + s, 0, j] for j in range(states)]
            for r in range(sectors):
                slot = jnp.int32(states)
                for j in range(states):
                    slot = jnp.where(reached[j] == r, j, slot)
                inv_ref[kind * half + s, r] = jnp.where(wants[r], slot, states)
            return c

        lax.fori_loop(0, half, route, 0)

    def widest(n, most):
        return tuple(jnp.maximum(m, seen[n, 0, states + j]) for j, m in enumerate(most))

    most = lax.fori_loop(0, others, widest, (jnp.int32(0),) * (states + sectors))
    pick = jnp.int32(len(LADDER) - 1)
    for at in range(len(LADDER) - 2, -1, -1):
        caps = LADDER[at][0] + LADDER[at][1]
        fits = most[0] <= caps[0] * rows
        for j in range(1, states + sectors):
            fits = fits & (most[j] <= caps[j] * rows)
        pick = jnp.where(fits, at, pick)
    pick_ref[0] = pick
    l_own.wait()
    l_copy.wait()


def kernel(caps, crops, inv_ref, meta_ref, lf, ms, o_ref, mr, pb, px, xb, tb, w0, w1, up, down, via,
           msend, mrecv, xsend, xrecv, zsend, zrecv, usend, drecv, vsend, vrecv, fsend):
    me = lax.axis_index("charge")
    h = lax.axis_index("split")
    states, span, width = ms.shape
    sectors, rows = o_ref.shape[0], o_ref.shape[1]
    devices = span // rows
    half = devices // 2
    empty = states
    f32, bf16 = jnp.float32, jnp.bfloat16
    own, seat = lax.div(me, half), lax.rem(me, half)
    partner = {"charge": lax.rem(me + half, devices)}
    wide = [j for j in range(states) if caps[j] > half]
    rights, orders, ranks = 2 * states + 1, 2 * states + 1 + sectors, 2 * states + 1 + 2 * sectors

    def blocks(cap, side):
        return min(cap, half) if side == 0 else max(cap - half, 0)

    def live(cap, side):
        return blocks(cap, side) * rows

    barrier = pltpu.get_barrier_semaphore()
    pl.semaphore_signal(barrier, inc=1, device_id={"split": 1 - h}, device_id_type=MESH)
    pl.semaphore_signal(barrier, inc=1, device_id=partner, device_id_type=MESH)
    across = {"charge": lax.rem(me + half, devices), "split": 1 - h}
    pl.semaphore_signal(barrier, inc=1, device_id=across, device_id_type=MESH)
    for i in range(1, half):
        pl.semaphore_signal(
            barrier, inc=1, device_id={"charge": own * half + lax.rem(seat + i, half)}, device_id_type=MESH)
    pl.semaphore_wait(barrier, half + 2)

    def m_copy(j):
        columns = pl.ds(0, live(caps[j], 1 - HOST[j]))
        return pltpu.make_async_remote_copy(
            src_ref=ms.at[j, :, columns], dst_ref=mr.at[j, :, columns], send_sem=msend.at[j],
            recv_sem=mrecv.at[j], device_id={"split": 1 - h}, device_id_type=MESH)

    def x_copy(j, b):
        s = HOST[j]
        columns = pl.ds(0, live(caps[j], 1 - s))
        here, there = (pl.ds(pl.multiple_of((n + b) * rows, rows), rows) for n in (0, s * half))
        return pltpu.make_async_remote_copy(
            src_ref=xb.at[j, here, columns], dst_ref=tb.at[j, there, columns],
            send_sem=xsend.at[j, b], recv_sem=xrecv.at[j, b], device_id={"split": 1 - h}, device_id_type=MESH)

    def chunk(j, part, side, to, source, kind):
        w = (w0, w1)[kind]
        columns = pl.ds(0, live(caps[j], side))
        from_rows = pl.ds(pl.multiple_of((part * half + to) * rows, rows), rows)
        return pltpu.make_async_remote_copy(
            src_ref=tb.at[j, from_rows, columns], dst_ref=w.at[source, j, :, columns],
            send_sem=zsend.at[j, part * half + to], recv_sem=zrecv.at[kind, source, j],
            device_id={"charge": own * half + to}, device_id_type=MESH)

    def forward(j, part, side, to):
        columns = live(caps[j], side)
        for kind in range(2):
            w = (w0, w1)[kind]

            @pl.when((own == part ^ kind) & (to != seat))
            def _():
                chunk(j, part, side, to, seat, kind).start()

            @pl.when((own == part ^ kind) & (to == seat))
            def _():
                def move(i, c):
                    here = pl.ds(pl.multiple_of((part * half + to) * rows + i * 32, 32), 32)
                    w[seat, j, pl.ds(pl.multiple_of(i * 32, 32), 32), 0:columns] = tb[j, here, 0:columns]
                    return c

                lax.fori_loop(0, rows // 32, move, 0)

    def scatter(j, part, side):
        count = blocks(caps[j], part)

        def one(i, c):
            forward(j, part, side, lax.rem(seat + 1 + i, count))
            return c

        lax.fori_loop(0, count, one, 0)

    def arrive(j, part, side, kind):
        if live(caps[j], side) == 0 or blocks(caps[j], part) == 0:
            return

        @pl.when(seat < blocks(caps[j], part))
        def _():
            def one(i, c):
                chunk(j, part, side, seat, lax.rem(seat + i, half), kind).wait_recv()
                return c

            lax.fori_loop(1, half, one, 0)

    def sent(j, part, side):
        count = blocks(caps[j], part)
        if live(caps[j], side) == 0 or count == 0:
            return

        def one(to, c):
            pl.when(to != seat)(lambda: chunk(j, part, side, to, seat, 0).wait_send())
            return c

        lax.fori_loop(0, count, one, 0)

    def hand(k, side):
        columns = pl.ds(0, live(crops[k], side))
        return pltpu.make_async_remote_copy(
            src_ref=up.at[k, :, columns], dst_ref=down.at[k, :, columns], send_sem=usend.at[k],
            recv_sem=drecv.at[k], device_id=partner, device_id_type=MESH)

    def aside(k):
        columns = pl.ds(0, live(crops[k], 0))
        return pltpu.make_async_remote_copy(
            src_ref=up.at[k, :, columns], dst_ref=via.at[k - AROUND, :, columns], send_sem=vsend.at[k - AROUND],
            recv_sem=vrecv.at[k - AROUND], device_id={"split": 1 - h}, device_id_type=MESH)

    def diagonal(k):
        columns = pl.ds(0, live(crops[k], 0))
        return pltpu.make_async_remote_copy(
            src_ref=via.at[k - AROUND, :, columns], dst_ref=down.at[k, :, columns], send_sem=fsend.at[k - AROUND],
            recv_sem=drecv.at[k], device_id=across, device_id_type=MESH)

    def split_up(k, part, side, around, across):
        if part != 0 or side != 0 or k < AROUND:
            across()
        elif k > AROUND:
            around()
        else:
            pl.when(seat < half // 2)(around)
            pl.when(seat >= half // 2)(across)

    def handed(k, part, side, act):
        if live(crops[k], side) and blocks(crops[k], part):
            pl.when(seat < blocks(crops[k], part))(act)

    def relay(k, part, side, full):
        def act():
            columns = live(crops[k], side)
            r = meta_ref[orders + k]
            slots = [inv_ref[half + source, r] for source in range(half)]

            def tile(i, c):
                at = pl.ds(pl.multiple_of(i * 32, 32), 32)
                total = jnp.zeros((32, columns), f32)
                for source in range(half):
                    if full:
                        total = total + w1[source, slots[source], at, 0:columns].astype(f32)
                    else:
                        for j in range(k + 1):
                            one = w1[source, j, at, 0:columns].astype(f32)
                            total = total + jnp.where(slots[source] == j, one, 0.0)
                up[k, at, 0:columns] = total.astype(bf16)
                return c

            lax.fori_loop(0, rows // 32, tile, 0)
            split_up(k, part, side, lambda: aside(k).start(), lambda: hand(k, side).start())

        handed(k, part, side, act)

    def product(j):
        def tile(i, c):
            part = pl.ds(pl.multiple_of(i * 256, 256), 256)
            pb[j, part] = jnp.dot(lf[part], ms[j], preferred_element_type=f32).astype(bf16)
            return c

        lax.fori_loop(0, span // 256, tile, 0)

    def flipped(columns, right):
        return lax.dot_general(columns, right, (((0,), (0,)), ((), ())), preferred_element_type=f32).astype(bf16)

    def near(j, c):
        @pl.when((j < len(wide)) | (h == 0))
        def _():
            product(j)

            def tile(i, c):
                part = pl.ds(pl.multiple_of(h * width + i * 256, 256), 256)
                tb[j, part] = flipped(ms[j, :, pl.ds(pl.multiple_of(i * 256, 256), 256)], pb[j])
                return c

            lax.fori_loop(0, width // 256, tile, 0)

        for slot in range(states):
            for side in range(2):
                if live(caps[slot], side):
                    pl.when((h == side) & (j == slot))(functools.partial(scatter, slot, side, side))
        return c

    def turned(i, s, count):
        return count - 1 - i

    def far(j, s):
        o = 1 - s
        columns = live(caps[j], o)
        m_copy(j).wait_recv()

        def tile(i, c):
            part = pl.ds(pl.multiple_of(i * 256, 256), 256)
            px[part, 0:columns] = jnp.dot(lf[part], mr[j, :, 0:columns], preferred_element_type=f32).astype(bf16)
            return c

        lax.fori_loop(0, span // 256, tile, 0)

        def back(i, c):
            i = turned(i, s, blocks(caps[j], s))
            part = pl.ds(pl.multiple_of(i * rows, rows), rows)
            xb[j, part, 0:columns] = flipped(ms[j, :, part], px[:, 0:columns])
            x_copy(j, i).start()
            return c

        lax.fori_loop(0, blocks(caps[j], s), back, 0)

        def there(i, c):
            part = pl.ds(pl.multiple_of(o * width + i * rows, rows), rows)
            tb[j, part] = flipped(mr[j, :, pl.ds(pl.multiple_of(i * rows, rows), rows)], pb[j])
            return c

        lax.fori_loop(0, blocks(caps[j], o), there, 0)
        scatter(j, o, s)

    hosts = [[j for j in reversed(wide) if HOST[j] == s] for s in range(2)]
    if sum(caps[j] - half for j in wide[2:]) > 1:
        hosts[0].sort(key=lambda j: (j != 1, -j))
    for s in range(2):
        @pl.when(h == s)
        def _():
            for j in hosts[1 - s]:
                m_copy(j).start()
    lax.fori_loop(0, states, near, 0)
    w0[:, empty] = jnp.zeros((half, rows, width), bf16)
    w1[:, empty] = jnp.zeros((half, rows, width), bf16)

    def pass_on(s, part, slots, some, full):
        @pl.when(own == 1 - part)
        def _():
            for j in slots:
                arrive(j, part, s, 1)
            for k in some:
                relay(k, part, s, full)

    def turn_over():
        @pl.when(own == 1)
        def _():
            for k in range(AROUND, sectors):
                def act(k=k):
                    aside(k).wait_recv()
                    diagonal(k).start()

                handed(k, 0, 0, lambda k=k, act=act: split_up(k, 0, 0, act, lambda: None))

    def course(s):
        for j in range(states - 1):
            pass_on(s, s, [j], [j], False)
        last = functools.partial(pass_on, s, s, [states - 1], range(states - 1, sectors), True)
        mine, theirs = hosts[s], hosts[1 - s]
        done = int(mine == [0])
        for j in mine[:-1]:
            far(j, s)
        if not done:
            last()
        far(mine[-1], s)
        if done:
            last()
            pass_on(s, 1 - s, [0], [0], False)
        for j in theirs[:-1]:
            def step(b, c, j=j):
                x_copy(j, b).wait_recv()
                forward(j, 1 - s, s, b)
                return c

            lax.fori_loop(0, blocks(caps[j], 1 - s), step, 0)
        if s == 1:
            turn_over()
        j = theirs[-1]
        count = blocks(caps[j], 1 - s)

        def step(b, c):
            b = turned(b, 1 - s, count)
            x_copy(j, b).wait_recv()
            forward(j, 1 - s, s, b)
            return c

        lax.fori_loop(0, count, step, 0)
        pass_on(s, 1 - s, range(done, states), range(sectors - 1, done - 1, -1), True)
        for part in range(2):
            @pl.when(own == part)
            def _():
                for j in range(states):
                    arrive(j, part, s, 0)

    for s in range(2):
        pl.when(h == s)(functools.partial(course, s))

    def gather(r, c):
        total = w0[0, inv_ref[0, r]].astype(f32)
        for source in range(1, half):
            total = total + w0[source, inv_ref[source, r]].astype(f32)
        o_ref[r] = total
        return c

    lax.fori_loop(0, sectors, gather, 0)

    def received(s):
        for part in range(2):
            @pl.when(own == part)
            def _():
                for k in range(sectors):
                    handed(k, part, s, lambda k=k: hand(k, s).wait_recv())

    for s in range(2):
        pl.when(h == s)(functools.partial(received, s))

    def add(r, c):
        size = meta_ref[rights + r]
        col_ids = lax.broadcasted_iota(jnp.int32, (rows, width), 1) + h * width
        limit = jnp.where(size > me * rows, size, 0)
        o_ref[r] = jnp.where(col_ids < limit, o_ref[r] + down[meta_ref[ranks + r]].astype(f32), 0.0)
        return c

    lax.fori_loop(0, sectors, add, 0)

    def settle(s):
        for j in hosts[1 - s]:
            m_copy(j).wait_send()
        for j in hosts[s]:
            def left(b, c, j=j):
                x_copy(j, b).wait_send()
                return c

            lax.fori_loop(0, blocks(caps[j], s), left, 0)
        for j in range(states):
            for part in range(2):
                sent(j, part, s)
        for part in range(2):
            @pl.when(own == 1 - part)
            def _():
                for k in range(sectors):
                    handed(k, part, s, lambda k=k, part=part: split_up(
                        k, part, s, lambda: aside(k).wait_send(), lambda: hand(k, s).wait_send()))
        if s == 1:
            @pl.when(own == 1)
            def _():
                for k in range(AROUND, sectors):
                    handed(k, 0, 0, lambda k=k: split_up(
                        k, 0, 0, lambda: diagonal(k).wait_send(), lambda: None))

    for s in range(2):
        pl.when(h == s)(functools.partial(settle, s))


def fused(at, inv, meta, whole, site):
    caps, crops = LADDER[at]
    states, span, width = site.shape
    devices, sectors = inv.shape
    rows, half = span // devices, devices // 2
    wide = max(j + 1 for j in range(states) if caps[j] > half)
    bf16 = jnp.bfloat16
    dma = pltpu.SemaphoreType.DMA
    return pl.pallas_call(
        functools.partial(kernel, caps, crops),
        out_shape=jax.ShapeDtypeStruct((sectors, rows, width), jnp.float32),
        in_specs=[pl.BlockSpec(memory_space=pltpu.SMEM)] * 2 + [pl.BlockSpec(memory_space=pltpu.VMEM)] * 2,
        out_specs=pl.BlockSpec(memory_space=pltpu.VMEM),
        scratch_shapes=[
            pltpu.VMEM((wide, span, width), bf16),
            pltpu.VMEM((states, span, width), bf16),
            pltpu.VMEM((span, width), bf16),
            pltpu.VMEM((wide, width, width), bf16),
            pltpu.VMEM((states, span, width), bf16),
            pltpu.VMEM((half, states + 1, rows, width), bf16),
            pltpu.VMEM((half, states + 1, rows, width), bf16),
            pltpu.VMEM((sectors, rows, width), bf16),
            pltpu.VMEM((sectors, rows, width), bf16),
            pltpu.VMEM((sectors - AROUND, rows, width), bf16),
            dma((wide,)), dma((wide,)), dma((wide, half)), dma((wide, half)),
            dma((states, devices)), dma((2, half, states)),
            dma((sectors,)), dma((sectors,)),
            dma((sectors - AROUND,)), dma((sectors - AROUND,)), dma((sectors - AROUND,)),
        ],
        compiler_params=pltpu.CompilerParams(
            collective_id=1 + at, has_side_effects=True, vmem_limit_bytes=50 * 2**20),
        cost_estimate=pl.CostEstimate(
            flops=4 * states * span * span * width, bytes_accessed=16 * 2**20, transcendentals=0),
    )(inv, meta, whole, site)


def body(groups, devices, left_env, site_tensor, left_sizes, right_sizes, targets):
    states = site_tensor.shape[1]
    sectors = right_sizes.shape[0]
    others = groups * devices
    i32 = jnp.int32
    dma = pltpu.SemaphoreType.DMA
    smem = pl.BlockSpec(memory_space=pltpu.SMEM)
    vmem = pl.BlockSpec(memory_space=pltpu.VMEM)
    inv, meta, pick, whole, masked = pl.pallas_call(
        agree,
        out_shape=[
            jax.ShapeDtypeStruct((devices, sectors), i32),
            jax.ShapeDtypeStruct((2 * states + 1 + 3 * sectors,), i32),
            jax.ShapeDtypeStruct((1,), i32),
            jax.ShapeDtypeStruct((site_tensor.shape[2],) * 2, jnp.bfloat16),
            jax.ShapeDtypeStruct(site_tensor.shape[1:], jnp.bfloat16),
        ],
        in_specs=[smem] * 3 + [pl.BlockSpec(memory_space=pltpu.HBM)] * 2,
        out_specs=[smem] * 3 + [vmem] * 2,
        scratch_shapes=[
            pltpu.VMEM((8, 128), i32), pltpu.VMEM((others, 8, 128), i32), pltpu.SMEM((others, 8, 128), i32),
            pltpu.VMEM(site_tensor.shape[1:], jnp.bfloat16),
            dma((others,)), dma((others,)), dma, dma, dma, dma, dma,
        ],
        compiler_params=pltpu.CompilerParams(collective_id=0, has_side_effects=True, vmem_limit_bytes=54 * 2**20),
    )(targets, left_sizes, right_sizes, left_env[0], site_tensor[0])
    branches = [functools.partial(fused, at) for at in range(len(LADDER))]
    return lax.switch(pick[0], branches, inv, meta, whole, masked)


def solution(mesh):
    in_specs = (
        P(("groups", "charge"), "split", None),
        P(("groups", "charge"), None, None, "split"),
        P(("groups", "charge")),
        P("groups"),
        P(("groups", "charge"), None),
    )
    out_specs = P("groups", "charge", "split")
    if mesh.shape["split"] == 2 and mesh.shape["charge"] == 8:
        inner = functools.partial(body, mesh.shape["groups"], mesh.shape["charge"])
    else:
        inner = gathered_body
    return jax.shard_map(inner, mesh=mesh, in_specs=in_specs, out_specs=out_specs, check_vma=False)
```
